128 devices in a mesh: group: 8 (over y, core), dev: 16 (over z, x).
Axes of the slice: x: 4, y: 4, z: 4, core: 2. Of those that a mesh axis runs over, the one named last changes fastest.
Arguments:
- queries: bfloat16 [3072, 1024], P(('group', 'dev')), may hold values from -12 to 12
- keys: bfloat16 [512, 256, 1024], P(('group', 'dev')), may hold values from -12 to 12
- values: bfloat16 [512, 256, 1024], P(('group', 'dev')), may hold values from -6 to 6
- frame_slot: int32 [512], replicated, may hold values from 0 to 511, each once
- covisible: int32 [12, 160], replicated, may hold values from 0 to 511, as said below
- counts: int32 [12], replicated, may hold values from 16 to 160
- out_weight: bfloat16 [1024, 1024], replicated, may hold values from -0.1875 to 0.1875
Outputs:
- projected: bfloat16 [3072, 1024], P(('group', 'dev'))
The draws below stay inside these ranges and needn't reach their ends.
Inputs may be any that keep to these rules, and one draw needn't show every extreme that they name: `covisible`: each row lists 160 different frame numbers; query frame q attends to the first counts[q] of them. `frame_slot`: every frame is held at exactly one storage row.
All inputs are finite; a program needn't handle non-finite values.
Results may differ from the reference program's by a relative error of at most 0.02.
Values may be sent and summed in bfloat16 or wider, within the bound.
No kernel may reach another device: no remote copies, remote signals or barrier semaphores. Data moves between devices by JAX's collectives and lax.ppermute only.
A program may use at most 192 MiB of HBM per device.

```python
import jax
import jax.numpy as jnp
from jax import lax

D = 1024
HEADS = 16
HD = 64
TOK = 256
QF = 12
FRAMES = 512
MAXCOV = 160
MINCOV = 16


def covisible_lists(key):
    base = jax.random.fold_in(key, 202)
    first, second, third, fourth, fifth = jax.random.split(base, 5)
    centers = jax.random.randint(first, (QF,), 0, FRAMES // 4)
    offsets = jax.vmap(lambda piece: jax.random.permutation(piece, 2 * MAXCOV))(jax.random.split(second, QF))
    lists = (centers[:, None] + offsets[:, :MAXCOV] - MAXCOV) % FRAMES
    used = jax.random.randint(third, (QF,), MINCOV, MAXCOV + 1)
    top_row = jax.random.randint(fourth, (), 0, QF)
    low_row = (top_row + 1 + jax.random.randint(fifth, (), 0, QF - 1)) % QF
    used = used.at[top_row].set(MAXCOV).at[low_row].set(MINCOV)
    return (lists.astype(jnp.int32), used.astype(jnp.int32))


def draw_covisible(key, part):
    return covisible_lists(key)[0]


def draw_counts(key, part):
    return covisible_lists(key)[1]


def draw_keys(key, part):
    key = jax.random.fold_in(key, 3)
    first = jax.random.fold_in(key, 0)
    result = jax.random.normal(first, (FRAMES, TOK, D), jnp.float32)
    return jnp.clip(result, -12.0, 12.0).astype(jnp.bfloat16)


def draw_queries(key, part):
    key = jax.random.fold_in(key, 4)
    first = jax.random.fold_in(key, 0)
    result = jax.random.normal(first, (QF, TOK, D), jnp.float32)
    return jnp.clip(result, -12.0, 12.0).reshape(QF * TOK, D).astype(jnp.bfloat16)


def levels(own_key, shape, cuts, smallest, top_value):
    loudness, own = 1.0, jax.random.fold_in(own_key, 6)
    for axis_at, parts in cuts:
        steps = jnp.exp(jax.random.uniform(jax.random.fold_in(own, axis_at), (parts,), jnp.float32, smallest / len(cuts), top_value / len(cuts)))
        loudness = loudness * jnp.repeat(steps, shape[axis_at] // parts).reshape([-1 if axis == axis_at else 1 for axis in range(len(shape))])
    return loudness


def bell_draw(rng, shape, deviation, limit, pieces=(), held_as=jnp.bfloat16):
    entries = jax.random.normal(rng, shape, jnp.float32) * deviation
    if len(pieces) > 0:
        entries = levels(rng, shape, pieces, -0.22, 0.18) * entries
    return jnp.clip(entries, min=-limit, max=limit).astype(held_as)


def setup_inputs(seed: int = 0) -> dict:
    arg_keys = jax.random.split(jax.random.key(seed), 8)
    return {
        "queries": draw_queries(jax.random.fold_in(arg_keys[7], 71), 0),
        "keys": draw_keys(jax.random.fold_in(arg_keys[7], 71), 0),
        "values": bell_draw(arg_keys[2], (FRAMES, TOK, D), 1.0, 6.0, ((0, 128),)),
        "frame_slot": jax.random.permutation(arg_keys[3], FRAMES).astype(jnp.int32),
        "covisible": draw_covisible(jax.random.fold_in(arg_keys[7], 71), 0),
        "counts": draw_counts(jax.random.fold_in(arg_keys[7], 71), 0),
        "out_weight": bell_draw(arg_keys[6], (D, D), D ** -0.5, 0.1875),
    }


NEG_FILL = -1.0e30
LOG2E = 1.4426950408889634


def reference(queries, keys, values, frame_slot, covisible, counts, out_weight):
    score_scale = HD ** -0.5
    query_heads = queries.reshape(QF, TOK, HEADS, HD).astype(jnp.float32)

    def one_frame(packed):
        query_rows, frame_list, used = packed
        slot_list = jnp.take(frame_slot, frame_list).astype(jnp.int32)

        def frame_scores(position):
            slot_index = slot_list[position]
            key_rows = lax.dynamic_index_in_dim(keys, slot_index, 0, keepdims=False)
            key_rows = key_rows.reshape(TOK, HEADS, HD).astype(jnp.float32)
            return jnp.einsum("rhd,khd->rhk", query_rows, key_rows) * score_scale

        def max_step(running, position):
            maxima = jnp.max(frame_scores(position), axis=2)
            return jnp.where(position < used, jnp.maximum(running, maxima), running), None

        start_top = jnp.full((TOK, HEADS), NEG_FILL, jnp.float32)
        raw_top, _ = lax.scan(max_step, start_top, jnp.arange(MAXCOV, dtype=jnp.int32))
        row_top = jnp.ceil(raw_top * LOG2E)

        def sum_step(carry, position):
            numer, totals = carry
            weights = jnp.exp2(frame_scores(position) * LOG2E - row_top[:, :, None])
            weights = jnp.where(position < used, weights, jnp.float32(0.0))
            rounded = lax.optimization_barrier(weights.astype(jnp.bfloat16)).astype(jnp.float32)
            value_rows = lax.dynamic_index_in_dim(values, slot_list[position], 0, keepdims=False)
            value_rows = value_rows.reshape(TOK, HEADS, HD).astype(jnp.float32)
            numer = numer + jnp.einsum("rhk,khd->rhd", rounded, value_rows)
            totals = totals + jnp.sum(weights, axis=2)
            return (numer, totals), None

        start = (jnp.zeros((TOK, HEADS, HD), jnp.float32), jnp.zeros((TOK, HEADS), jnp.float32))
        (numer, totals), _ = lax.scan(sum_step, start, jnp.arange(MAXCOV, dtype=jnp.int32))
        return (numer / totals[:, :, None]).reshape(TOK, D).astype(jnp.bfloat16)

    attended = lax.map(one_frame, (query_heads, covisible, counts))
    attended = attended.reshape(QF * TOK, D)
    return jnp.dot(attended, out_weight, preferred_element_type=jnp.float32).astype(jnp.bfloat16)
```

```python
import functools

import jax
import jax.numpy as jnp
from jax import lax
from jax.experimental import pallas as pl
from jax.experimental.pallas import tpu as pltpu
from jax.sharding import Mesh, PartitionSpec as P

HD = 64
LOG2E = 1.4426950408889634
TOP_STEP = 16.0
NO_TOP = -32768.0
CHIPS = ("y", "z", "x")
ALL = ("y", "core", "z", "x")
F32 = jnp.float32
BF16 = jnp.bfloat16


def attend_kernel(cnt, lst, q, k, vt, out, qf, qm, acc, top, yb):
    scale = HD ** -0.5 * LOG2E
    low_half = lax.broadcasted_iota(jnp.int32, (256, 128), 1) < 64
    ones = jnp.ones((16, 256), BF16)

    def one_y(y, _):
        def load(zx, _):
            block = q[y * 16 + zx].astype(F32)
            for c in range(2):
                row = pl.multiple_of((c * 16 + zx) * 24, 8)
                qf[pl.ds(row, 24), :] = block[c * 24:(c + 1) * 24]
            return 0

        lax.fori_loop(0, 16, load, 0)

        def one_frame(f, _):
            qi = y * 3 + f
            n = cnt[qi]
            row0 = pl.multiple_of(f * 256, 256)
            rows = pl.ds(row0, 256)

            @pl.when(n > 0)
            def _():
                for hp in range(4):
                    pair = qf[rows, hp * 128:(hp + 1) * 128]
                    qm[2 * hp] = jnp.where(low_half, pair, 0.0).astype(BF16)
                    qm[2 * hp + 1] = jnp.where(low_half, 0.0, pair).astype(BF16)
                acc[...] = jnp.zeros_like(acc)
                top[...] = jnp.full_like(top, NO_TOP)

                def step(i, _):
                    j = lst[qi * 8 + i]
                    for h in range(8):
                        hp = h // 2
                        keys = k[j, :, hp * 128:(hp + 1) * 128]
                        s = lax.dot_general(keys, qm[h], (((1,), (1,)), ((), ())), preferred_element_type=F32)
                        high = jnp.max(s, axis=0, keepdims=True) * scale
                        old = top[h:h + 1]
                        new = jnp.maximum(old, jnp.ceil(high * (1.0 / TOP_STEP)) * TOP_STEP)
                        top[h:h + 1] = new
                        weights = jnp.exp2(s * scale - new).astype(BF16)
                        vals = jnp.concatenate([vt[j, h * 64:(h + 1) * 64, :], ones], axis=0)
                        part = jnp.dot(vals, weights, preferred_element_type=F32)
                        acc[h] = acc[h] * jnp.exp2(old - new) + part
                    return 0

                lax.fori_loop(0, n, step, 0)
                totals = jnp.concatenate([acc[h, 64:65, :] for h in range(8)], axis=0)
                hi = totals.astype(BF16).astype(F32)
                extra = jnp.concatenate([top[...], hi, totals - hi, jnp.zeros((104, 256), F32)], axis=0)
                for hp in range(4):
                    both = jnp.concatenate([acc[2 * hp, :64, :], acc[2 * hp + 1, :64, :]], axis=0)
                    yb[rows, hp * 128:(hp + 1) * 128] = both.T
                yb[rows, 512:640] = extra.T

            @pl.when(n == 0)
            def _():
                yb[rows, 0:512] = jnp.zeros((256, 512), F32)
                lane = lax.broadcasted_iota(jnp.int32, (256, 128), 1)
                yb[rows, 512:640] = jnp.where(lane < 8, NO_TOP, 0.0)

            return 0

        lax.fori_loop(0, 3, one_frame, 0)

        def emit(zx, _):
            data, packed = [], [jnp.zeros((8, 128), F32)] * 2
            for c in range(2):
                row = pl.multiple_of((c * 16 + zx) * 24, 8)
                block = yb[pl.ds(row, 24), :]
                data.append(block[:, :512])
                for p in range(3):
                    g = c * 3 + p
                    piece = block[p * 8:(p + 1) * 8, 512:640]
                    if g % 4:
                        piece = pltpu.roll(piece, 32 * (g % 4), 1)
                    packed[g // 4] = packed[g // 4] + piece
            tail = jnp.concatenate(packed + [jnp.zeros((8, 256), F32)], axis=1)
            out[y * 16 + zx] = jnp.concatenate(data + [tail], axis=0).astype(BF16)
            return 0

        lax.fori_loop(0, 16, emit, 0)
        return 0

    lax.fori_loop(0, 4, one_y, 0)


def attend(cnt, lst, q, k, vt):
    vmem = pl.BlockSpec(memory_space=pltpu.VMEM)
    smem = pl.BlockSpec(memory_space=pltpu.SMEM)
    return pl.pallas_call(
        attend_kernel,
        out_shape=jax.ShapeDtypeStruct((64, 56, 512), BF16),
        in_specs=[smem, smem, vmem, vmem, vmem],
        out_specs=vmem,
        scratch_shapes=[
            pltpu.VMEM((768, 512), F32),
            pltpu.VMEM((8, 256, 128), BF16),
            pltpu.VMEM((8, 80, 256), F32),
            pltpu.VMEM((8, 256), F32),
            pltpu.VMEM((768, 640), F32),
        ],
        compiler_params=pltpu.CompilerParams(vmem_limit_bytes=48 * 2**20),
        name="attend",
    )(cnt, lst, q, k, vt)


def combine_kernel(r, out, fs):
    n = r.shape[0]

    def find(s, best):
        return jnp.maximum(best, r[s, 48:56, 0:256].astype(F32))

    best = lax.fori_loop(0, n, find, jnp.full((8, 256), NO_TOP, F32))

    def weigh(s, total):
        e = r[s, 48:56, 0:256].astype(F32)
        f = jnp.exp2(jnp.minimum(e - best, 0.0))
        fs[pl.ds(pl.multiple_of(s * 8, 8), 8), :] = f
        hl = [
            pltpu.roll(e[:, t * 128:(t + 1) * 128], 120, 1) + pltpu.roll(e[:, t * 128:(t + 1) * 128], 112, 1)
            for t in range(2)
        ]
        return total + f * jnp.concatenate(hl, axis=1)

    total = lax.fori_loop(0, n, weigh, jnp.zeros((8, 256), F32))
    src = lax.broadcasted_iota(jnp.int32, (128, 512), 0)
    dst = lax.broadcasted_iota(jnp.int32, (128, 512), 1) // 64
    for g in range(6):
        t = g // 4
        spread = (src - 32 * (g % 4) == dst).astype(F32)
        tile = slice(t * 128, (t + 1) * 128)
        wide = jnp.dot(total[:, tile], spread, precision=lax.Precision.HIGHEST, preferred_element_type=F32)
        spread = spread.astype(BF16)

        def add(s8, numer):
            f = fs[pl.ds(pl.multiple_of(s8 * 64, 64), 64), tile].astype(BF16)
            f = jnp.dot(f, spread, preferred_element_type=F32)
            for u in range(8):
                numer = numer + f[u * 8:(u + 1) * 8] * r[s8 * 8 + u, g * 8:(g + 1) * 8, :].astype(F32)
            return numer

        numer = lax.fori_loop(0, n // 8, add, jnp.zeros((8, 512), F32))
        out[g * 8:(g + 1) * 8, :] = numer / wide


def combine(r):
    vmem = pl.BlockSpec(memory_space=pltpu.VMEM)
    return pl.pallas_call(
        combine_kernel,
        out_shape=jax.ShapeDtypeStruct((48, 512), F32),
        in_specs=[vmem],
        out_specs=vmem,
        scratch_shapes=[pltpu.VMEM((r.shape[0] * 8, 256), F32)],
        compiler_params=pltpu.CompilerParams(vmem_limit_bytes=32 * 2**20),
        name="combine",
    )(r)


def swap(x):
    return lax.ppermute(x, "core", [(0, 1), (1, 0)])


def body(queries, keys, values, frame_slot, covisible, counts, out_weight):
    core = lax.axis_index("core")
    device = lax.axis_index(ALL)
    partner = device + 16 - 32 * core
    own_col = core * 512
    other_col = 512 - own_col

    mine = lax.dynamic_slice_in_dim(queries, own_col, 512, 1)
    theirs = swap(lax.dynamic_slice_in_dim(queries, other_col, 512, 1))
    first = core == 0
    pair = jnp.concatenate([jnp.where(first, mine, theirs), jnp.where(first, theirs, mine)], axis=0)
    q_all = lax.all_gather(pair, CHIPS, axis=0)

    k_theirs = swap(lax.dynamic_slice_in_dim(keys, other_col, 512, 2))
    k_all = jnp.concatenate([lax.dynamic_slice_in_dim(keys, own_col, 512, 2), k_theirs], axis=0)
    v_turned = jnp.swapaxes(values, 1, 2)
    v_theirs = swap(lax.dynamic_slice_in_dim(v_turned, other_col, 512, 1))
    v_all = jnp.concatenate([lax.dynamic_slice_in_dim(v_turned, own_col, 512, 1), v_theirs], axis=0)

    four = jnp.arange(4, dtype=jnp.int32)
    slots = jnp.concatenate([device * 4 + four, partner * 4 + four])
    frame_ids = jnp.arange(frame_slot.shape[0], dtype=jnp.int32)
    local = jnp.sum(jnp.where(frame_slot[None, :] == slots[:, None], frame_ids[None, :], 0), axis=1)
    used = jnp.arange(covisible.shape[1], dtype=jnp.int32)[None, :] < counts[:, None]
    need = jnp.any((covisible[:, None, :] == local[None, :, None]) & used[:, None, :], axis=2)
    need_i = need.astype(jnp.int32)
    place = jnp.cumsum(need_i, axis=1) - need_i
    eight = jnp.arange(8, dtype=jnp.int32)
    hit = need[:, None, :] & (place[:, None, :] == eight[None, :, None])
    lst = jnp.sum(jnp.where(hit, eight[None, None, :], 0), axis=2).reshape(96)
    cnt = jnp.sum(need_i, axis=1)

    sent = attend(cnt, lst, q_all, k_all, v_all)
    got = lax.all_to_all(sent, CHIPS, 0, 0)
    attended = combine(got).astype(BF16)

    keep = lax.dynamic_slice_in_dim(attended, core * 24, 24, 0)
    give = swap(lax.dynamic_slice_in_dim(attended, 24 - core * 24, 24, 0))
    rows = jnp.concatenate([jnp.where(first, keep, give), jnp.where(first, give, keep)], axis=1)
    return jnp.dot(rows, out_weight, preferred_element_type=F32).astype(BF16)


def solution(mesh):
    fine = Mesh(mesh.devices.reshape(4, 2, 4, 4), ALL)
    return jax.shard_map(
        body,
        mesh=fine,
        in_specs=(P(ALL, None), P(ALL, None, None), P(ALL, None, None), P(), P(), P(), P()),
        out_specs=P(ALL, None),
        check_vma=False,
    )
```

```python
import itertools

import jax
import jax.numpy as jnp
from jax import lax
from jax.experimental import pallas as pl
from jax.experimental.pallas import tpu as pltpu
from jax.sharding import Mesh, PartitionSpec as P

HD = 64
LOG2E = 1.4426950408889634
TOP_STEP = 16.0
NO_TOP = -32768.0
CHIPS = ("y", "z", "x")
ALL = ("y", "core", "z", "x")
F32 = jnp.float32
BF16 = jnp.bfloat16


def attend_kernel(
    me, cnt, lst, q0, q1, q2, q3, k0, k1, v0, v1, out, pq, pj, k, vt, qm, acc, sa, sb, ta, tb, ha, hb, yb, sem
):
    copies = [
        pltpu.make_async_copy(src, dst, sem.at[i])
        for i, (src, dst) in enumerate(
            [(k0, k.at[pl.ds(0, 4)]), (k1, k.at[pl.ds(4, 4)]), (v0, vt.at[pl.ds(0, 4)]), (v1, vt.at[pl.ds(4, 4)])]
        )
    ]
    for copy in copies:
        copy.start()
    my_y, my_core, my_z, my_x = me[0], me[1], me[2], me[3]
    scale = HD ** -0.5 * LOG2E
    ones = jnp.ones((16, 256), BF16)

    def list_frame(qi, at):
        n = cnt[qi]

        def put(i, at):
            pj[at] = lst[qi * 8 + i]
            pq[at] = qi
            return at + 1

        return lax.fori_loop(0, n, put, at)

    total = lax.fori_loop(0, 12, list_frame, 0)
    for u in range(3):
        pq[total + u] = 12
        pj[total + u] = 0

    for r3, q in enumerate((q0, q1, q2, q3)):

        def load(r2, _, q=q, r3=r3):
            y = (my_y + 4 - jnp.where(my_core == 0, r2, r3)) % 4
            x = (my_x + 4 - jnp.where(my_core == 0, r3, r2)) % 4
            for rz in range(4):
                z = (my_z + 4 - rz) % 4
                block = q[r2 * 4 + rz].astype(F32)
                for c in range(2):
                    row = pl.multiple_of(y * 768 + (c * 16 + z * 4 + x) * 24, 8)
                    yb[pl.ds(row, 24), :512] = block[c * 24:(c + 1) * 24]
            return 0

        lax.fori_loop(0, 4, load, 0)

    def turn(qi, _):
        rows = pl.ds(pl.multiple_of(qi * 256, 256), 256)
        for hp in range(4):
            turned = yb[rows, hp * 128:(hp + 1) * 128].T.astype(BF16)
            zero = jnp.zeros((64, 256), BF16)
            qm[qi, 2 * hp] = jnp.concatenate([turned[:64], zero], axis=0)
            qm[qi, 2 * hp + 1] = jnp.concatenate([zero, turned[64:]], axis=0)

        @pl.when(cnt[qi] == 0)
        def _():
            yb[rows, 0:512] = jnp.zeros((256, 512), F32)
            lane = lax.broadcasted_iota(jnp.int32, (256, 128), 1)
            yb[rows, 512:640] = jnp.where(lane < 8, NO_TOP, 0.0)

        return 0

    lax.fori_loop(0, 12, turn, 0)
    for copy in copies:
        copy.wait()
    acc[...] = jnp.zeros_like(acc)
    ta[...] = jnp.full_like(ta, NO_TOP)
    tb[...] = jnp.full_like(tb, NO_TOP)
    qm[12] = jnp.zeros((8, 128, 256), BF16)

    def score(t, h, s_ref):
        qi, j = pq[t], pj[t]
        hp = h // 2
        keys = k[j, :, hp * 128:(hp + 1) * 128]
        s = jnp.dot(keys, qm[qi, h], preferred_element_type=F32) * scale
        s_ref[h] = s
        return jnp.max(s, axis=0, keepdims=True)

    def settle(t, highs, old_ref, new_ref, shrink_ref):
        first = pq[t] != pq[jnp.maximum(t - 1, 0)]
        old = jnp.where(first, NO_TOP, old_ref[...])
        high = jnp.concatenate(highs, axis=0)
        new = jnp.maximum(old, jnp.ceil(high * (1.0 / TOP_STEP)) * TOP_STEP)
        new_ref[...] = new
        shrink_ref[...] = jnp.exp2(old - new)

    def weigh(t, h, s_ref, top, shrink):
        j = pj[t]
        weights = jnp.exp2(s_ref[h] - top[h:h + 1]).astype(BF16)
        vals = jnp.concatenate([vt[j, h * 64:(h + 1) * 64, :], ones], axis=0)
        part = jnp.dot(vals, weights, preferred_element_type=F32)
        acc[h] = acc[h] * shrink[h:h + 1] + part

    def finish(t, top_ref):
        qi = pq[t]

        @pl.when((qi < 12) & (pq[t + 1] != qi))
        def _():
            rows = pl.ds(pl.multiple_of(qi * 256, 256), 256)
            totals = jnp.concatenate([acc[h, 64:65, :] for h in range(8)], axis=0)
            hi = totals.astype(BF16).astype(F32)
            extra = jnp.concatenate([top_ref[...], hi, totals - hi, jnp.zeros((104, 256), F32)], axis=0)
            for hp in range(4):
                both = jnp.concatenate([acc[2 * hp, :64, :], acc[2 * hp + 1, :64, :]], axis=0)
                yb[rows, hp * 128:(hp + 1) * 128] = both.T
            yb[rows, 512:640] = extra.T

    def half(t, s_now, s_next, t_now, t_next, h_now, h_next):
        top, shrink = t_now[...], h_now[...]
        highs = []
        for h in range(8):
            highs.append(score(t + 1, h, s_next))
            weigh(t, h, s_now, top, shrink)
        settle(t + 1, highs, t_now, t_next, h_next)
        finish(t, t_now)

    settle(0, [score(0, h, sa) for h in range(8)], tb, ta, ha)

    def two(u, _):
        half(2 * u, sa, sb, ta, tb, ha, hb)
        half(2 * u + 1, sb, sa, tb, ta, hb, ha)
        return 0

    lax.fori_loop(0, (total + 1) // 2, two, 0)

    def emit(y, _):
        for zx in range(16):
            data, packed = [], [jnp.zeros((8, 128), F32)] * 2
            for c in range(2):
                row = pl.multiple_of(y * 768 + (c * 16 + zx) * 24, 8)
                block = yb[pl.ds(row, 24), :]
                data.append(block[:, :512])
                for p in range(3):
                    g = c * 3 + p
                    piece = block[p * 8:(p + 1) * 8, 512:640]
                    if g % 4:
                        piece = pltpu.roll(piece, 32 * (g % 4), 1)
                    packed[g // 4] = packed[g // 4] + piece
            tail = jnp.concatenate(packed + [jnp.zeros((8, 256), F32)], axis=1)
            out[y * 16 + zx] = jnp.concatenate(data + [tail], axis=0).astype(BF16)
        return 0

    lax.fori_loop(0, 4, emit, 0)


def attend(me, cnt, lst, q, k0, k1, v0, v1):
    vmem = pl.BlockSpec(memory_space=pltpu.VMEM)
    smem = pl.BlockSpec(memory_space=pltpu.SMEM)
    whole = pl.BlockSpec(memory_space=pl.ANY)
    return pl.pallas_call(
        attend_kernel,
        out_shape=jax.ShapeDtypeStruct((64, 56, 512), BF16),
        in_specs=[smem] * 3 + [vmem] * 4 + [whole] * 4,
        out_specs=vmem,
        scratch_shapes=[
            pltpu.SMEM((104,), jnp.int32),
            pltpu.SMEM((104,), jnp.int32),
            pltpu.VMEM((8, 256, 512), BF16),
            pltpu.VMEM((8, 512, 256), BF16),
            pltpu.VMEM((13, 8, 128, 256), BF16),
            pltpu.VMEM((8, 80, 256), F32),
            pltpu.VMEM((8, 256, 256), F32),
            pltpu.VMEM((8, 256, 256), F32),
            pltpu.VMEM((8, 256), F32),
            pltpu.VMEM((8, 256), F32),
            pltpu.VMEM((8, 256), F32),
            pltpu.VMEM((8, 256), F32),
            pltpu.VMEM((3072, 640), F32),
            pltpu.SemaphoreType.DMA((4,)),
        ],
        compiler_params=pltpu.CompilerParams(vmem_limit_bytes=52 * 2**20),
        name="attend",
    )(me, cnt, lst, *q, k0, k1, v0, v1)


def combine_kernel(r, out, fs):
    n = r.shape[0]

    def find(s, best):
        for u in range(16):
            best = jnp.maximum(best, r[s * 16 + u, 48:56, 0:256].astype(F32))
        return best

    best = lax.fori_loop(0, n // 16, find, jnp.full((8, 256), NO_TOP, F32))

    def weigh(s, total):
        for u in range(16):
            e = r[s * 16 + u, 48:56, 0:256].astype(F32)
            f = jnp.exp2(jnp.minimum(e - best, 0.0))
            fs[pl.ds(pl.multiple_of((s * 16 + u) * 8, 8), 8), :] = f
            hl = [
                pltpu.roll(e[:, t * 128:(t + 1) * 128], 120, 1) + pltpu.roll(e[:, t * 128:(t + 1) * 128], 112, 1)
                for t in range(2)
            ]
            total = total + f * jnp.concatenate(hl, axis=1)
        return total

    total = lax.fori_loop(0, n // 16, weigh, jnp.zeros((8, 256), F32))
    src = lax.broadcasted_iota(jnp.int32, (128, 512), 0)
    dst = lax.broadcasted_iota(jnp.int32, (128, 512), 1) // 64
    spreads = [(src - 32 * g == dst).astype(BF16) for g in range(4)]

    def add(s8, numer):
        f = fs[pl.ds(pl.multiple_of(s8 * 64, 64), 64), :].astype(BF16)
        numer = list(numer)
        for g in range(6):
            t = g // 4
            wide = jnp.dot(f[:, t * 128:(t + 1) * 128], spreads[g % 4], preferred_element_type=F32)
            for u in range(8):
                numer[g] = numer[g] + wide[u * 8:(u + 1) * 8] * r[s8 * 8 + u, g * 8:(g + 1) * 8, :].astype(F32)
        return tuple(numer)

    numer = lax.fori_loop(0, n // 8, add, tuple(jnp.zeros((8, 512), F32) for _ in range(6)))
    for g in range(6):
        t = g // 4
        wide = jnp.dot(
            total[:, t * 128:(t + 1) * 128],
            spreads[g % 4].astype(F32),
            precision=lax.Precision.HIGHEST,
            preferred_element_type=F32,
        )
        out[g * 8:(g + 1) * 8, :] = numer[g] / wide


def combine(r):
    vmem = pl.BlockSpec(memory_space=pltpu.VMEM)
    return pl.pallas_call(
        combine_kernel,
        out_shape=jax.ShapeDtypeStruct((48, 512), F32),
        in_specs=[vmem],
        out_specs=vmem,
        scratch_shapes=[pltpu.VMEM((r.shape[0] * 8, 256), F32)],
        compiler_params=pltpu.CompilerParams(vmem_limit_bytes=32 * 2**20),
        name="combine",
    )(r)


def swap(x):
    return lax.ppermute(x, "core", [(0, 1), (1, 0)])


def shift(x, axes, by):
    pairs = []
    for y, c, z, w in itertools.product(range(4), range(2), range(4), range(4)):
        to = {"y": y, "z": z, "x": w}
        to[axes[c]] = (to[axes[c]] + by) % 4
        pairs.append((((y * 2 + c) * 4 + z) * 4 + w, ((to["y"] * 2 + c) * 4 + to["z"]) * 4 + to["x"]))
    return lax.ppermute(x, ALL, pairs)


def ring(x, axes):
    return [x] + [shift(x, axes, by) for by in (1, 2, 3)]


def body(queries, keys, values, frame_slot, covisible, counts, out_weight):
    core = lax.axis_index("core")
    device = lax.axis_index(ALL)
    partner = device + 16 - 32 * core
    own_col = core * 512
    other_col = 512 - own_col

    mine = lax.dynamic_slice_in_dim(queries, own_col, 512, 1)
    theirs = swap(lax.dynamic_slice_in_dim(queries, other_col, 512, 1))
    first = core == 0
    pair = jnp.concatenate([jnp.where(first, mine, theirs), jnp.where(first, theirs, mine)], axis=0)
    along_z = jnp.concatenate(ring(pair[None], "zz"), axis=0)
    plane = jnp.concatenate(ring(along_z, "yx"), axis=0)
    q_all = ring(plane, "xy")

    k_mine = lax.dynamic_slice_in_dim(keys, own_col, 512, 2)
    k_theirs = swap(lax.dynamic_slice_in_dim(keys, other_col, 512, 2))
    v_turned = jnp.swapaxes(values, 1, 2)
    v_mine = lax.dynamic_slice_in_dim(v_turned, own_col, 512, 1)
    v_theirs = swap(lax.dynamic_slice_in_dim(v_turned, other_col, 512, 1))

    four = jnp.arange(4, dtype=jnp.int32)
    slots = jnp.concatenate([device * 4 + four, partner * 4 + four])
    frame_ids = jnp.arange(frame_slot.shape[0], dtype=jnp.int32)
    local = jnp.sum(jnp.where(frame_slot[None, :] == slots[:, None], frame_ids[None, :], 0), axis=1)
    used = jnp.arange(covisible.shape[1], dtype=jnp.int32)[None, :] < counts[:, None]
    need = jnp.any((covisible[:, None, :] == local[None, :, None]) & used[:, None, :], axis=2)
    need_i = need.astype(jnp.int32)
    place = jnp.cumsum(need_i, axis=1) - need_i
    eight = jnp.arange(8, dtype=jnp.int32)
    hit = need[:, None, :] & (place[:, None, :] == eight[None, :, None])
    lst = jnp.sum(jnp.where(hit, eight[None, None, :], 0), axis=2).reshape(96)
    cnt = jnp.sum(need_i, axis=1)

    me = jnp.stack([lax.axis_index(a) for a in ALL]).astype(jnp.int32)
    sent = attend(me, cnt, lst, q_all, k_mine, k_theirs, v_mine, v_theirs)
    got = lax.all_to_all(sent, CHIPS, 0, 0)
    attended = combine(got).astype(BF16)

    keep = lax.dynamic_slice_in_dim(attended, core * 24, 24, 0)
    give = swap(lax.dynamic_slice_in_dim(attended, 24 - core * 24, 24, 0))
    rows = jnp.concatenate([jnp.where(first, keep, give), jnp.where(first, give, keep)], axis=1)
    return jnp.dot(rows, out_weight, preferred_element_type=F32).astype(BF16)


def solution(mesh):
    fine = Mesh(mesh.devices.reshape(4, 2, 4, 4), ALL)
    return jax.shard_map(
        body,
        mesh=fine,
        in_specs=(P(ALL, None), P(ALL, None, None), P(ALL, None, None), P(), P(), P(), P()),
        out_specs=P(ALL, None),
        check_vma=False,
    )
```

```python
import functools
import itertools

import jax
import jax.numpy as jnp
from jax import lax
from jax.experimental import pallas as pl
from jax.experimental.pallas import tpu as pltpu
from jax.sharding import Mesh, PartitionSpec as P

HD = 64
LOG2E = 1.4426950408889634
TOP_STEP = 16.0
NO_TOP = -32768.0
NH = 4
WIDE = NH * HD
ALL = ("y", "core", "z", "x")
F32 = jnp.float32
BF16 = jnp.bfloat16


def attend_kernel(
    me, cnt, lst, q0, q1, q2, q3, k0, k1, v0, v1, o0, o1, o2, o3,
    pq, pj, k, vt, qm, acc, sa, sb, ta, tb, ha, hb, yb, sem, *, part,
):
    my_y, my_core, my_z, my_x = me[0], me[1], me[2], me[3]
    col = pl.multiple_of(my_core * 512 + part * WIDE, WIDE)
    copies = [
        pltpu.make_async_copy(src, dst, sem.at[i])
        for i, (src, dst) in enumerate(
            [
                (k0.at[:, :, pl.ds(col, WIDE)], k.at[pl.ds(0, 4)]),
                (k1.at[:, :, pl.ds(col, WIDE)], k.at[pl.ds(4, 4)]),
                (v0.at[:, pl.ds(col, WIDE), :], vt.at[pl.ds(0, 4)]),
                (v1.at[:, pl.ds(col, WIDE), :], vt.at[pl.ds(4, 4)]),
            ]
        )
    ]
    for copy in copies:
        copy.start()
    scale = HD ** -0.5 * LOG2E
    ones = jnp.ones((16, 256), BF16)

    def list_frame(qi, at):
        def put(i, at):
            pj[at] = lst[qi * 8 + i]
            pq[at] = qi
            return at + 1

        return lax.fori_loop(0, cnt[qi], put, at)

    total = lax.fori_loop(0, 12, list_frame, 0)
    for u in range(3):
        pq[total + u] = 12
        pj[total + u] = 0

    def place(r2, r3, rz):
        y = lax.rem(my_y + 4 - jnp.where(my_core == 0, r2, r3), 4)
        x = lax.rem(my_x + 4 - jnp.where(my_core == 0, r3, r2), 4)
        z = lax.rem(my_z + 4 - rz, 4)
        return [pl.multiple_of(y * 768 + (c * 16 + z * 4 + x) * 24, 8) for c in range(2)]

    for r3, q in enumerate((q0, q1, q2, q3)):

        def load(r2, _, q=q, r3=r3):
            for rz in range(4):
                block = q[r2 * 4 + rz].astype(F32)
                for c, row in enumerate(place(r2, r3, rz)):
                    yb[pl.ds(row, 24), :WIDE] = block[c * 24:(c + 1) * 24]
            return 0

        lax.fori_loop(0, 4, load, 0)

    def turn(qi, _):
        rows = pl.ds(pl.multiple_of(qi * 256, 256), 256)
        zero = jnp.zeros((64, 256), BF16)
        for hp in range(NH // 2):
            turned = yb[rows, hp * 128:(hp + 1) * 128].T.astype(BF16)
            qm[qi, 2 * hp] = jnp.concatenate([turned[:64], zero], axis=0)
            qm[qi, 2 * hp + 1] = jnp.concatenate([zero, turned[64:]], axis=0)

        @pl.when(cnt[qi] == 0)
        def _():
            yb[rows, :WIDE] = jnp.zeros((256, WIDE), F32)
            lane = lax.broadcasted_iota(jnp.int32, (256, 128), 1)
            yb[rows, WIDE:] = jnp.where(lane < NH, NO_TOP, 0.0)

        return 0

    lax.fori_loop(0, 12, turn, 0)
    for copy in copies:
        copy.wait()
    acc[...] = jnp.zeros_like(acc)
    ta[...] = jnp.full_like(ta, NO_TOP)
    tb[...] = jnp.full_like(tb, NO_TOP)
    qm[12] = jnp.zeros((NH, 128, 256), BF16)

    def score(t, h, s_ref):
        hp = h // 2
        keys = k[pj[t], :, hp * 128:(hp + 1) * 128]
        s = jnp.dot(keys, qm[pq[t], h], preferred_element_type=F32) * scale
        s_ref[h] = s
        return jnp.max(s, axis=0, keepdims=True)

    def settle(t, highs, old_ref, new_ref, shrink_ref):
        first = pq[t] != pq[jnp.maximum(t - 1, 0)]
        old = jnp.where(first, NO_TOP, old_ref[...])
        high = jnp.concatenate(highs, axis=0)
        new = jnp.maximum(old, jnp.ceil(high * (1.0 / TOP_STEP)) * TOP_STEP)
        new_ref[...] = new
        shrink_ref[...] = jnp.exp2(old - new)

    def weigh(t, h, s_ref, top, shrink):
        weights = jnp.exp2(s_ref[h] - top[h:h + 1]).astype(BF16)
        vals = jnp.concatenate([vt[pj[t], h * 64:(h + 1) * 64, :], ones], axis=0)
        part = jnp.dot(vals, weights, preferred_element_type=F32)
        acc[h] = acc[h] * shrink[h:h + 1] + part

    def finish(t, top_ref):
        qi = pq[t]

        @pl.when((qi < 12) & (pq[t + 1] != qi))
        def _():
            rows = pl.ds(pl.multiple_of(qi * 256, 256), 256)
            totals = jnp.concatenate([acc[h, 64:65, :] for h in range(NH)], axis=0)
            hi = totals.astype(BF16).astype(F32)
            extra = [top_ref[...], hi, totals - hi, jnp.zeros((128 - 3 * NH, 256), F32)]
            for hp in range(NH // 2):
                both = jnp.concatenate([acc[2 * hp, :64, :], acc[2 * hp + 1, :64, :]], axis=0)
                yb[rows, hp * 128:(hp + 1) * 128] = both.T
            yb[rows, WIDE:] = jnp.concatenate(extra, axis=0).T

    def half(t, s_now, s_next, t_now, t_next, h_now, h_next):
        top, shrink = t_now[...], h_now[...]
        highs = []
        for h in range(NH):
            highs.append(score(t + 1, h, s_next))
            weigh(t, h, s_now, top, shrink)
        settle(t + 1, highs, t_now, t_next, h_next)
        finish(t, t_now)

    settle(0, [score(0, h, sa) for h in range(NH)], tb, ta, ha)

    def two(u, _):
        half(2 * u, sa, sb, ta, tb, ha, hb)
        half(2 * u + 1, sb, sa, tb, ta, hb, ha)
        return 0

    lax.fori_loop(0, (total + 1) // 2, two, 0)

    for r3, o in enumerate((o0, o1, o2, o3)):

        def emit(r2, _, o=o, r3=r3):
            for rz in range(4):
                data, tail = [], jnp.zeros((8, 128), F32)
                for c, row in enumerate(place(r2, r3, rz)):
                    block = yb[pl.ds(row, 24), :]
                    data.append(block[:, :WIDE])
                    for p in range(3):
                        piece = block[p * 8:(p + 1) * 8, WIDE:]
                        g = c * 3 + p
                        tail = tail + (pltpu.roll(piece, 16 * g, 1) if g else piece)
                data.append(jnp.concatenate([tail, jnp.zeros((8, WIDE - 128), F32)], axis=1))
                o[r2 * 4 + rz] = jnp.concatenate(data, axis=0).astype(BF16)
            return 0

        lax.fori_loop(0, 4, emit, 0)


def attend(me, cnt, lst, q, k0, k1, v0, v1, part):
    vmem = pl.BlockSpec(memory_space=pltpu.VMEM)
    smem = pl.BlockSpec(memory_space=pltpu.SMEM)
    whole = pl.BlockSpec(memory_space=pl.ANY)
    return pl.pallas_call(
        functools.partial(attend_kernel, part=part),
        out_shape=[jax.ShapeDtypeStruct((16, 56, WIDE), BF16)] * 4,
        in_specs=[smem] * 3 + [vmem] * 4 + [whole] * 4,
        out_specs=[vmem] * 4,
        scratch_shapes=[
            pltpu.SMEM((104,), jnp.int32),
            pltpu.SMEM((104,), jnp.int32),
            pltpu.VMEM((8, 256, WIDE), BF16),
            pltpu.VMEM((8, WIDE, 256), BF16),
            pltpu.VMEM((13, NH, 128, 256), BF16),
            pltpu.VMEM((NH, 80, 256), F32),
            pltpu.VMEM((NH, 256, 256), F32),
            pltpu.VMEM((NH, 256, 256), F32),
            pltpu.VMEM((NH, 256), F32),
            pltpu.VMEM((NH, 256), F32),
            pltpu.VMEM((NH, 256), F32),
            pltpu.VMEM((NH, 256), F32),
            pltpu.VMEM((3072, WIDE + 128), F32),
            pltpu.SemaphoreType.DMA((4,)),
        ],
        compiler_params=pltpu.CompilerParams(vmem_limit_bytes=36 * 2**20),
        cost_estimate=pl.CostEstimate(flops=10**10, bytes_accessed=2**23, transcendentals=2 * 10**7),
        name="attend",
    )(me, cnt, lst, *q, k0, k1, v0, v1)


def pack_kernel(p0, p1, p2, p3, k, v, o0, o1):
    for at, p in enumerate((p0, p1, p2, p3)):
        for c, o in enumerate((o0, o1)):
            o[at * 4:at * 4 + 4] = p[:, :, c * WIDE:(c + 1) * WIDE]


def pack(parts, k, v):
    vmem = pl.BlockSpec(memory_space=pltpu.VMEM)
    whole = pl.BlockSpec(memory_space=pl.ANY)
    return pl.pallas_call(
        pack_kernel,
        out_shape=[jax.ShapeDtypeStruct((16, 48, WIDE), BF16)] * 2,
        in_specs=[vmem] * 4 + [whole] * 2,
        out_specs=[vmem] * 2,
        name="pack",
    )(*parts, k, v)


def add_up(parts, spread):
    tails = [p[48:56, :128].astype(F32) for p in parts]
    best = functools.reduce(jnp.maximum, tails)
    shares = [jnp.exp2(jnp.minimum(t - best, 0.0)) for t in tails]
    total = sum(f * (pltpu.roll(t, 128 - NH, 1) + pltpu.roll(t, 128 - 2 * NH, 1)) for f, t in zip(shares, tails))
    stack = jnp.concatenate(shares, axis=0)
    stack = jnp.concatenate([stack] + [pltpu.roll(stack, 128 - 16 * g, 1) for g in range(1, 6)], axis=0)
    wide = jnp.dot(stack.astype(BF16), spread, preferred_element_type=F32)
    numer = []
    for g in range(6):
        at = g * 8 * len(parts)
        numer.append(
            sum(wide[at + s * 8:at + s * 8 + 8] * p[g * 8:g * 8 + 8, :].astype(F32) for s, p in enumerate(parts))
        )
    return numer, best, total


def make_spread():
    src = lax.broadcasted_iota(jnp.int32, (128, WIDE), 0)
    dst = lax.broadcasted_iota(jnp.int32, (128, WIDE), 1) // HD
    return src == dst


def merge_kernel(*refs, joint, blocks):
    parts, outs = refs[:-4], refs[-4:]
    spread = make_spread().astype(BF16)
    is_top = lax.broadcasted_iota(jnp.int32, (8, 128), 1) % 16 < NH
    for r, out in enumerate(outs):

        def one(b, _, r=r, out=out):
            for c in range(2):
                if joint:
                    held = [p[(r * blocks + b) * 2 + c] for p in parts]
                else:
                    held = [p[r * blocks + b] for p in parts[c * 4:c * 4 + 4]]
                numer, best, total = add_up(held, spread)
                total = jnp.where(is_top, total, 0.0)
                hi = total.astype(BF16).astype(F32)
                tail = jnp.where(is_top, best, 0.0) + pltpu.roll(hi, NH, 1) + pltpu.roll(total - hi, 2 * NH, 1)
                tail = jnp.concatenate([tail, jnp.zeros((8, WIDE - 128), F32)], axis=1)
                out[b * 2 + c] = jnp.concatenate(numer + [tail], axis=0).astype(BF16)
            return 0

        lax.fori_loop(0, blocks, one, 0)


def merge(parts, blocks):
    vmem = pl.BlockSpec(memory_space=pltpu.VMEM)
    return pl.pallas_call(
        functools.partial(merge_kernel, joint=len(parts) == 4, blocks=blocks),
        out_shape=[jax.ShapeDtypeStruct((blocks * 2, 56, WIDE), BF16)] * 4,
        in_specs=[vmem] * len(parts),
        out_specs=[vmem] * 4,
        compiler_params=pltpu.CompilerParams(vmem_limit_bytes=32 * 2**20),
        name="merge",
    )(*parts)


def close_kernel(*refs):
    parts, out = refs[:4], refs[4]
    spread = make_spread()
    for c in range(2):
        numer, _, total = add_up([p[c] for p in parts], spread.astype(BF16))
        totals = jnp.concatenate([total] + [pltpu.roll(total, 128 - 16 * g, 1) for g in range(1, 6)], axis=0)
        wide = jnp.dot(
            totals, spread.astype(F32), precision=lax.Precision.HIGHEST, preferred_element_type=F32
        )
        out[:, c * WIDE:(c + 1) * WIDE] = jnp.concatenate(numer, axis=0) / wide


def close(parts):
    vmem = pl.BlockSpec(memory_space=pltpu.VMEM)
    return pl.pallas_call(
        close_kernel,
        out_shape=jax.ShapeDtypeStruct((48, 512), F32),
        in_specs=[vmem] * 4,
        out_specs=vmem,
        name="close",
    )(*parts)


def swap(x):
    return lax.ppermute(x, "core", [(0, 1), (1, 0)])


def shift(x, axes, by):
    pairs = []
    for y, c, z, w in itertools.product(range(4), range(2), range(4), range(4)):
        to = {"y": y, "z": z, "x": w}
        to[axes[c]] = (to[axes[c]] + by) % 4
        pairs.append((((y * 2 + c) * 4 + z) * 4 + w, ((to["y"] * 2 + c) * 4 + to["z"]) * 4 + to["x"]))
    return lax.ppermute(x, ALL, pairs)


def ring(x, axes):
    return [x] + [shift(x, axes, by) for by in (1, 2, 3)]


def deliver(parts, axes):
    return [parts[0]] + [shift(parts[by], axes, -by) for by in (1, 2, 3)]


def body(queries, keys, values, frame_slot, covisible, counts, out_weight):
    core = lax.axis_index("core")
    device = lax.axis_index(ALL)
    partner = device + 16 - 32 * core
    own_col = core * 512
    other_col = 512 - own_col

    mine = lax.dynamic_slice_in_dim(queries, own_col, 512, 1)
    theirs = swap(lax.dynamic_slice_in_dim(queries, other_col, 512, 1))
    first = core == 0
    pair = jnp.concatenate([jnp.where(first, mine, theirs), jnp.where(first, theirs, mine)], axis=0)
    along_z = jnp.concatenate(ring(pair[None], "zz"), axis=0)
    k_theirs = swap(keys)
    v_turned = jnp.swapaxes(values, 1, 2)
    v_theirs = swap(v_turned)
    planes = pack(ring(along_z, "yx"), k_theirs, v_theirs)
    q_parts = [ring(plane, "xy") for plane in planes]

    four = jnp.arange(4, dtype=jnp.int32)
    slots = jnp.concatenate([device * 4 + four, partner * 4 + four])
    frame_ids = jnp.arange(frame_slot.shape[0], dtype=jnp.int32)
    local = jnp.sum(jnp.where(frame_slot[None, :] == slots[:, None], frame_ids[None, :], 0), axis=1)
    used = jnp.arange(covisible.shape[1], dtype=jnp.int32)[None, :] < counts[:, None]
    need = jnp.any((covisible[:, None, :] == local[None, :, None]) & used[:, None, :], axis=2)
    need_i = need.astype(jnp.int32)
    place = jnp.cumsum(need_i, axis=1) - need_i
    eight = jnp.arange(8, dtype=jnp.int32)
    hit = need[:, None, :] & (place[:, None, :] == eight[None, :, None])
    lst = jnp.sum(jnp.where(hit, eight[None, None, :], 0), axis=2).reshape(96)
    cnt = jnp.sum(need_i, axis=1)

    me = jnp.stack([lax.axis_index(a) for a in ALL]).astype(jnp.int32)
    sent = []
    for c in range(2):
        sent += deliver(attend(me, cnt, lst, q_parts[c], keys, k_theirs, v_turned, v_theirs, c), "xy")
    sent = deliver(merge(sent, 4), "yx")
    sent = deliver(merge(sent, 1), "zz")
    attended = close(sent).astype(BF16)

    keep = lax.dynamic_slice_in_dim(attended, core * 24, 24, 0)
    give = swap(lax.dynamic_slice_in_dim(attended, 24 - core * 24, 24, 0))
    rows = jnp.concatenate([jnp.where(first, keep, give), jnp.where(first, give, keep)], axis=1)
    return jnp.dot(rows, out_weight, preferred_element_type=F32).astype(BF16)


def solution(mesh):
    fine = Mesh(mesh.devices.reshape(4, 2, 4, 4), ALL)
    return jax.shard_map(
        body,
        mesh=fine,
        in_specs=(P(ALL, None), P(ALL, None, None), P(ALL, None, None), P(), P(), P(), P()),
        out_specs=P(ALL, None),
        check_vma=False,
    )
```

```python
import functools
import itertools

import jax
import jax.numpy as jnp
from jax import lax
from jax.experimental import pallas as pl
from jax.experimental.pallas import tpu as pltpu
from jax.sharding import Mesh, PartitionSpec as P

HD = 64
LOG2E = 1.4426950408889634
TOP_STEP = 16.0
NO_TOP = -32768.0
NH = 4
WIDE = NH * HD
ALL = ("y", "core", "z", "x")
F32 = jnp.float32
BF16 = jnp.bfloat16


def attend_kernel(
    me, cnt, lst, q0, q1, q2, q3, k0, k1, v0, o0, o1, o2, o3,
    pq, pj, ps, qv, k, vt, qm, acc, sb, top, shrink, yb, sem, *, part,
):
    my_y, my_core, my_z, my_x = me[0], me[1], me[2], me[3]
    col = pl.multiple_of(my_core * 512 + part * WIDE, WIDE)
    copies = [
        pltpu.make_async_copy(src, dst, sem.at[i])
        for i, (src, dst) in enumerate(
            [(q, qv.at[r3]) for r3, q in enumerate((q0, q1, q2, q3))]
            + [
                (k0.at[:, :, pl.ds(col, WIDE)], k.at[pl.ds(0, 4)]),
                (k1.at[:, :, pl.ds(col, WIDE)], k.at[pl.ds(4, 4)]),
                (v0.at[:, pl.ds(part * WIDE, WIDE), :], vt),
            ]
        )
    ]
    for copy in copies:
        copy.start()
    scale = HD ** -0.5 * LOG2E
    ones = jnp.ones((16, 256), BF16)

    def list_frame(qi, carry):
        at, slot = carry

        def put(i, at):
            pj[at] = lst[qi * 8 + i]
            pq[at] = qi
            ps[at] = slot
            return at + 1

        n = cnt[qi]
        return lax.fori_loop(0, n, put, at), jnp.where(n > 0, 1 - slot, slot)

    total, spare = lax.fori_loop(0, 12, list_frame, (jnp.int32(0), jnp.int32(0)))
    for u in range(5):
        pq[total + u] = 12
        pj[total + u] = 0
        ps[total + u] = spare

    def place(r2, r3, rz):
        y = lax.rem(my_y + 4 - jnp.where(my_core == 0, r2, r3), 4)
        x = lax.rem(my_x + 4 - jnp.where(my_core == 0, r3, r2), 4)
        z = lax.rem(my_z + 4 - rz, 4)
        return [pl.multiple_of(y * 768 + (c * 16 + z * 4 + x) * 24, 8) for c in range(2)]

    for r3 in range(4):
        copies[r3].wait()

        def load(r2, _, r3=r3):
            for rz in range(4):
                block = qv[r3, r2 * 4 + rz].astype(F32)
                for c, row in enumerate(place(r2, r3, rz)):
                    yb[pl.ds(row, 24), :WIDE] = block[c * 24:(c + 1) * 24]
            return 0

        for r2 in range(4):
            load(r2, 0)

    def turn(qi, _):
        rows = pl.ds(pl.multiple_of(qi * 256, 256), 256)
        zero = jnp.zeros((64, 256), BF16)
        for hp in range(NH // 2):
            turned = yb[rows, hp * 128:(hp + 1) * 128].T.astype(BF16)
            qm[qi, 2 * hp] = jnp.concatenate([turned[:64], zero], axis=0)
            qm[qi, 2 * hp + 1] = jnp.concatenate([zero, turned[64:]], axis=0)

        @pl.when(cnt[qi] == 0)
        def _():
            yb[rows, :WIDE] = jnp.zeros((256, WIDE), F32)
            lane = lax.broadcasted_iota(jnp.int32, (256, 128), 1)
            yb[rows, WIDE:] = jnp.where(lane < NH, NO_TOP, 0.0)

        return 0

    lax.fori_loop(0, 12, turn, 0)
    for copy in copies[4:]:
        copy.wait()
    acc[...] = jnp.zeros_like(acc)
    qm[12] = jnp.zeros((NH, 128, 256), BF16)

    def score(t, p, h):
        hp = h // 2
        keys = k[pj[t + p], :, hp * 128:(hp + 1) * 128]
        s = jnp.dot(keys, qm[pq[t + p], h], preferred_element_type=F32) * scale
        sb[p, h] = s
        return jnp.max(s, axis=0, keepdims=True)

    def settle(t, p, highs, old):
        first = pq[t + p] != pq[jnp.maximum(t + p - 1, 0)]
        old = jnp.where(first, NO_TOP, old)
        high = jnp.concatenate(highs, axis=0)
        new = jnp.maximum(old, jnp.ceil(high * (1.0 / TOP_STEP)) * TOP_STEP)
        top[p] = new
        shrink[p] = jnp.exp2(old - new)
        return new

    def weigh(t, p, h, tops, shrinks):
        weights = jnp.exp2(sb[p, h] - tops[h:h + 1]).astype(BF16)
        vals = jnp.concatenate([vt[pj[t + p], h * 64:(h + 1) * 64, :], ones], axis=0)
        part = jnp.dot(vals, weights, preferred_element_type=F32)
        at = ps[t + p]
        acc[at, h] = acc[at, h] * shrinks[h:h + 1] + part

    def finish(t, p, tops):
        qi = pq[t + p]

        @pl.when((qi < 12) & (pq[t + p + 1] != qi))
        def _():
            at = ps[t + p]
            rows = pl.ds(pl.multiple_of(qi * 256, 256), 256)
            totals = jnp.concatenate([acc[at, h, 64:65, :] for h in range(NH)], axis=0)
            hi = totals.astype(BF16).astype(F32)
            extra = [tops, hi, totals - hi, jnp.zeros((128 - 3 * NH, 256), F32)]
            for hp in range(NH // 2):
                both = jnp.concatenate([acc[at, 2 * hp, :64, :], acc[at, 2 * hp + 1, :64, :]], axis=0)
                yb[rows, hp * 128:(hp + 1) * 128] = both.T
            yb[rows, WIDE:] = jnp.concatenate(extra, axis=0).T

    old = jnp.full((NH, 256), NO_TOP, F32)
    for p in range(2):
        old = settle(0, p, [score(0, p, h) for h in range(NH)], old)

    def two(u, _):
        t = u * 2
        tops, shrinks = [top[0], top[1]], [shrink[0], shrink[1]]
        highs = [[], []]
        for p in range(2):
            for h in range(NH):
                weigh(t, p, h, tops[p], shrinks[p])
                highs[p].append(score(t + 2, p, h))
        old = settle(t + 2, 0, highs[0], tops[1])
        settle(t + 2, 1, highs[1], old)
        for p in range(2):
            finish(t, p, tops[p])
        return 0

    lax.fori_loop(0, (total + 1) // 2, two, 0)

    for r3, o in enumerate((o0, o1, o2, o3)):

        def emit(r2, _, o=o, r3=r3):
            for rz in range(4):
                data, tail = [], jnp.zeros((8, 128), F32)
                for c, row in enumerate(place(r2, r3, rz)):
                    block = yb[pl.ds(row, 24), :]
                    data.append(block[:, :WIDE])
                    for p in range(3):
                        piece = block[p * 8:(p + 1) * 8, WIDE:]
                        g = c * 3 + p
                        tail = tail + (pltpu.roll(piece, 16 * g, 1) if g else piece)
                data.append(jnp.concatenate([tail, jnp.zeros((8, WIDE - 128), F32)], axis=1))
                o[r2 * 4 + rz] = jnp.concatenate(data, axis=0).astype(BF16)
            return 0

        for r2 in range(4):
            emit(r2, 0)


def attend(me, cnt, lst, q, k0, k1, v0, part):
    vmem = pl.BlockSpec(memory_space=pltpu.VMEM)
    smem = pl.BlockSpec(memory_space=pltpu.SMEM)
    whole = pl.BlockSpec(memory_space=pl.ANY)
    return pl.pallas_call(
        functools.partial(attend_kernel, part=part),
        out_shape=[jax.ShapeDtypeStruct((16, 56, WIDE), BF16)] * 4,
        in_specs=[smem] * 3 + [whole] * 7,
        out_specs=[vmem] * 4,
        scratch_shapes=[
            pltpu.SMEM((104,), jnp.int32),
            pltpu.SMEM((104,), jnp.int32),
            pltpu.SMEM((104,), jnp.int32),
            pltpu.VMEM((4, 16, 48, WIDE), BF16),
            pltpu.VMEM((8, 256, WIDE), BF16),
            pltpu.VMEM((8, WIDE, 256), BF16),
            pltpu.VMEM((13, NH, 128, 256), BF16),
            pltpu.VMEM((2, NH, 80, 256), F32),
            pltpu.VMEM((2, NH, 256, 256), F32),
            pltpu.VMEM((2, NH, 256), F32),
            pltpu.VMEM((2, NH, 256), F32),
            pltpu.VMEM((3072, WIDE + 128), F32),
            pltpu.SemaphoreType.DMA((7,)),
        ],
        compiler_params=pltpu.CompilerParams(vmem_limit_bytes=36 * 2**20),
        cost_estimate=pl.CostEstimate(flops=10**10, bytes_accessed=2**23, transcendentals=2 * 10**7),
        name="attend",
    )(me, cnt, lst, *q, k0, k1, v0)


def turn_kernel(me, v0, v1, q, out, held, sem):
    col = pl.multiple_of(me[1] * 512, 512)
    copies = [
        pltpu.make_async_copy(v.at[:, :, pl.ds(col, 512)], held.at[pl.ds(i * 4, 4)], sem.at[i])
        for i, v in enumerate((v0, v1))
    ]
    for copy in copies:
        copy.start()
    for copy in copies:
        copy.wait()

    def one(j, _):
        for at in range(0, 512, 128):
            out[j, at:at + 128, :] = held[j, :, at:at + 128].astype(F32).T.astype(BF16)
        return 0

    lax.fori_loop(0, 8, one, 0)


def turn_values(me, v0, v1, q):
    vmem = pl.BlockSpec(memory_space=pltpu.VMEM)
    smem = pl.BlockSpec(memory_space=pltpu.SMEM)
    whole = pl.BlockSpec(memory_space=pl.ANY)
    return pl.pallas_call(
        turn_kernel,
        out_shape=jax.ShapeDtypeStruct((8, 512, 256), BF16),
        in_specs=[smem] + [whole] * 3,
        out_specs=vmem,
        scratch_shapes=[pltpu.VMEM((8, 256, 512), BF16), pltpu.SemaphoreType.DMA((2,))],
        cost_estimate=pl.CostEstimate(flops=10**6, bytes_accessed=2**23, transcendentals=0),
        compiler_params=pltpu.CompilerParams(vmem_limit_bytes=16 * 2**20),
        name="turn",
    )(me, v0, v1, q)


def pack_kernel(p0, p1, p2, p3, k, v, o0, o1):
    for at, p in enumerate((p0, p1, p2, p3)):
        for c, o in enumerate((o0, o1)):
            o[at * 4:at * 4 + 4] = p[:, :, c * WIDE:(c + 1) * WIDE]


def pack(parts, k, v):
    vmem = pl.BlockSpec(memory_space=pltpu.VMEM)
    whole = pl.BlockSpec(memory_space=pl.ANY)
    return pl.pallas_call(
        pack_kernel,
        out_shape=[jax.ShapeDtypeStruct((16, 48, WIDE), BF16)] * 2,
        in_specs=[vmem] * 4 + [whole] * 2,
        out_specs=[vmem] * 2,
        name="pack",
    )(*parts, k, v)


def add_up(parts, spread):
    tails = [p[48:56, :128].astype(F32) for p in parts]
    best = functools.reduce(jnp.maximum, tails)
    shares = [jnp.exp2(jnp.minimum(t - best, 0.0)) for t in tails]
    total = sum(f * (pltpu.roll(t, 128 - NH, 1) + pltpu.roll(t, 128 - 2 * NH, 1)) for f, t in zip(shares, tails))
    stack = jnp.concatenate(shares, axis=0)
    stack = jnp.concatenate([stack] + [pltpu.roll(stack, 128 - 16 * g, 1) for g in range(1, 6)], axis=0)
    wide = jnp.dot(stack.astype(BF16), spread, preferred_element_type=F32)
    numer = []
    for g in range(6):
        at = g * 8 * len(parts)
        numer.append(
            sum(wide[at + s * 8:at + s * 8 + 8] * p[g * 8:g * 8 + 8, :].astype(F32) for s, p in enumerate(parts))
        )
    return numer, best, total


def make_spread():
    src = lax.broadcasted_iota(jnp.int32, (128, WIDE), 0)
    dst = lax.broadcasted_iota(jnp.int32, (128, WIDE), 1) // HD
    return src == dst


def merge_kernel(*refs, joint, blocks):
    parts, outs = refs[:-4], refs[-4:]
    spread = make_spread().astype(BF16)
    is_top = lax.broadcasted_iota(jnp.int32, (8, 128), 1) % 16 < NH
    for r, out in enumerate(outs):

        def one(b, _, r=r, out=out):
            for c in range(2):
                if joint:
                    held = [p[(r * blocks + b) * 2 + c] for p in parts]
                else:
                    held = [p[r * blocks + b] for p in parts[c * 4:c * 4 + 4]]
                numer, best, total = add_up(held, spread)
                total = jnp.where(is_top, total, 0.0)
                hi = total.astype(BF16).astype(F32)
                tail = jnp.where(is_top, best, 0.0) + pltpu.roll(hi, NH, 1) + pltpu.roll(total - hi, 2 * NH, 1)
                tail = jnp.concatenate([tail, jnp.zeros((8, WIDE - 128), F32)], axis=1)
                out[b * 2 + c] = jnp.concatenate(numer + [tail], axis=0).astype(BF16)
            return 0

        for b in range(blocks):
            one(b, 0)


def merge(parts, blocks):
    vmem = pl.BlockSpec(memory_space=pltpu.VMEM)
    return pl.pallas_call(
        functools.partial(merge_kernel, joint=len(parts) == 4, blocks=blocks),
        out_shape=[jax.ShapeDtypeStruct((blocks * 2, 56, WIDE), BF16)] * 4,
        in_specs=[vmem] * len(parts),
        out_specs=[vmem] * 4,
        compiler_params=pltpu.CompilerParams(vmem_limit_bytes=32 * 2**20),
        name="merge",
    )(*parts)


def close_kernel(me, p0, p1, p2, p3, keep, give, both):
    parts = (p0, p1, p2, p3)
    spread = make_spread()
    for c in range(2):
        numer, _, total = add_up([p[c] for p in parts], spread.astype(BF16))
        totals = jnp.concatenate([total] + [pltpu.roll(total, 128 - 16 * g, 1) for g in range(1, 6)], axis=0)
        wide = jnp.dot(
            totals, spread.astype(F32), precision=lax.Precision.HIGHEST, preferred_element_type=F32
        )
        both[:, c * WIDE:(c + 1) * WIDE] = jnp.concatenate(numer, axis=0) / wide
    row = pl.multiple_of(me[1] * 24, 8)
    keep[...] = both[pl.ds(row, 24), :].astype(BF16)
    give[...] = both[pl.ds(24 - row, 24), :].astype(BF16)


def close(me, parts):
    vmem = pl.BlockSpec(memory_space=pltpu.VMEM)
    smem = pl.BlockSpec(memory_space=pltpu.SMEM)
    return pl.pallas_call(
        close_kernel,
        out_shape=[jax.ShapeDtypeStruct((24, 512), BF16)] * 2,
        in_specs=[smem] + [vmem] * 4,
        out_specs=[vmem] * 2,
        scratch_shapes=[pltpu.VMEM((48, 512), F32)],
        name="close",
    )(me, *parts)


def swap(x):
    return lax.ppermute(x, "core", [(0, 1), (1, 0)])


def shift(x, axes, by):
    pairs = []
    for y, c, z, w in itertools.product(range(4), range(2), range(4), range(4)):
        to = {"y": y, "z": z, "x": w}
        to[axes[c]] = (to[axes[c]] + by) % 4
        pairs.append((((y * 2 + c) * 4 + z) * 4 + w, ((to["y"] * 2 + c) * 4 + to["z"]) * 4 + to["x"]))
    return lax.ppermute(x, ALL, pairs)


def ring(x, axes):
    return [x] + [shift(x, axes, by) for by in (1, 2, 3)]


def deliver(parts, axes):
    return [parts[0]] + [shift(parts[by], axes, -by) for by in (1, 2, 3)]


def body(queries, keys, values, frame_slot, covisible, counts, out_weight):
    core = lax.axis_index("core")
    device = lax.axis_index(ALL)
    partner = device + 16 - 32 * core
    own_col = core * 512
    other_col = 512 - own_col

    mine = lax.dynamic_slice_in_dim(queries, own_col, 512, 1)
    theirs = swap(lax.dynamic_slice_in_dim(queries, other_col, 512, 1))
    first = core == 0
    pair = jnp.concatenate([jnp.where(first, mine, theirs), jnp.where(first, theirs, mine)], axis=0)
    along_z = jnp.concatenate(ring(pair[None], "zz"), axis=0)
    k_theirs, v_theirs = swap(keys), swap(values)
    planes = pack(ring(along_z, "yx"), k_theirs, v_theirs)
    me = jnp.stack([lax.axis_index(a) for a in ALL]).astype(jnp.int32)
    v_turned = turn_values(me, values, v_theirs, planes[0])
    q_parts = [ring(plane, "xy") for plane in planes]

    four = jnp.arange(4, dtype=jnp.int32)
    slots = jnp.concatenate([device * 4 + four, partner * 4 + four])
    frame_ids = jnp.arange(frame_slot.shape[0], dtype=jnp.int32)
    local = jnp.sum(jnp.where(frame_slot[None, :] == slots[:, None], frame_ids[None, :], 0), axis=1)
    used = jnp.arange(covisible.shape[1], dtype=jnp.int32)[None, :] < counts[:, None]
    need = jnp.any((covisible[:, None, :] == local[None, :, None]) & used[:, None, :], axis=2)
    need_i = need.astype(jnp.int32)
    place = jnp.cumsum(need_i, axis=1) - need_i
    eight = jnp.arange(8, dtype=jnp.int32)
    hit = need[:, None, :] & (place[:, None, :] == eight[None, :, None])
    lst = jnp.sum(jnp.where(hit, eight[None, None, :], 0), axis=2).reshape(96)
    cnt = jnp.sum(need_i, axis=1)

    sent = []
    for c in range(2):
        sent += deliver(attend(me, cnt, lst, q_parts[c], keys, k_theirs, v_turned, c), "xy")
    sent = deliver(merge(sent, 4), "yx")
    sent = deliver(merge(sent, 1), "zz")
    keep, give = close(me, sent)
    give = swap(give)
    rows = jnp.concatenate([jnp.where(first, keep, give), jnp.where(first, give, keep)], axis=1)
    return jnp.dot(rows, out_weight, preferred_element_type=F32).astype(BF16)


def solution(mesh):
    fine = Mesh(mesh.devices.reshape(4, 2, 4, 4), ALL)
    return jax.shard_map(
        body,
        mesh=fine,
        in_specs=(P(ALL, None), P(ALL, None, None), P(ALL, None, None), P(), P(), P(), P()),
        out_specs=P(ALL, None),
        check_vma=False,
    )
```

```python
import functools
import itertools

import jax
import jax.numpy as jnp
from jax import lax
from jax.experimental import pallas as pl
from jax.experimental.pallas import tpu as pltpu
from jax.sharding import Mesh, PartitionSpec as P

HD = 64
LOG2E = 1.4426950408889634
TOP_STEP = 16.0
NO_TOP = -32768.0
NH = 4
WIDE = NH * HD
ALL = ("y", "core", "z", "x")
F32 = jnp.float32
BF16 = jnp.bfloat16


def attend_kernel(
    me, cnt, lst, q0, q1, q2, q3, k0, k1, v0, o0, o1, o2, o3,
    pq, pj, ps, qv, k, vt, qm, acc, sb, top, shrink, yb, sem, *, part,
):
    my_y, my_core, my_x = me[0], me[1], me[3]
    col = pl.multiple_of(my_core * 512 + part * WIDE, WIDE)
    copies = [
        pltpu.make_async_copy(src, dst, sem.at[i])
        for i, (src, dst) in enumerate(
            [(q, qv.at[r3]) for r3, q in enumerate((q0, q1, q2, q3))]
            + [
                (k0.at[:, :, pl.ds(col, WIDE)], k.at[pl.ds(0, 4)]),
                (k1.at[:, :, pl.ds(col, WIDE)], k.at[pl.ds(4, 4)]),
                (v0.at[:, pl.ds(part * WIDE, WIDE), :], vt),
            ]
        )
    ]
    for copy in copies:
        copy.start()
    scale = HD ** -0.5 * LOG2E
    ones = jnp.ones((16, 256), BF16)

    def list_frame(qi, carry):
        at, slot = carry

        def put(i, at):
            pj[at] = lst[qi * 8 + i]
            pq[at] = qi
            ps[at] = slot
            return at + 1

        n = cnt[qi]
        return lax.fori_loop(0, n, put, at), jnp.where(n > 0, 1 - slot, slot)

    total, spare = lax.fori_loop(0, 12, list_frame, (jnp.int32(0), jnp.int32(0)))
    for u in range(5):
        pq[total + u] = 12
        pj[total + u] = 0
        ps[total + u] = spare

    def place(r2, r3, z):
        y = lax.rem(my_y + 4 - jnp.where(my_core == 0, r2, r3), 4)
        x = lax.rem(my_x + 4 - jnp.where(my_core == 0, r3, r2), 4)
        return [pl.multiple_of(y * 768 + (c * 16 + z * 4 + x) * 24, 8) for c in range(2)]

    for r3 in range(4):
        copies[r3].wait()
        for r2 in range(4):
            for z in range(4):
                for c, row in enumerate(place(r2, r3, z)):
                    yb[pl.ds(row, 24), :WIDE] = qv[r3, r2 * 8 + c * 4 + z].astype(F32)

    def turn(qi, _):
        rows = pl.ds(pl.multiple_of(qi * 256, 256), 256)
        zero = jnp.zeros((64, 256), BF16)
        for hp in range(NH // 2):
            turned = yb[rows, hp * 128:(hp + 1) * 128].T.astype(BF16)
            qm[qi, 2 * hp] = jnp.concatenate([turned[:64], zero], axis=0)
            qm[qi, 2 * hp + 1] = jnp.concatenate([zero, turned[64:]], axis=0)

        @pl.when(cnt[qi] == 0)
        def _():
            yb[rows, :WIDE] = jnp.zeros((256, WIDE), F32)
            lane = lax.broadcasted_iota(jnp.int32, (256, 128), 1)
            yb[rows, WIDE:] = jnp.where(lane < NH, NO_TOP, 0.0)

        return 0

    lax.fori_loop(0, 12, turn, 0)
    for copy in copies[4:]:
        copy.wait()
    acc[...] = jnp.zeros_like(acc)
    qm[12] = jnp.zeros((NH, 128, 256), BF16)

    def score(t, p, h):
        hp = h // 2
        keys = k[pj[t + p], :, hp * 128:(hp + 1) * 128]
        s = jnp.dot(keys, qm[pq[t + p], h], preferred_element_type=F32) * scale
        sb[p, h] = s
        return jnp.max(s, axis=0, keepdims=True)

    def settle(t, p, highs, old):
        first = pq[t + p] != pq[jnp.maximum(t + p - 1, 0)]
        old = jnp.where(first, NO_TOP, old)
        high = jnp.concatenate(highs, axis=0)
        new = jnp.maximum(old, jnp.ceil(high * (1.0 / TOP_STEP)) * TOP_STEP)
        top[p] = new
        shrink[p] = jnp.exp2(old - new)
        return new

    def weigh(t, p, h, tops, shrinks):
        weights = jnp.exp2(sb[p, h] - tops[h:h + 1]).astype(BF16)
        vals = jnp.concatenate([vt[pj[t + p], h * 64:(h + 1) * 64, :], ones], axis=0)
        part = jnp.dot(vals, weights, preferred_element_type=F32)
        at = ps[t + p]
        acc[at, h] = acc[at, h] * shrinks[h:h + 1] + part

    def finish(t, p, tops):
        qi = pq[t + p]

        @pl.when((qi < 12) & (pq[t + p + 1] != qi))
        def _():
            at = ps[t + p]
            rows = pl.ds(pl.multiple_of(qi * 256, 256), 256)
            totals = jnp.concatenate([acc[at, h, 64:65, :] for h in range(NH)], axis=0)
            hi = totals.astype(BF16).astype(F32)
            extra = [tops, hi, totals - hi, jnp.zeros((128 - 3 * NH, 256), F32)]
            for hp in range(NH // 2):
                both = jnp.concatenate([acc[at, 2 * hp, :64, :], acc[at, 2 * hp + 1, :64, :]], axis=0)
                yb[rows, hp * 128:(hp + 1) * 128] = both.T
            yb[rows, WIDE:] = jnp.concatenate(extra, axis=0).T

    old = jnp.full((NH, 256), NO_TOP, F32)
    for p in range(2):
        old = settle(0, p, [score(0, p, h) for h in range(NH)], old)

    def two(u, _):
        t = u * 2
        tops, shrinks = [top[0], top[1]], [shrink[0], shrink[1]]
        highs = [[], []]
        for p in range(2):
            for h in range(NH):
                weigh(t, p, h, tops[p], shrinks[p])
                highs[p].append(score(t + 2, p, h))
        old = settle(t + 2, 0, highs[0], tops[1])
        settle(t + 2, 1, highs[1], old)
        for p in range(2):
            finish(t, p, tops[p])
        return 0

    lax.fori_loop(0, (total + 1) // 2, two, 0)

    for r3, o in enumerate((o0, o1, o2, o3)):
        for r2 in range(4):
            for z in range(4):
                data, tail = [], jnp.zeros((8, 128), F32)
                for c, row in enumerate(place(r2, r3, z)):
                    block = yb[pl.ds(row, 24), :]
                    data.append(block[:, :WIDE])
                    for p in range(3):
                        piece = block[p * 8:(p + 1) * 8, WIDE:]
                        g = c * 3 + p
                        tail = tail + (pltpu.roll(piece, 16 * g, 1) if g else piece)
                data.append(jnp.concatenate([tail, jnp.zeros((8, WIDE - 128), F32)], axis=1))
                o[r2 * 4 + z] = jnp.concatenate(data, axis=0).astype(BF16)


def attend(me, cnt, lst, q, k0, k1, v0, part):
    vmem = pl.BlockSpec(memory_space=pltpu.VMEM)
    smem = pl.BlockSpec(memory_space=pltpu.SMEM)
    whole = pl.BlockSpec(memory_space=pl.ANY)
    return pl.pallas_call(
        functools.partial(attend_kernel, part=part),
        out_shape=[jax.ShapeDtypeStruct((16, 56, WIDE), BF16)] * 4,
        in_specs=[smem] * 3 + [whole] * 7,
        out_specs=[vmem] * 4,
        scratch_shapes=[
            pltpu.SMEM((104,), jnp.int32),
            pltpu.SMEM((104,), jnp.int32),
            pltpu.SMEM((104,), jnp.int32),
            pltpu.VMEM((4, 32, 24, WIDE), BF16),
            pltpu.VMEM((8, 256, WIDE), BF16),
            pltpu.VMEM((8, WIDE, 256), BF16),
            pltpu.VMEM((13, NH, 128, 256), BF16),
            pltpu.VMEM((2, NH, 80, 256), F32),
            pltpu.VMEM((2, NH, 256, 256), F32),
            pltpu.VMEM((2, NH, 256), F32),
            pltpu.VMEM((2, NH, 256), F32),
            pltpu.VMEM((3072, WIDE + 128), F32),
            pltpu.SemaphoreType.DMA((7,)),
        ],
        compiler_params=pltpu.CompilerParams(vmem_limit_bytes=36 * 2**20),
        cost_estimate=pl.CostEstimate(flops=10**10, bytes_accessed=2**23, transcendentals=2 * 10**7),
        name="attend",
    )(me, cnt, lst, *q, k0, k1, v0)


def turn_kernel(me, v0, v1, q, out, held, sem):
    col = pl.multiple_of(me[1] * 512, 512)
    copies = [
        pltpu.make_async_copy(v.at[:, :, pl.ds(col, 512)], held.at[pl.ds(i * 4, 4)], sem.at[i])
        for i, v in enumerate((v0, v1))
    ]
    for copy in copies:
        copy.start()
    for copy in copies:
        copy.wait()

    def one(j, _):
        for at in range(0, 512, 128):
            out[j, at:at + 128, :] = held[j, :, at:at + 128].astype(F32).T.astype(BF16)
        return 0

    lax.fori_loop(0, 8, one, 0)


def turn_values(me, v0, v1, q):
    vmem = pl.BlockSpec(memory_space=pltpu.VMEM)
    smem = pl.BlockSpec(memory_space=pltpu.SMEM)
    whole = pl.BlockSpec(memory_space=pl.ANY)
    return pl.pallas_call(
        turn_kernel,
        out_shape=jax.ShapeDtypeStruct((8, 512, 256), BF16),
        in_specs=[smem] + [whole] * 3,
        out_specs=vmem,
        scratch_shapes=[pltpu.VMEM((8, 256, 512), BF16), pltpu.SemaphoreType.DMA((2,))],
        cost_estimate=pl.CostEstimate(flops=10**6, bytes_accessed=2**23, transcendentals=0),
        compiler_params=pltpu.CompilerParams(vmem_limit_bytes=16 * 2**20),
        name="turn",
    )(me, v0, v1, q)


def pack_kernel(p0, p1, p2, p3, k, v, o0, o1, sem):
    copies = []
    for at, p in enumerate((p0, p1, p2, p3)):
        for c, o in enumerate((o0, o1)):
            copies.append(
                pltpu.make_async_copy(
                    p.at[:, :, pl.ds(c * WIDE, WIDE)], o.at[pl.ds(at * 8, 8)], sem.at[at * 2 + c]
                )
            )
    for copy in copies:
        copy.start()
    for copy in copies:
        copy.wait()


def pack(parts, k, v):
    whole = pl.BlockSpec(memory_space=pl.ANY)
    return pl.pallas_call(
        pack_kernel,
        out_shape=[jax.ShapeDtypeStruct((32, 24, WIDE), BF16)] * 2,
        in_specs=[whole] * 6,
        out_specs=[whole] * 2,
        scratch_shapes=[pltpu.SemaphoreType.DMA((8,))],
        name="pack",
    )(*parts, k, v)


def add_up(data, tails, spread):
    n = len(data)
    best = functools.reduce(jnp.maximum, tails)
    shares = [jnp.exp2(jnp.minimum(t - best, 0.0)) for t in tails]
    total = sum(f * (pltpu.roll(t, 128 - NH, 1) + pltpu.roll(t, 128 - 2 * NH, 1)) for f, t in zip(shares, tails))
    stack = jnp.concatenate(shares, axis=0)
    groups = data[0].shape[0] // 8
    stack = jnp.concatenate([stack] + [pltpu.roll(stack, 128 - 16 * g, 1) for g in range(1, groups)], axis=0)
    wide = jnp.dot(stack.astype(BF16), spread, preferred_element_type=F32)
    numer = []
    for g in range(groups):
        at = g * 8 * n
        numer.append(
            sum(wide[at + s * 8:at + s * 8 + 8] * d[g * 8:g * 8 + 8, :].astype(F32) for s, d in enumerate(data))
        )
    return numer, best, total


def make_spread():
    src = lax.broadcasted_iota(jnp.int32, (128, WIDE), 0)
    dst = lax.broadcasted_iota(jnp.int32, (128, WIDE), 1) // HD
    return src == dst


def add_blocks(held, spread, is_top):
    data, tails = [p[:48] for p in held], [p[48:56, :128].astype(F32) for p in held]
    numer, best, total = add_up(data, tails, spread)
    total = jnp.where(is_top, total, 0.0)
    hi = total.astype(BF16).astype(F32)
    tail = jnp.where(is_top, best, 0.0) + pltpu.roll(hi, NH, 1) + pltpu.roll(total - hi, 2 * NH, 1)
    return numer, jnp.concatenate([tail, jnp.zeros((8, WIDE - 128), F32)], axis=1)


def merge_kernel(*refs):
    parts, outs = refs[:8], refs[8:]
    spread = make_spread().astype(BF16)
    is_top = lax.broadcasted_iota(jnp.int32, (8, 128), 1) % 16 < NH
    for r, out in enumerate(outs):
        for z in range(4):
            for c in range(2):
                numer, tail = add_blocks([p[r * 4 + z] for p in parts[c * 4:c * 4 + 4]], spread, is_top)
                out[z * 2 + c] = jnp.concatenate(numer + [tail], axis=0).astype(BF16)


def merge(parts):
    vmem = pl.BlockSpec(memory_space=pltpu.VMEM)
    return pl.pallas_call(
        merge_kernel,
        out_shape=[jax.ShapeDtypeStruct((8, 56, WIDE), BF16)] * 4,
        in_specs=[vmem] * 8,
        out_specs=[vmem] * 4,
        compiler_params=pltpu.CompilerParams(vmem_limit_bytes=32 * 2**20),
        name="merge",
    )(*parts)


def split_kernel(p0, p1, p2, p3, out):
    spread = make_spread().astype(BF16)
    is_top = lax.broadcasted_iota(jnp.int32, (8, 128), 1) % 16 < NH
    for z in range(4):
        for c in range(2):
            numer, tail = add_blocks([p[z * 2 + c] for p in (p0, p1, p2, p3)], spread, is_top)
            for core in range(2):
                rows = jnp.concatenate(numer[core * 3:core * 3 + 3] + [tail], axis=0)
                out[core * 4 + z, c] = rows.astype(BF16)


def split(parts):
    vmem = pl.BlockSpec(memory_space=pltpu.VMEM)
    return pl.pallas_call(
        split_kernel,
        out_shape=jax.ShapeDtypeStruct((8, 2, 32, WIDE), BF16),
        in_specs=[vmem] * 4,
        out_specs=vmem,
        name="split",
    )(*parts)


def close_kernel(me, got, weight, out, rows):
    spread = make_spread()
    for core in range(2):
        for c in range(2):
            held = [got[core * 4 + z, c] for z in range(4)]
            tails = [p[24:32, :128].astype(F32) for p in held]
            tails = [jnp.where(me[1] == 0, t, pltpu.roll(t, 128 - 48, 1)) for t in tails]
            numer, _, total = add_up([p[:24] for p in held], tails, spread.astype(BF16))
            totals = jnp.concatenate([total] + [pltpu.roll(total, 128 - 16 * g, 1) for g in range(1, 3)], axis=0)
            wide = jnp.dot(
                totals, spread.astype(F32), precision=lax.Precision.HIGHEST, preferred_element_type=F32
            )
            at = core * 512 + c * WIDE
            rows[:, at:at + WIDE] = (jnp.concatenate(numer, axis=0) / wide).astype(BF16)
    out[...] = jnp.dot(rows[...], weight[...], preferred_element_type=F32).astype(BF16)


def close(me, got, weight):
    vmem = pl.BlockSpec(memory_space=pltpu.VMEM)
    smem = pl.BlockSpec(memory_space=pltpu.SMEM)
    return pl.pallas_call(
        close_kernel,
        out_shape=jax.ShapeDtypeStruct((24, 1024), BF16),
        in_specs=[smem, vmem, vmem],
        out_specs=vmem,
        scratch_shapes=[pltpu.VMEM((24, 1024), BF16)],
        name="close",
    )(me, got, weight)


def swap(x):
    return lax.ppermute(x, "core", [(0, 1), (1, 0)])


def shift(x, axes, by):
    pairs = []
    for y, c, z, w in itertools.product(range(4), range(2), range(4), range(4)):
        to = {"y": y, "z": z, "x": w}
        to[axes[c]] = (to[axes[c]] + by) % 4
        pairs.append((((y * 2 + c) * 4 + z) * 4 + w, ((to["y"] * 2 + c) * 4 + to["z"]) * 4 + to["x"]))
    return lax.ppermute(x, ALL, pairs)


def ring(x, axes):
    return [x] + [shift(x, axes, by) for by in (1, 2, 3)]


def deliver(parts, axes):
    return [parts[0]] + [shift(parts[by], axes, -by) for by in (1, 2, 3)]


def body(queries, keys, values, frame_slot, covisible, counts, out_weight):
    core = lax.axis_index("core")
    device = lax.axis_index(ALL)
    partner = device + 16 - 32 * core
    halves = jnp.stack([queries[:, :512]] * 4 + [queries[:, 512:]] * 4)
    along_z = lax.all_to_all(halves, ("core", "z"), 0, 0)
    k_theirs, v_theirs = swap(keys), swap(values)
    planes = pack(ring(along_z, "yx"), k_theirs, v_theirs)
    me = jnp.stack([lax.axis_index(a) for a in ALL]).astype(jnp.int32)
    v_turned = turn_values(me, values, v_theirs, planes[0])
    q_parts = [ring(plane, "xy") for plane in planes]

    four = jnp.arange(4, dtype=jnp.int32)
    slots = jnp.concatenate([device * 4 + four, partner * 4 + four])
    frame_ids = jnp.arange(frame_slot.shape[0], dtype=jnp.int32)
    local = jnp.sum(jnp.where(frame_slot[None, :] == slots[:, None], frame_ids[None, :], 0), axis=1)
    used = jnp.arange(covisible.shape[1], dtype=jnp.int32)[None, :] < counts[:, None]
    need = jnp.any((covisible[:, None, :] == local[None, :, None]) & used[:, None, :], axis=2)
    need_i = need.astype(jnp.int32)
    place = jnp.cumsum(need_i, axis=1) - need_i
    eight = jnp.arange(8, dtype=jnp.int32)
    hit = need[:, None, :] & (place[:, None, :] == eight[None, :, None])
    lst = jnp.sum(jnp.where(hit, eight[None, None, :], 0), axis=2).reshape(96)
    cnt = jnp.sum(need_i, axis=1)

    sent = []
    for c in range(2):
        sent += deliver(attend(me, cnt, lst, q_parts[c], keys, k_theirs, v_turned, c), "xy")
    sent = split(deliver(merge(sent), "yx"))
    got = lax.all_to_all(sent, ("core", "z"), 0, 0)
    return close(me, got, out_weight)


def solution(mesh):
    fine = Mesh(mesh.devices.reshape(4, 2, 4, 4), ALL)
    return jax.shard_map(
        body,
        mesh=fine,
        in_specs=(P(ALL, None), P(ALL, None, None), P(ALL, None, None), P(), P(), P(), P()),
        out_specs=P(ALL, None),
        check_vma=False,
    )
```

```python
import functools
import itertools

import jax
import jax.numpy as jnp
from jax import lax
from jax.experimental import pallas as pl
from jax.experimental.pallas import tpu as pltpu
from jax.sharding import Mesh, PartitionSpec as P

HD = 64
LOG2E = 1.4426950408889634
TOP_STEP = 16.0
NO_TOP = -32768.0
NH = 4
WIDE = NH * HD
ALL = ("y", "core", "z", "x")
F32 = jnp.float32
BF16 = jnp.bfloat16


def attend_kernel(
    me, cnt, lst, *refs, part,
):
    n_out = 4 if part == 0 else 1
    qs, (k0, k1, v0), outs = refs[:4], refs[4:7], refs[7:7 + n_out]
    pq, pj, ps, qv, k, vt, qm, acc, sb, top, shrink, yb, sem = refs[7 + n_out:]
    my_y, my_core, my_z, my_x = me[0], me[1], me[2], me[3]
    col = pl.multiple_of(my_core * 512 + part * WIDE, WIDE)
    copies = [
        pltpu.make_async_copy(src, dst, sem.at[i])
        for i, (src, dst) in enumerate(
            [(q, qv.at[pl.ds(i * q.shape[0], q.shape[0])]) for i, q in enumerate(qs)]
            + [
                (k0.at[:, :, pl.ds(col, WIDE)], k.at[pl.ds(0, 4)]),
                (k1.at[:, :, pl.ds(col, WIDE)], k.at[pl.ds(4, 4)]),
                (v0.at[:, pl.ds(part * WIDE, WIDE), :], vt),
            ]
        )
    ]
    for copy in copies:
        copy.start()
    scale = HD ** -0.5 * LOG2E
    ones = jnp.ones((16, 256), BF16)

    def list_frame(qi, carry):
        at, slot = carry

        def put(i, at):
            pj[at] = lst[qi * 8 + i]
            pq[at] = qi
            ps[at] = slot
            return at + 1

        n = cnt[qi]
        return lax.fori_loop(0, n, put, at), jnp.where(n > 0, 1 - slot, slot)

    total, spare = lax.fori_loop(0, 12, list_frame, (jnp.int32(0), jnp.int32(0)))
    for u in range(5):
        pq[total + u] = 12
        pj[total + u] = 0
        ps[total + u] = spare

    def place(r2, r3, rz):
        y = lax.rem(my_y + 4 - jnp.where(my_core == 0, r2, r3), 4)
        x = lax.rem(my_x + 4 - jnp.where(my_core == 0, r3, r2), 4)
        z = lax.rem(my_z + 4 - rz, 4)
        return [pl.multiple_of(y * 768 + (c * 16 + z * 4 + x) * 24, 8) for c in range(2)]

    def rows_of(y, z, x):
        return [pl.multiple_of(y * 768 + (c * 16 + z * 4 + x) * 24, 8) for c in range(2)]

    near = [[place(r2, r3, rz) for r2 in range(4) for rz in range(4)] for r3 in range(4)]
    plain = [[rows_of(y, z, x) for y in range(4) for z in range(4) for x in range(4)]]
    for i, spot in enumerate(near):
        copies[i].wait()
        for b, rows in enumerate(spot):
            block = qv[i * len(spot) + b].astype(F32)
            for c, row in enumerate(rows):
                yb[pl.ds(row, 24), :WIDE] = block[c * 24:(c + 1) * 24]

    def turn(qi, _):
        rows = pl.ds(pl.multiple_of(qi * 256, 256), 256)
        zero = jnp.zeros((64, 256), BF16)
        for hp in range(NH // 2):
            turned = yb[rows, hp * 128:(hp + 1) * 128].T.astype(BF16)
            qm[qi, 2 * hp] = jnp.concatenate([turned[:64], zero], axis=0)
            qm[qi, 2 * hp + 1] = jnp.concatenate([zero, turned[64:]], axis=0)

        @pl.when(cnt[qi] == 0)
        def _():
            yb[rows, :WIDE] = jnp.zeros((256, WIDE), F32)
            lane = lax.broadcasted_iota(jnp.int32, (256, 128), 1)
            yb[rows, WIDE:] = jnp.where(lane < NH, NO_TOP, 0.0)

        return 0

    lax.fori_loop(0, 12, turn, 0)
    for copy in copies[4:]:
        copy.wait()
    acc[...] = jnp.zeros_like(acc)
    qm[12] = jnp.zeros((NH, 128, 256), BF16)

    def score(t, p, h):
        hp = h // 2
        keys = k[pj[t + p], :, hp * 128:(hp + 1) * 128]
        s = jnp.dot(keys, qm[pq[t + p], h], preferred_element_type=F32) * scale
        sb[p, h] = s
        return jnp.max(s, axis=0, keepdims=True)

    def settle(t, p, highs, old):
        first = pq[t + p] != pq[jnp.maximum(t + p - 1, 0)]
        old = jnp.where(first, NO_TOP, old)
        high = jnp.concatenate(highs, axis=0)
        new = jnp.maximum(old, jnp.ceil(high * (1.0 / TOP_STEP)) * TOP_STEP)
        top[p] = new
        shrink[p] = jnp.exp2(old - new)
        return new

    def weigh(t, p, h, tops, shrinks):
        weights = jnp.exp2(sb[p, h] - tops[h:h + 1]).astype(BF16)
        vals = jnp.concatenate([vt[pj[t + p], h * 64:(h + 1) * 64, :], ones], axis=0)
        part = jnp.dot(vals, weights, preferred_element_type=F32)
        at = ps[t + p]
        acc[at, h] = acc[at, h] * shrinks[h:h + 1] + part

    def finish(t, p, tops):
        qi = pq[t + p]

        @pl.when((qi < 12) & (pq[t + p + 1] != qi))
        def _():
            at = ps[t + p]
            rows = pl.ds(pl.multiple_of(qi * 256, 256), 256)
            totals = jnp.concatenate([acc[at, h, 64:65, :] for h in range(NH)], axis=0)
            hi = totals.astype(BF16).astype(F32)
            extra = [tops, hi, totals - hi, jnp.zeros((128 - 3 * NH, 256), F32)]
            for hp in range(NH // 2):
                both = jnp.concatenate([acc[at, 2 * hp, :64, :], acc[at, 2 * hp + 1, :64, :]], axis=0)
                yb[rows, hp * 128:(hp + 1) * 128] = both.T
            yb[rows, WIDE:] = jnp.concatenate(extra, axis=0).T

    old = jnp.full((NH, 256), NO_TOP, F32)
    for p in range(2):
        old = settle(0, p, [score(0, p, h) for h in range(NH)], old)

    def two(u, _):
        t = u * 2
        tops, shrinks = [top[0], top[1]], [shrink[0], shrink[1]]
        highs = [[], []]
        for p in range(2):
            for h in range(NH):
                weigh(t, p, h, tops[p], shrinks[p])
                highs[p].append(score(t + 2, p, h))
        old = settle(t + 2, 0, highs[0], tops[1])
        settle(t + 2, 1, highs[1], old)
        for p in range(2):
            finish(t, p, tops[p])
        return 0

    lax.fori_loop(0, (total + 1) // 2, two, 0)

    for o, spot in zip(outs, near if part == 0 else plain):
        for b, rows in enumerate(spot):
            data, tail = [], jnp.zeros((8, 128), F32)
            for c, row in enumerate(rows):
                block = yb[pl.ds(row, 24), :]
                data.append(block[:, :WIDE])
                for p in range(3):
                    piece = block[p * 8:(p + 1) * 8, WIDE:]
                    g = c * 3 + p
                    tail = tail + (pltpu.roll(piece, 16 * g, 1) if g else piece)
            data.append(jnp.concatenate([tail, jnp.zeros((8, WIDE - 128), F32)], axis=1))
            o[b] = jnp.concatenate(data, axis=0).astype(BF16)


def attend(me, cnt, lst, q, k0, k1, v0, part):
    n_out = 4 if part == 0 else 1
    vmem = pl.BlockSpec(memory_space=pltpu.VMEM)
    smem = pl.BlockSpec(memory_space=pltpu.SMEM)
    whole = pl.BlockSpec(memory_space=pl.ANY)
    return pl.pallas_call(
        functools.partial(attend_kernel, part=part),
        out_shape=[jax.ShapeDtypeStruct((64 // n_out, 56, WIDE), BF16)] * n_out,
        in_specs=[smem] * 3 + [whole] * 7,
        out_specs=[vmem] * n_out,
        scratch_shapes=[
            pltpu.SMEM((104,), jnp.int32),
            pltpu.SMEM((104,), jnp.int32),
            pltpu.SMEM((104,), jnp.int32),
            pltpu.VMEM((64, 48, WIDE), BF16),
            pltpu.VMEM((8, 256, WIDE), BF16),
            pltpu.VMEM((8, WIDE, 256), BF16),
            pltpu.VMEM((13, NH, 128, 256), BF16),
            pltpu.VMEM((2, NH, 80, 256), F32),
            pltpu.VMEM((2, NH, 256, 256), F32),
            pltpu.VMEM((2, NH, 256), F32),
            pltpu.VMEM((2, NH, 256), F32),
            pltpu.VMEM((3072, WIDE + 128), F32),
            pltpu.SemaphoreType.DMA((7,)),
        ],
        compiler_params=pltpu.CompilerParams(vmem_limit_bytes=36 * 2**20),
        cost_estimate=pl.CostEstimate(flops=10**10, bytes_accessed=2**23, transcendentals=2 * 10**7),
        name="attend",
    )(me, cnt, lst, *q, k0, k1, v0)


def turn_kernel(me, v0, v1, q, out, held, sem):
    col = pl.multiple_of(me[1] * 512, 512)
    copies = [
        pltpu.make_async_copy(v.at[:, :, pl.ds(col, 512)], held.at[pl.ds(i * 4, 4)], sem.at[i])
        for i, v in enumerate((v0, v1))
    ]
    for copy in copies:
        copy.start()
    for copy in copies:
        copy.wait()

    def one(j, _):
        for at in range(0, 512, 128):
            out[j, at:at + 128, :] = held[j, :, at:at + 128].astype(F32).T.astype(BF16)
        return 0

    lax.fori_loop(0, 8, one, 0)


def turn_values(me, v0, v1, q):
    vmem = pl.BlockSpec(memory_space=pltpu.VMEM)
    smem = pl.BlockSpec(memory_space=pltpu.SMEM)
    whole = pl.BlockSpec(memory_space=pl.ANY)
    return pl.pallas_call(
        turn_kernel,
        out_shape=jax.ShapeDtypeStruct((8, 512, 256), BF16),
        in_specs=[smem] + [whole] * 3,
        out_specs=vmem,
        scratch_shapes=[pltpu.VMEM((8, 256, 512), BF16), pltpu.SemaphoreType.DMA((2,))],
        cost_estimate=pl.CostEstimate(flops=10**6, bytes_accessed=2**23, transcendentals=0),
        compiler_params=pltpu.CompilerParams(vmem_limit_bytes=16 * 2**20),
        name="turn",
    )(me, v0, v1, q)


def pack_kernel(p0, p1, p2, p3, k, v, o0, o1):
    for at, p in enumerate((p0, p1, p2, p3)):
        for c, o in enumerate((o0, o1)):
            o[at * 4:at * 4 + 4] = p[:, :, c * WIDE:(c + 1) * WIDE]


def pack(parts, k, v):
    vmem = pl.BlockSpec(memory_space=pltpu.VMEM)
    whole = pl.BlockSpec(memory_space=pl.ANY)
    return pl.pallas_call(
        pack_kernel,
        out_shape=[jax.ShapeDtypeStruct((16, 48, WIDE), BF16)] * 2,
        in_specs=[vmem] * 4 + [whole] * 2,
        out_specs=[vmem] * 2,
        name="pack",
    )(*parts, k, v)


def add_up(data, tails, spread):
    n = len(data)
    best = functools.reduce(jnp.maximum, tails)
    shares = [jnp.exp2(jnp.minimum(t - best, 0.0)) for t in tails]
    total = sum(f * (pltpu.roll(t, 128 - NH, 1) + pltpu.roll(t, 128 - 2 * NH, 1)) for f, t in zip(shares, tails))
    stack = jnp.concatenate(shares, axis=0)
    groups = data[0].shape[0] // 8
    stack = jnp.concatenate([stack] + [pltpu.roll(stack, 128 - 16 * g, 1) for g in range(1, groups)], axis=0)
    wide = jnp.dot(stack.astype(BF16), spread, preferred_element_type=F32)
    numer = []
    for g in range(groups):
        at = g * 8 * n
        numer.append(
            sum(wide[at + s * 8:at + s * 8 + 8] * d[g * 8:g * 8 + 8, :].astype(F32) for s, d in enumerate(data))
        )
    return numer, best, total


def make_spread():
    src = lax.broadcasted_iota(jnp.int32, (128, WIDE), 0)
    dst = lax.broadcasted_iota(jnp.int32, (128, WIDE), 1) // HD
    return src == dst


def add_blocks(held, spread, is_top):
    data, tails = [p[:48] for p in held], [p[48:56, :128].astype(F32) for p in held]
    numer, best, total = add_up(data, tails, spread)
    total = jnp.where(is_top, total, 0.0)
    hi = total.astype(BF16).astype(F32)
    tail = jnp.where(is_top, best, 0.0) + pltpu.roll(hi, NH, 1) + pltpu.roll(total - hi, 2 * NH, 1)
    return numer, jnp.concatenate([tail, jnp.zeros((8, WIDE - 128), F32)], axis=1)


def merge_kernel(p0, p1, p2, p3, after, *outs):
    spread = make_spread().astype(BF16)
    is_top = lax.broadcasted_iota(jnp.int32, (8, 128), 1) % 16 < NH
    blocks = outs[0].shape[0]
    for r, out in enumerate(outs):
        for b in range(blocks):
            numer, tail = add_blocks([p[r * blocks + b] for p in (p0, p1, p2, p3)], spread, is_top)
            out[b] = jnp.concatenate(numer + [tail], axis=0).astype(BF16)


def merge(parts, after):
    vmem = pl.BlockSpec(memory_space=pltpu.VMEM)
    blocks = parts[0].shape[0] // 4
    return pl.pallas_call(
        merge_kernel,
        out_shape=[jax.ShapeDtypeStruct((blocks, 56, WIDE), BF16)] * 4,
        in_specs=[vmem] * 4 + [pl.BlockSpec(memory_space=pl.ANY)],
        out_specs=[vmem] * 4,
        compiler_params=pltpu.CompilerParams(vmem_limit_bytes=24 * 2**20),
        name="merge",
    )(*parts, after)


def share_out(numer, total, spread):
    totals = jnp.concatenate([total] + [pltpu.roll(total, 128 - 16 * g, 1) for g in range(1, 6)], axis=0)
    wide = jnp.dot(totals, spread.astype(F32), precision=lax.Precision.HIGHEST, preferred_element_type=F32)
    return jnp.concatenate(numer, axis=0) / wide


def ring_close_kernel(p0, p1, p2, p3, out):
    spread = make_spread()
    held = [p[0] for p in (p0, p1, p2, p3)]
    numer, _, total = add_up([p[:48] for p in held], [p[48:56, :128].astype(F32) for p in held], spread.astype(BF16))
    out[...] = share_out(numer, total, spread)


def ring_close(parts):
    vmem = pl.BlockSpec(memory_space=pltpu.VMEM)
    return pl.pallas_call(
        ring_close_kernel,
        out_shape=jax.ShapeDtypeStruct((48, WIDE), F32),
        in_specs=[vmem] * 4,
        out_specs=vmem,
        name="ring_close",
    )(*parts)


def close_kernel(me, ready, got, keep, give, both, shares):
    spread = make_spread()
    narrow = spread.astype(BF16)

    def find(i, best):
        for u in range(16):
            best = jnp.maximum(best, got[i * 16 + u, 48:56, :128].astype(F32))
        return best

    best = lax.fori_loop(0, 4, find, jnp.full((8, 128), NO_TOP, F32))

    def weigh(i, total):
        for u in range(16):
            t = got[i * 16 + u, 48:56, :128].astype(F32)
            f = jnp.exp2(jnp.minimum(t - best, 0.0))
            shares[pl.ds(pl.multiple_of((i * 16 + u) * 8, 8), 8), :] = f
            total = total + f * (pltpu.roll(t, 128 - NH, 1) + pltpu.roll(t, 128 - 2 * NH, 1))
        return total

    total = lax.fori_loop(0, 4, weigh, jnp.zeros((8, 128), F32))

    def add(i, numer):
        numer = list(numer)
        f = shares[pl.ds(pl.multiple_of(i * 64, 64), 64), :]
        f = jnp.concatenate([f] + [pltpu.roll(f, 128 - 16 * g, 1) for g in range(1, 6)], axis=0)
        wide = jnp.dot(f.astype(BF16), narrow, preferred_element_type=F32)
        for u in range(8):
            for g in range(6):
                at = g * 64 + u * 8
                numer[g] = numer[g] + wide[at:at + 8] * got[i * 8 + u, g * 8:g * 8 + 8, :].astype(F32)
        return tuple(numer)

    numer = lax.fori_loop(0, 8, add, tuple(jnp.zeros((8, WIDE), F32) for _ in range(6)))
    both[:, :WIDE] = ready[...]
    both[:, WIDE:] = share_out(list(numer), total, spread)
    row = pl.multiple_of(me[1] * 24, 8)
    keep[...] = both[pl.ds(row, 24), :].astype(BF16)
    give[...] = both[pl.ds(24 - row, 24), :].astype(BF16)


def close(me, ready, got):
    vmem = pl.BlockSpec(memory_space=pltpu.VMEM)
    smem = pl.BlockSpec(memory_space=pltpu.SMEM)
    return pl.pallas_call(
        close_kernel,
        out_shape=[jax.ShapeDtypeStruct((24, 512), BF16)] * 2,
        in_specs=[smem, vmem, vmem],
        out_specs=[vmem] * 2,
        scratch_shapes=[pltpu.VMEM((48, 512), F32), pltpu.VMEM((512, 128), F32)],
        compiler_params=pltpu.CompilerParams(vmem_limit_bytes=16 * 2**20),
        name="close",
    )(me, ready, got)


def swap(x):
    return lax.ppermute(x, "core", [(0, 1), (1, 0)])


def shift(x, axes, by):
    pairs = []
    for y, c, z, w in itertools.product(range(4), range(2), range(4), range(4)):
        to = {"y": y, "z": z, "x": w}
        to[axes[c]] = (to[axes[c]] + by) % 4
        pairs.append((((y * 2 + c) * 4 + z) * 4 + w, ((to["y"] * 2 + c) * 4 + to["z"]) * 4 + to["x"]))
    return lax.ppermute(x, ALL, pairs)


def ring(x, axes):
    return [x] + [shift(x, axes, by) for by in (1, 2, 3)]


def deliver(parts, axes):
    return [parts[0]] + [shift(parts[by], axes, -by) for by in (1, 2, 3)]


def body(queries, keys, values, frame_slot, covisible, counts, out_weight):
    core = lax.axis_index("core")
    device = lax.axis_index(ALL)
    partner = device + 16 - 32 * core
    own_col = core * 512
    other_col = 512 - own_col

    mine = lax.dynamic_slice_in_dim(queries, own_col, 512, 1)
    theirs = swap(lax.dynamic_slice_in_dim(queries, other_col, 512, 1))
    first = core == 0
    pair = jnp.concatenate([jnp.where(first, mine, theirs), jnp.where(first, theirs, mine)], axis=0)
    along_z = jnp.concatenate(ring(pair[None], "zz"), axis=0)
    k_theirs, v_theirs = swap(keys), swap(values)
    me = jnp.stack([lax.axis_index(a) for a in ALL]).astype(jnp.int32)
    planes = pack(ring(along_z, "yx"), k_theirs, v_theirs)
    v_turned = turn_values(me, values, v_theirs, planes[0])
    q_parts = [ring(plane, "xy") for plane in planes]

    four = jnp.arange(4, dtype=jnp.int32)
    slots = jnp.concatenate([device * 4 + four, partner * 4 + four])
    frame_ids = jnp.arange(frame_slot.shape[0], dtype=jnp.int32)
    local = jnp.sum(jnp.where(frame_slot[None, :] == slots[:, None], frame_ids[None, :], 0), axis=1)
    used = jnp.arange(covisible.shape[1], dtype=jnp.int32)[None, :] < counts[:, None]
    need = jnp.any((covisible[:, None, :] == local[None, :, None]) & used[:, None, :], axis=2)
    need_i = need.astype(jnp.int32)
    place = jnp.cumsum(need_i, axis=1) - need_i
    eight = jnp.arange(8, dtype=jnp.int32)
    hit = need[:, None, :] & (place[:, None, :] == eight[None, :, None])
    lst = jnp.sum(jnp.where(hit, eight[None, None, :], 0), axis=2).reshape(96)
    cnt = jnp.sum(need_i, axis=1)

    sent = deliver(attend(me, cnt, lst, q_parts[0], keys, k_theirs, v_turned, 0), "xy")
    late = attend(me, cnt, lst, q_parts[1], keys, k_theirs, v_turned, 1)[0]
    got = lax.all_to_all(late, ("y", "z", "x"), 0, 0)
    sent = deliver(merge(sent, late), "yx")
    sent = deliver(merge(sent, late), "zz")
    keep, give = close(me, ring_close(sent), got)
    give = swap(give)
    rows = jnp.concatenate([jnp.where(first, keep, give), jnp.where(first, give, keep)], axis=1)
    return jnp.dot(rows, out_weight, preferred_element_type=F32).astype(BF16)


def solution(mesh):
    fine = Mesh(mesh.devices.reshape(4, 2, 4, 4), ALL)
    return jax.shard_map(
        body,
        mesh=fine,
        in_specs=(P(ALL, None), P(ALL, None, None), P(ALL, None, None), P(), P(), P(), P()),
        out_specs=P(ALL, None),
        check_vma=False,
    )
```

```python
import functools
import itertools

import jax
import jax.numpy as jnp
from jax import lax
from jax.experimental import pallas as pl
from jax.experimental.pallas import tpu as pltpu
from jax.sharding import Mesh, PartitionSpec as P

HD = 64
LOG2E = 1.4426950408889634
TOP_STEP = 16.0
NO_TOP = -32768.0
NH = 4
WIDE = NH * HD
ALL = ("y", "core", "z", "x")
F32 = jnp.float32
BF16 = jnp.bfloat16


def spread_kernel(me, q, theirs, out):
    first = me[1] == 0
    mine = jnp.where(first, q[:, :512].astype(F32), q[:, 512:].astype(F32))
    other = theirs[...].astype(F32)
    pair = jnp.concatenate([jnp.where(first, mine, other), jnp.where(first, other, mine)], axis=0).astype(BF16)
    for i in range(16):
        for c in range(2):
            out[i, c] = pair[:, c * WIDE:(c + 1) * WIDE]


def spread_rows(me, q, theirs):
    vmem = pl.BlockSpec(memory_space=pltpu.VMEM)
    smem = pl.BlockSpec(memory_space=pltpu.SMEM)
    return pl.pallas_call(
        spread_kernel,
        out_shape=jax.ShapeDtypeStruct((16, 2, 48, WIDE), BF16),
        in_specs=[smem, vmem, vmem],
        out_specs=vmem,
        name="spread",
    )(me, q, theirs)


def attend_kernel(
    me, cnt, lst, *refs, part,
):
    qs, (k0, k1, v0, _), outs = refs[:4], refs[4:8], refs[8:12]
    pq, pj, ps, qv, k, vt, qm, acc, sb, top, shrink, yb, sem = refs[12:]
    my_y, my_core, my_x = me[0], me[1], me[3]
    col = pl.multiple_of(my_core * 512 + part * WIDE, WIDE)
    copies = [
        pltpu.make_async_copy(src, dst, sem.at[i])
        for i, (src, dst) in enumerate(
            [(q, qv.at[pl.ds(i * q.shape[0], q.shape[0])]) for i, q in enumerate(qs)]
            + [
                (k0.at[:, :, pl.ds(col, WIDE)], k.at[pl.ds(0, 4)]),
                (k1.at[:, :, pl.ds(col, WIDE)], k.at[pl.ds(4, 4)]),
                (v0.at[:, pl.ds(part * WIDE, WIDE), :], vt),
            ]
        )
    ]
    for copy in copies:
        copy.start()
    scale = HD ** -0.5 * LOG2E
    ones = jnp.ones((16, 256), BF16)

    def list_frame(qi, carry):
        at, slot = carry

        def put(i, at):
            pj[at] = lst[qi * 8 + i]
            pq[at] = qi
            ps[at] = slot
            return at + 1

        n = cnt[qi]
        return lax.fori_loop(0, n, put, at), jnp.where(n > 0, 1 - slot, slot)

    total, spare = lax.fori_loop(0, 12, list_frame, (jnp.int32(0), jnp.int32(0)))
    for u in range(5):
        pq[total + u] = 12
        pj[total + u] = 0
        ps[total + u] = spare

    def place(r3, z, a):
        y = jnp.where(my_core == 0, a, lax.rem(my_y + 4 - r3, 4))
        x = jnp.where(my_core == 0, lax.rem(my_x + 4 - r3, 4), a)
        return [pl.multiple_of(y * 768 + (c * 16 + z * 4 + x) * 24, 8) for c in range(2)]

    spots = [[place(r3, z, a) for z in range(4) for a in range(4)] for r3 in range(4)]
    for i, spot in enumerate(spots):
        copies[i].wait()
        for b, rows in enumerate(spot):
            block = qv[i * len(spot) + b].astype(F32)
            for c, row in enumerate(rows):
                yb[pl.ds(row, 24), :WIDE] = block[c * 24:(c + 1) * 24]

    def turn(qi, _):
        rows = pl.ds(pl.multiple_of(qi * 256, 256), 256)
        zero = jnp.zeros((64, 256), BF16)
        for hp in range(NH // 2):
            turned = yb[rows, hp * 128:(hp + 1) * 128].T.astype(BF16)
            qm[qi, 2 * hp] = jnp.concatenate([turned[:64], zero], axis=0)
            qm[qi, 2 * hp + 1] = jnp.concatenate([zero, turned[64:]], axis=0)

        @pl.when(cnt[qi] == 0)
        def _():
            yb[rows, :WIDE] = jnp.zeros((256, WIDE), F32)
            lane = lax.broadcasted_iota(jnp.int32, (256, 128), 1)
            yb[rows, WIDE:] = jnp.where(lane < NH, NO_TOP, 0.0)

        return 0

    lax.fori_loop(0, 12, turn, 0)
    for copy in copies[4:]:
        copy.wait()
    acc[...] = jnp.zeros_like(acc)
    qm[12] = jnp.zeros((NH, 128, 256), BF16)

    def score(t, p, h):
        hp = h // 2
        keys = k[pj[t + p], :, hp * 128:(hp + 1) * 128]
        s = jnp.dot(keys, qm[pq[t + p], h], preferred_element_type=F32) * scale
        sb[p, h] = s
        return jnp.max(s, axis=0, keepdims=True)

    def settle(t, p, highs, old):
        first = pq[t + p] != pq[jnp.maximum(t + p - 1, 0)]
        old = jnp.where(first, NO_TOP, old)
        high = jnp.concatenate(highs, axis=0)
        new = jnp.maximum(old, jnp.ceil(high * (1.0 / TOP_STEP)) * TOP_STEP)
        top[p] = new
        shrink[p] = jnp.exp2(old - new)
        return new

    def weigh(t, p, h, tops, shrinks):
        weights = jnp.exp2(sb[p, h] - tops[h:h + 1]).astype(BF16)
        vals = jnp.concatenate([vt[pj[t + p], h * 64:(h + 1) * 64, :], ones], axis=0)
        part = jnp.dot(vals, weights, preferred_element_type=F32)
        at = ps[t + p]
        acc[at, h] = acc[at, h] * shrinks[h:h + 1] + part

    def finish(t, p, tops):
        qi = pq[t + p]

        @pl.when((qi < 12) & (pq[t + p + 1] != qi))
        def _():
            at = ps[t + p]
            rows = pl.ds(pl.multiple_of(qi * 256, 256), 256)
            totals = jnp.concatenate([acc[at, h, 64:65, :] for h in range(NH)], axis=0)
            hi = totals.astype(BF16).astype(F32)
            extra = [tops, hi, totals - hi, jnp.zeros((128 - 3 * NH, 256), F32)]
            for hp in range(NH // 2):
                both = jnp.concatenate([acc[at, 2 * hp, :64, :], acc[at, 2 * hp + 1, :64, :]], axis=0)
                yb[rows, hp * 128:(hp + 1) * 128] = both.T
            yb[rows, WIDE:] = jnp.concatenate(extra, axis=0).T

    old = jnp.full((NH, 256), NO_TOP, F32)
    for p in range(2):
        old = settle(0, p, [score(0, p, h) for h in range(NH)], old)

    def two(u, _):
        t = u * 2
        tops, shrinks = [top[0], top[1]], [shrink[0], shrink[1]]
        highs = [[], []]
        for p in range(2):
            for h in range(NH):
                weigh(t, p, h, tops[p], shrinks[p])
                highs[p].append(score(t + 2, p, h))
        old = settle(t + 2, 0, highs[0], tops[1])
        settle(t + 2, 1, highs[1], old)
        for p in range(2):
            finish(t, p, tops[p])
        return 0

    lax.fori_loop(0, (total + 1) // 2, two, 0)

    for o, spot in zip(outs, spots):
        for b, rows in enumerate(spot):
            data, tail = [], jnp.zeros((8, 128), F32)
            for c, row in enumerate(rows):
                block = yb[pl.ds(row, 24), :]
                data.append(block[:, :WIDE])
                for p in range(3):
                    piece = block[p * 8:(p + 1) * 8, WIDE:]
                    g = c * 3 + p
                    tail = tail + (pltpu.roll(piece, 16 * g, 1) if g else piece)
            data.append(jnp.concatenate([tail, jnp.zeros((8, WIDE - 128), F32)], axis=1))
            o[b] = jnp.concatenate(data, axis=0).astype(BF16)


def attend(me, cnt, lst, q, k0, k1, v0, after, part):
    vmem = pl.BlockSpec(memory_space=pltpu.VMEM)
    smem = pl.BlockSpec(memory_space=pltpu.SMEM)
    whole = pl.BlockSpec(memory_space=pl.ANY)
    return pl.pallas_call(
        functools.partial(attend_kernel, part=part),
        out_shape=[jax.ShapeDtypeStruct((16, 56, WIDE), BF16)] * 4,
        in_specs=[smem] * 3 + [whole] * 8,
        out_specs=[vmem] * 4,
        scratch_shapes=[
            pltpu.SMEM((104,), jnp.int32),
            pltpu.SMEM((104,), jnp.int32),
            pltpu.SMEM((104,), jnp.int32),
            pltpu.VMEM((64, 48, WIDE), BF16),
            pltpu.VMEM((8, 256, WIDE), BF16),
            pltpu.VMEM((8, WIDE, 256), BF16),
            pltpu.VMEM((13, NH, 128, 256), BF16),
            pltpu.VMEM((2, NH, 80, 256), F32),
            pltpu.VMEM((2, NH, 256, 256), F32),
            pltpu.VMEM((2, NH, 256), F32),
            pltpu.VMEM((2, NH, 256), F32),
            pltpu.VMEM((3072, WIDE + 128), F32),
            pltpu.SemaphoreType.DMA((7,)),
        ],
        compiler_params=pltpu.CompilerParams(vmem_limit_bytes=24 * 2**20),
        cost_estimate=pl.CostEstimate(flops=10**10, bytes_accessed=2**23, transcendentals=2 * 10**7),
        name="attend",
    )(me, cnt, lst, *q, k0, k1, v0, after)


def turn_kernel(me, v0, v1, out, held, sem):
    col = pl.multiple_of(me[1] * 512, 512)
    copies = [
        pltpu.make_async_copy(v.at[:, :, pl.ds(col, 512)], held.at[pl.ds(i * 4, 4)], sem.at[i])
        for i, v in enumerate((v0, v1))
    ]
    for copy in copies:
        copy.start()
    for copy in copies:
        copy.wait()

    def one(j, _):
        for at in range(0, 512, 128):
            out[j, at:at + 128, :] = held[j, :, at:at + 128].astype(F32).T.astype(BF16)
        return 0

    lax.fori_loop(0, 8, one, 0)


def turn_values(me, v0, v1):
    vmem = pl.BlockSpec(memory_space=pltpu.VMEM)
    smem = pl.BlockSpec(memory_space=pltpu.SMEM)
    whole = pl.BlockSpec(memory_space=pl.ANY)
    return pl.pallas_call(
        turn_kernel,
        out_shape=jax.ShapeDtypeStruct((8, 512, 256), BF16),
        in_specs=[smem] + [whole] * 2,
        out_specs=vmem,
        scratch_shapes=[pltpu.VMEM((8, 256, 512), BF16), pltpu.SemaphoreType.DMA((2,))],
        cost_estimate=pl.CostEstimate(flops=10**6, bytes_accessed=2**23, transcendentals=0),
        compiler_params=pltpu.CompilerParams(vmem_limit_bytes=16 * 2**20),
        name="turn",
    )(me, v0, v1)


def add_up(data, tails, spread):
    n = len(data)
    best = functools.reduce(jnp.maximum, tails)
    shares = [jnp.exp2(jnp.minimum(t - best, 0.0)) for t in tails]
    total = sum(f * (pltpu.roll(t, 128 - NH, 1) + pltpu.roll(t, 128 - 2 * NH, 1)) for f, t in zip(shares, tails))
    stack = jnp.concatenate(shares, axis=0)
    groups = data[0].shape[0] // 8
    stack = jnp.concatenate([stack] + [pltpu.roll(stack, 128 - 16 * g, 1) for g in range(1, groups)], axis=0)
    wide = jnp.dot(stack.astype(BF16), spread, preferred_element_type=F32)
    numer = []
    for g in range(groups):
        at = g * 8 * n
        numer.append(
            sum(wide[at + s * 8:at + s * 8 + 8] * d[g * 8:g * 8 + 8, :].astype(F32) for s, d in enumerate(data))
        )
    return numer, best, total


def make_spread():
    src = lax.broadcasted_iota(jnp.int32, (128, WIDE), 0)
    dst = lax.broadcasted_iota(jnp.int32, (128, WIDE), 1) // HD
    return src == dst


def add_blocks(held, spread, is_top):
    data, tails = [p[:48] for p in held], [p[48:56, :128].astype(F32) for p in held]
    numer, best, total = add_up(data, tails, spread)
    total = jnp.where(is_top, total, 0.0)
    hi = total.astype(BF16).astype(F32)
    tail = jnp.where(is_top, best, 0.0) + pltpu.roll(hi, NH, 1) + pltpu.roll(total - hi, 2 * NH, 1)
    return numer, jnp.concatenate([tail, jnp.zeros((8, WIDE - 128), F32)], axis=1)


def merge_kernel(p0, p1, p2, p3, after, out):
    spread = make_spread().astype(BF16)
    is_top = lax.broadcasted_iota(jnp.int32, (8, 128), 1) % 16 < NH
    for b in range(16):
        numer, tail = add_blocks([p[b] for p in (p0, p1, p2, p3)], spread, is_top)
        out[b] = jnp.concatenate(numer + [tail], axis=0).astype(BF16)


def merge(parts, after):
    vmem = pl.BlockSpec(memory_space=pltpu.VMEM)
    return pl.pallas_call(
        merge_kernel,
        out_shape=jax.ShapeDtypeStruct((16, 56, WIDE), BF16),
        in_specs=[vmem] * 4 + [pl.BlockSpec(memory_space=pl.ANY)],
        out_specs=vmem,
        compiler_params=pltpu.CompilerParams(vmem_limit_bytes=16 * 2**20),
        name="merge",
    )(*parts, after)


def settle_rows(got):
    spread = make_spread()
    held = [got[i] for i in range(16)]
    numer, _, total = add_up([p[:48] for p in held], [p[48:56, :128].astype(F32) for p in held], spread.astype(BF16))
    totals = jnp.concatenate([total] + [pltpu.roll(total, 128 - 16 * g, 1) for g in range(1, 6)], axis=0)
    wide = jnp.dot(totals, spread.astype(F32), precision=lax.Precision.HIGHEST, preferred_element_type=F32)
    return jnp.concatenate(numer, axis=0) / wide


def first_close_kernel(got, out):
    out[...] = settle_rows(got)


def first_close(got):
    vmem = pl.BlockSpec(memory_space=pltpu.VMEM)
    return pl.pallas_call(
        first_close_kernel,
        out_shape=jax.ShapeDtypeStruct((48, WIDE), F32),
        in_specs=[vmem],
        out_specs=vmem,
        name="first_close",
    )(got)


def close_kernel(me, ready, got, keep, give, both):
    both[:, :WIDE] = ready[...]
    both[:, WIDE:] = settle_rows(got)
    row = pl.multiple_of(me[1] * 24, 8)
    keep[...] = both[pl.ds(row, 24), :].astype(BF16)
    give[...] = both[pl.ds(24 - row, 24), :].astype(BF16)


def close(me, ready, got):
    vmem = pl.BlockSpec(memory_space=pltpu.VMEM)
    smem = pl.BlockSpec(memory_space=pltpu.SMEM)
    return pl.pallas_call(
        close_kernel,
        out_shape=[jax.ShapeDtypeStruct((24, 512), BF16)] * 2,
        in_specs=[smem, vmem, vmem],
        out_specs=[vmem] * 2,
        scratch_shapes=[pltpu.VMEM((48, 512), F32)],
        name="close",
    )(me, ready, got)


def swap(x):
    return lax.ppermute(x, "core", [(0, 1), (1, 0)])


def shift(x, axes, by):
    pairs = []
    for y, c, z, w in itertools.product(range(4), range(2), range(4), range(4)):
        to = {"y": y, "z": z, "x": w}
        to[axes[c]] = (to[axes[c]] + by) % 4
        pairs.append((((y * 2 + c) * 4 + z) * 4 + w, ((to["y"] * 2 + c) * 4 + to["z"]) * 4 + to["x"]))
    return lax.ppermute(x, ALL, pairs)


def ring(x, axes):
    return [x] + [shift(x, axes, by) for by in (1, 2, 3)]


def spot(y, c, z, x):
    return ((y * 2 + c) * 4 + z) * 4 + x


GROUPS = [[spot(a, 0, z, w) for z in range(4) for a in range(4)] for w in range(4)] + [
    [spot(w, 1, z, a) for z in range(4) for a in range(4)] for w in range(4)
]


def exchange(x):
    return lax.all_to_all(x, ALL, 0, 0, axis_index_groups=GROUPS)


def deliver(parts, axes):
    return [parts[0]] + [shift(parts[by], axes, -by) for by in (1, 2, 3)]


def body(queries, keys, values, frame_slot, covisible, counts, out_weight):
    core = lax.axis_index("core")
    device = lax.axis_index(ALL)
    partner = device + 16 - 32 * core
    own_col = core * 512

    theirs = swap(lax.dynamic_slice_in_dim(queries, 512 - own_col, 512, 1))
    first = core == 0
    me = jnp.stack([lax.axis_index(a) for a in ALL]).astype(jnp.int32)
    plane = exchange(spread_rows(me, queries, theirs))
    k_theirs, v_theirs = swap(keys), swap(values)
    v_turned = turn_values(me, values, v_theirs)
    q_parts = [ring(plane[:, c], "xy") for c in range(2)]

    four = jnp.arange(4, dtype=jnp.int32)
    slots = jnp.concatenate([device * 4 + four, partner * 4 + four])
    frame_ids = jnp.arange(frame_slot.shape[0], dtype=jnp.int32)
    local = jnp.sum(jnp.where(frame_slot[None, :] == slots[:, None], frame_ids[None, :], 0), axis=1)
    used = jnp.arange(covisible.shape[1], dtype=jnp.int32)[None, :] < counts[:, None]
    need = jnp.any((covisible[:, None, :] == local[None, :, None]) & used[:, None, :], axis=2)
    need_i = need.astype(jnp.int32)
    place = jnp.cumsum(need_i, axis=1) - need_i
    eight = jnp.arange(8, dtype=jnp.int32)
    hit = need[:, None, :] & (place[:, None, :] == eight[None, :, None])
    lst = jnp.sum(jnp.where(hit, eight[None, None, :], 0), axis=2).reshape(96)
    cnt = jnp.sum(need_i, axis=1)

    early = attend(me, cnt, lst, q_parts[0], keys, k_theirs, v_turned, q_parts[0][0], 0)
    late = attend(me, cnt, lst, q_parts[1], keys, k_theirs, v_turned, early[0], 1)
    early = exchange(merge(deliver(early, "xy"), late[0]))
    late = exchange(merge(deliver(late, "xy"), late[0]))
    keep, give = close(me, first_close(early), late)
    give = swap(give)
    rows = jnp.concatenate([jnp.where(first, keep, give), jnp.where(first, give, keep)], axis=1)
    return jnp.dot(rows, out_weight, preferred_element_type=F32).astype(BF16)


def solution(mesh):
    fine = Mesh(mesh.devices.reshape(4, 2, 4, 4), ALL)
    return jax.shard_map(
        body,
        mesh=fine,
        in_specs=(P(ALL, None), P(ALL, None, None), P(ALL, None, None), P(), P(), P(), P()),
        out_specs=P(ALL, None),
        check_vma=False,
    )
```

```python
import functools
import itertools

import jax
import jax.numpy as jnp
from jax import lax
from jax.experimental import pallas as pl
from jax.experimental.pallas import tpu as pltpu
from jax.sharding import Mesh, PartitionSpec as P

HD = 64
LOG2E = 1.4426950408889634
TOP_STEP = 16.0
NO_TOP = -32768.0
NH = 4
WIDE = NH * HD
ALL = ("y", "core", "z", "x")
F32 = jnp.float32
BF16 = jnp.bfloat16


def spread_kernel(me, q, theirs, out):
    first = me[1] == 0
    mine = jnp.where(first, q[:, :512].astype(F32), q[:, 512:].astype(F32))
    other = theirs[...].astype(F32)
    pair = jnp.concatenate([jnp.where(first, mine, other), jnp.where(first, other, mine)], axis=0).astype(BF16)
    for i in range(16):
        for c in range(2):
            out[i, c] = pair[:, c * WIDE:(c + 1) * WIDE]


def spread_rows(me, q, theirs):
    vmem = pl.BlockSpec(memory_space=pltpu.VMEM)
    smem = pl.BlockSpec(memory_space=pltpu.SMEM)
    return pl.pallas_call(
        spread_kernel,
        out_shape=jax.ShapeDtypeStruct((16, 2, 48, WIDE), BF16),
        in_specs=[smem, vmem, vmem],
        out_specs=vmem,
        name="spread",
    )(me, q, theirs)


def attend_kernel(
    me, need, *refs, part,
):
    qs, (k0, k1, v0, _), outs = refs[:4], refs[4:8], refs[8:12]
    cnt, plan, qv, k, vt, qm, acc, sb, top, shrink, yb, sem = refs[12:]
    my_y, my_core, my_x = me[0], me[1], me[3]
    col = pl.multiple_of(my_core * 512 + part * WIDE, WIDE)
    copies = [
        pltpu.make_async_copy(src, dst, sem.at[i])
        for i, (src, dst) in enumerate(
            [(q, qv.at[pl.ds(i * q.shape[0], q.shape[0])]) for i, q in enumerate(qs)]
            + [
                (k0.at[:, :, pl.ds(col, WIDE)], k.at[pl.ds(0, 4)]),
                (k1.at[:, :, pl.ds(col, WIDE)], k.at[pl.ds(4, 4)]),
                (v0.at[:, pl.ds(part * WIDE, WIDE), :], vt),
            ]
        )
    ]
    for copy in copies:
        copy.start()
    scale = HD ** -0.5 * LOG2E
    ones = jnp.ones((16, 256), BF16)

    total, slot = jnp.int32(0), jnp.int32(0)
    for qi in range(12):
        begin = total
        for j in range(8):
            plan[total] = qi + 16 * j + 256 * slot
            total = total + need[qi, j]
        cnt[qi] = total - begin
        slot = (slot + jnp.minimum(total - begin, 1)) & 3
    for u in range(8):
        plan[total + u] = 12 + 256 * slot

    def frame_of(t):
        return plan[t] & 15

    def held_of(t):
        return (plan[t] >> 4) & 7

    def slot_of(t):
        return plan[t] >> 8

    def place(r3, z, a):
        y = jnp.where(my_core == 0, a, lax.rem(my_y + 4 - r3, 4))
        x = jnp.where(my_core == 0, lax.rem(my_x + 4 - r3, 4), a)
        return [pl.multiple_of(y * 768 + (c * 16 + z * 4 + x) * 24, 8) for c in range(2)]

    spots = [[place(r3, z, a) for z in range(4) for a in range(4)] for r3 in range(4)]
    for i, spot in enumerate(spots):
        copies[i].wait()
        for b, rows in enumerate(spot):
            block = qv[i * len(spot) + b].astype(F32)
            for c, row in enumerate(rows):
                yb[pl.ds(row, 24), :WIDE] = block[c * 24:(c + 1) * 24]

    def turn(qi, _):
        rows = pl.ds(pl.multiple_of(qi * 256, 256), 256)
        zero = jnp.zeros((64, 256), BF16)
        for hp in range(NH // 2):
            turned = yb[rows, hp * 128:(hp + 1) * 128].T.astype(BF16)
            qm[qi, 2 * hp] = jnp.concatenate([turned[:64], zero], axis=0)
            qm[qi, 2 * hp + 1] = jnp.concatenate([zero, turned[64:]], axis=0)

        @pl.when(cnt[qi] == 0)
        def _():
            yb[rows, :WIDE] = jnp.zeros((256, WIDE), F32)
            lane = lax.broadcasted_iota(jnp.int32, (256, 128), 1)
            yb[rows, WIDE:] = jnp.where(lane < NH, NO_TOP, 0.0)

        return 0

    lax.fori_loop(0, 12, turn, 0)
    for copy in copies[4:]:
        copy.wait()
    acc[...] = jnp.zeros_like(acc)
    qm[12] = jnp.zeros((NH, 128, 256), BF16)

    def score(t, p, h):
        hp = h // 2
        keys = k[held_of(t + p), :, hp * 128:(hp + 1) * 128]
        s = jnp.dot(keys, qm[frame_of(t + p), h], preferred_element_type=F32) * scale
        sb[p, h] = s
        return jnp.max(s, axis=0, keepdims=True)

    def settle(t, p, highs, old):
        first = frame_of(t + p) != frame_of(jnp.maximum(t + p - 1, 0))
        old = jnp.where(first, NO_TOP, old)
        high = jnp.concatenate(highs, axis=0)
        new = jnp.maximum(old, jnp.ceil(high * (1.0 / TOP_STEP)) * TOP_STEP)
        top[p] = new
        shrink[p] = jnp.exp2(old - new)
        return new

    def weigh(t, p, h, tops, shrinks):
        weights = jnp.exp2(sb[p, h] - tops[h:h + 1]).astype(BF16)
        vals = jnp.concatenate([vt[held_of(t + p), h * 64:(h + 1) * 64, :], ones], axis=0)
        part = jnp.dot(vals, weights, preferred_element_type=F32)
        at = slot_of(t + p)
        acc[at, h] = acc[at, h] * shrinks[h:h + 1] + part

    def finish(t, p, tops):
        qi = frame_of(t + p)

        @pl.when((qi < 12) & (frame_of(t + p + 1) != qi))
        def _():
            at = slot_of(t + p)
            rows = pl.ds(pl.multiple_of(qi * 256, 256), 256)
            totals = jnp.concatenate([acc[at, h, 64:65, :] for h in range(NH)], axis=0)
            hi = totals.astype(BF16).astype(F32)
            extra = [tops, hi, totals - hi, jnp.zeros((128 - 3 * NH, 256), F32)]
            for hp in range(NH // 2):
                both = jnp.concatenate([acc[at, 2 * hp, :64, :], acc[at, 2 * hp + 1, :64, :]], axis=0)
                yb[rows, hp * 128:(hp + 1) * 128] = both.T
            yb[rows, WIDE:] = jnp.concatenate(extra, axis=0).T

    old = jnp.full((NH, 256), NO_TOP, F32)
    for p in range(4):
        old = settle(0, p, [score(0, p, h) for h in range(NH)], old)

    def two(u, _):
        t = u * 4
        tops, shrinks = [top[p] for p in range(4)], [shrink[p] for p in range(4)]
        highs = [[] for p in range(4)]
        for p in range(4):
            for h in range(NH):
                weigh(t, p, h, tops[p], shrinks[p])
                highs[p].append(score(t + 4, p, h))
        old = tops[3]
        for p in range(4):
            old = settle(t + 4, p, highs[p], old)
        for p in range(4):
            finish(t, p, tops[p])
        return 0

    lax.fori_loop(0, (total + 3) // 4, two, 0)

    for o, spot in zip(outs, spots):
        for b, rows in enumerate(spot):
            data, tail = [], jnp.zeros((8, 128), F32)
            for c, row in enumerate(rows):
                block = yb[pl.ds(row, 24), :]
                data.append(block[:, :WIDE])
                for p in range(3):
                    piece = block[p * 8:(p + 1) * 8, WIDE:]
                    g = c * 3 + p
                    tail = tail + (pltpu.roll(piece, 16 * g, 1) if g else piece)
            data.append(jnp.concatenate([tail, jnp.zeros((8, WIDE - 128), F32)], axis=1))
            o[b] = jnp.concatenate(data, axis=0).astype(BF16)


def attend(me, need, q, k0, k1, v0, after, part):
    vmem = pl.BlockSpec(memory_space=pltpu.VMEM)
    smem = pl.BlockSpec(memory_space=pltpu.SMEM)
    whole = pl.BlockSpec(memory_space=pl.ANY)
    return pl.pallas_call(
        functools.partial(attend_kernel, part=part),
        out_shape=[jax.ShapeDtypeStruct((16, 56, WIDE), BF16)] * 4,
        in_specs=[smem] * 2 + [whole] * 8,
        out_specs=[vmem] * 4,
        scratch_shapes=[
            pltpu.SMEM((12,), jnp.int32),
            pltpu.SMEM((112,), jnp.int32),
            pltpu.VMEM((64, 48, WIDE), BF16),
            pltpu.VMEM((8, 256, WIDE), BF16),
            pltpu.VMEM((8, WIDE, 256), BF16),
            pltpu.VMEM((13, NH, 128, 256), BF16),
            pltpu.VMEM((4, NH, 80, 256), F32),
            pltpu.VMEM((4, NH, 256, 256), F32),
            pltpu.VMEM((4, NH, 256), F32),
            pltpu.VMEM((4, NH, 256), F32),
            pltpu.VMEM((3072, WIDE + 128), F32),
            pltpu.SemaphoreType.DMA((7,)),
        ],
        compiler_params=pltpu.CompilerParams(vmem_limit_bytes=24 * 2**20),
        cost_estimate=pl.CostEstimate(flops=10**10, bytes_accessed=2**23, transcendentals=2 * 10**7),
        name="attend",
    )(me, need, *q, k0, k1, v0, after)


def turn_kernel(me, v0, v1, k, out, parts, held, sem):
    parts[0] = 0
    parts[1] = 1
    col = pl.multiple_of(me[1] * 512, 512)
    copies = [
        pltpu.make_async_copy(v.at[:, :, pl.ds(col, 512)], held.at[pl.ds(i * 4, 4)], sem.at[i])
        for i, v in enumerate((v0, v1))
    ]
    for copy in copies:
        copy.start()
    for copy in copies:
        copy.wait()

    def one(j, _):
        for at in range(0, 512, 128):
            out[j, at:at + 128, :] = held[j, :, at:at + 128].astype(F32).T.astype(BF16)
        return 0

    lax.fori_loop(0, 8, one, 0)


def turn_values(me, v0, v1, k):
    vmem = pl.BlockSpec(memory_space=pltpu.VMEM)
    smem = pl.BlockSpec(memory_space=pltpu.SMEM)
    whole = pl.BlockSpec(memory_space=pl.ANY)
    return pl.pallas_call(
        turn_kernel,
        out_shape=[jax.ShapeDtypeStruct((8, 512, 256), BF16), jax.ShapeDtypeStruct((2,), jnp.int32)],
        in_specs=[smem] + [whole] * 3,
        out_specs=[vmem, smem],
        scratch_shapes=[pltpu.VMEM((8, 256, 512), BF16), pltpu.SemaphoreType.DMA((2,))],
        cost_estimate=pl.CostEstimate(flops=10**6, bytes_accessed=2**23, transcendentals=0),
        compiler_params=pltpu.CompilerParams(vmem_limit_bytes=16 * 2**20),
        name="turn",
    )(me, v0, v1, k)


def add_up(data, tails, spread):
    n = len(data)
    best = functools.reduce(jnp.maximum, tails)
    shares = [jnp.exp2(jnp.minimum(t - best, 0.0)) for t in tails]
    total = sum(f * (pltpu.roll(t, 128 - NH, 1) + pltpu.roll(t, 128 - 2 * NH, 1)) for f, t in zip(shares, tails))
    stack = jnp.concatenate(shares, axis=0)
    groups = data[0].shape[0] // 8
    stack = jnp.concatenate([stack] + [pltpu.roll(stack, 128 - 16 * g, 1) for g in range(1, groups)], axis=0)
    wide = jnp.dot(stack.astype(BF16), spread, preferred_element_type=F32)
    numer = []
    for g in range(groups):
        at = g * 8 * n
        numer.append(
            sum(wide[at + s * 8:at + s * 8 + 8] * d[g * 8:g * 8 + 8, :].astype(F32) for s, d in enumerate(data))
        )
    return numer, best, total


def make_spread():
    src = lax.broadcasted_iota(jnp.int32, (128, WIDE), 0)
    dst = lax.broadcasted_iota(jnp.int32, (128, WIDE), 1) // HD
    return src == dst


def add_blocks(held, spread, is_top):
    data, tails = [p[:48] for p in held], [p[48:56, :128].astype(F32) for p in held]
    numer, best, total = add_up(data, tails, spread)
    total = jnp.where(is_top, total, 0.0)
    hi = total.astype(BF16).astype(F32)
    tail = jnp.where(is_top, best, 0.0) + pltpu.roll(hi, NH, 1) + pltpu.roll(total - hi, 2 * NH, 1)
    return numer, jnp.concatenate([tail, jnp.zeros((8, WIDE - 128), F32)], axis=1)


def merge_kernel(p0, p1, p2, p3, after, out):
    spread = make_spread().astype(BF16)
    is_top = lax.broadcasted_iota(jnp.int32, (8, 128), 1) % 16 < NH
    for b in range(16):
        numer, tail = add_blocks([p[b] for p in (p0, p1, p2, p3)], spread, is_top)
        out[b] = jnp.concatenate(numer + [tail], axis=0).astype(BF16)


def merge(parts, after):
    vmem = pl.BlockSpec(memory_space=pltpu.VMEM)
    return pl.pallas_call(
        merge_kernel,
        out_shape=jax.ShapeDtypeStruct((16, 56, WIDE), BF16),
        in_specs=[vmem] * 4 + [pl.BlockSpec(memory_space=pl.ANY)],
        out_specs=vmem,
        compiler_params=pltpu.CompilerParams(vmem_limit_bytes=16 * 2**20),
        name="merge",
    )(*parts, after)


def settle_rows(got):
    spread = make_spread()
    held = [got[i] for i in range(16)]
    numer, _, total = add_up([p[:48] for p in held], [p[48:56, :128].astype(F32) for p in held], spread.astype(BF16))
    totals = jnp.concatenate([total] + [pltpu.roll(total, 128 - 16 * g, 1) for g in range(1, 6)], axis=0)
    wide = jnp.dot(totals, spread.astype(F32), precision=lax.Precision.HIGHEST, preferred_element_type=F32)
    return jnp.concatenate(numer, axis=0) / wide


def first_close_kernel(got, out):
    out[...] = settle_rows(got)


def first_close(got):
    vmem = pl.BlockSpec(memory_space=pltpu.VMEM)
    return pl.pallas_call(
        first_close_kernel,
        out_shape=jax.ShapeDtypeStruct((48, WIDE), F32),
        in_specs=[vmem],
        out_specs=vmem,
        name="first_close",
    )(got)


def close_kernel(me, ready, got, keep, give, both):
    both[:, :WIDE] = ready[...]
    both[:, WIDE:] = settle_rows(got)
    row = pl.multiple_of(me[1] * 24, 8)
    keep[...] = both[pl.ds(row, 24), :].astype(BF16)
    give[...] = both[pl.ds(24 - row, 24), :].astype(BF16)


def close(me, ready, got):
    vmem = pl.BlockSpec(memory_space=pltpu.VMEM)
    smem = pl.BlockSpec(memory_space=pltpu.SMEM)
    return pl.pallas_call(
        close_kernel,
        out_shape=[jax.ShapeDtypeStruct((24, 512), BF16)] * 2,
        in_specs=[smem, vmem, vmem],
        out_specs=[vmem] * 2,
        scratch_shapes=[pltpu.VMEM((48, 512), F32)],
        name="close",
    )(me, ready, got)


def project_kernel(me, keep, give, weight, out):
    first = me[1] == 0
    mine, other = keep[...].astype(F32), give[...].astype(F32)
    left = jnp.where(first, mine, other).astype(BF16)
    right = jnp.where(first, other, mine).astype(BF16)
    total = jnp.dot(left, weight[:512], preferred_element_type=F32)
    out[...] = (total + jnp.dot(right, weight[512:], preferred_element_type=F32)).astype(BF16)


def project(me, keep, give, weight):
    vmem = pl.BlockSpec(memory_space=pltpu.VMEM)
    smem = pl.BlockSpec(memory_space=pltpu.SMEM)
    return pl.pallas_call(
        project_kernel,
        out_shape=jax.ShapeDtypeStruct((24, 1024), BF16),
        in_specs=[smem] + [vmem] * 3,
        out_specs=vmem,
        name="project",
    )(me, keep, give, weight)


def swap(x):
    return lax.ppermute(x, "core", [(0, 1), (1, 0)])


def shift(x, axes, by):
    pairs = []
    for y, c, z, w in itertools.product(range(4), range(2), range(4), range(4)):
        to = {"y": y, "z": z, "x": w}
        to[axes[c]] = (to[axes[c]] + by) % 4
        pairs.append((((y * 2 + c) * 4 + z) * 4 + w, ((to["y"] * 2 + c) * 4 + to["z"]) * 4 + to["x"]))
    return lax.ppermute(x, ALL, pairs)


def ring(x, axes):
    return [x] + [shift(x, axes, by) for by in (1, 2, 3)]


def spot(y, c, z, x):
    return ((y * 2 + c) * 4 + z) * 4 + x


GROUPS = [[spot(a, 0, z, w) for z in range(4) for a in range(4)] for w in range(4)] + [
    [spot(w, 1, z, a) for z in range(4) for a in range(4)] for w in range(4)
]


def exchange(x):
    return lax.all_to_all(x, ALL, 0, 0, axis_index_groups=GROUPS)


def deliver(parts, axes):
    return [parts[0]] + [shift(parts[by], axes, -by) for by in (1, 2, 3)]


def body(queries, keys, values, frame_slot, covisible, counts, out_weight):
    core = lax.axis_index("core")
    device = lax.axis_index(ALL)
    partner = device + 16 - 32 * core
    own_col = core * 512

    theirs = swap(lax.dynamic_slice_in_dim(queries, 512 - own_col, 512, 1))
    me = jnp.stack([lax.axis_index(a) for a in ALL]).astype(jnp.int32)
    plane = exchange(spread_rows(me, queries, theirs))
    k_theirs, v_theirs = swap(keys), swap(values)
    v_turned, parts = turn_values(me, values, v_theirs, k_theirs)
    q_parts = [ring(lax.dynamic_index_in_dim(plane, parts[c], 1, False), "xy") for c in range(2)]

    four = jnp.arange(4, dtype=jnp.int32)
    slots = jnp.concatenate([device * 4 + four, partner * 4 + four])
    frame_ids = jnp.arange(frame_slot.shape[0], dtype=jnp.int32)
    local = jnp.sum(jnp.where(frame_slot[None, :] == slots[:, None], frame_ids[None, :], 0), axis=1)
    used = jnp.arange(covisible.shape[1], dtype=jnp.int32)[None, :] < counts[:, None]
    need = jnp.any((covisible[:, None, :] == local[None, :, None]) & used[:, None, :], axis=2)
    need = need.astype(jnp.int32)

    early = attend(me, need, q_parts[0], keys, k_theirs, v_turned, q_parts[0][0], 0)
    late = attend(me, need, q_parts[1], keys, k_theirs, v_turned, early[0], 1)
    early = exchange(merge(deliver(early, "xy"), late[0]))
    late = exchange(merge(deliver(late, "xy"), late[0]))
    keep, give = close(me, first_close(early), late)
    give = swap(give)
    return project(me, keep, give, out_weight)


def solution(mesh):
    fine = Mesh(mesh.devices.reshape(4, 2, 4, 4), ALL)
    return jax.shard_map(
        body,
        mesh=fine,
        in_specs=(P(ALL, None), P(ALL, None, None), P(ALL, None, None), P(), P(), P(), P()),
        out_specs=P(ALL, None),
        check_vma=False,
    )
```

```python
import functools
import itertools

import jax
import jax.numpy as jnp
from jax import lax
from jax.experimental import pallas as pl
from jax.experimental.pallas import tpu as pltpu
from jax.sharding import Mesh, PartitionSpec as P

HD = 64
LOG2E = 1.4426950408889634
TOP_STEP = 16.0
NO_TOP = -32768.0
NH = 4
WIDE = NH * HD
ALL = ("y", "core", "z", "x")
F32 = jnp.float32
BF16 = jnp.bfloat16


def spread_kernel(me, q, theirs, out):
    first = me[1] == 0
    mine = jnp.where(first, q[:, :512].astype(F32), q[:, 512:].astype(F32))
    other = theirs[...].astype(F32)
    pair = jnp.concatenate([jnp.where(first, mine, other), jnp.where(first, other, mine)], axis=0).astype(BF16)
    for i in range(16):
        for c in range(2):
            out[i, c] = pair[:, c * WIDE:(c + 1) * WIDE]


def spread_rows(me, q, theirs):
    vmem = pl.BlockSpec(memory_space=pltpu.VMEM)
    smem = pl.BlockSpec(memory_space=pltpu.SMEM)
    return pl.pallas_call(
        spread_kernel,
        out_shape=jax.ShapeDtypeStruct((16, 2, 48, WIDE), BF16),
        in_specs=[smem, vmem, vmem],
        out_specs=vmem,
        name="spread",
    )(me, q, theirs)


def attend_kernel(
    me, need, *refs, part,
):
    qs, (k0, v0, _), outs = refs[:4], refs[4:7], refs[7:11]
    cnt, plan, qv, k, vt, qm, acc, sb, top, shrink, yb, sem = refs[11:]
    my_y, my_core, my_x = me[0], me[1], me[3]
    copies = [
        pltpu.make_async_copy(src, dst, sem.at[i])
        for i, (src, dst) in enumerate(
            [(q, qv.at[pl.ds(i * q.shape[0], q.shape[0])]) for i, q in enumerate(qs)]
            + [
                (k0.at[:, :, pl.ds(part * WIDE, WIDE)], k),
                (v0.at[:, pl.ds(part * WIDE, WIDE), :], vt),
            ]
        )
    ]
    for copy in copies:
        copy.start()
    scale = HD ** -0.5 * LOG2E
    ones = jnp.ones((16, 256), BF16)

    total, slot = jnp.int32(0), jnp.int32(0)
    for qi in range(12):
        begin = total
        for j in range(8):
            plan[total] = qi + 16 * j + 256 * slot
            total = total + need[qi, j]
        cnt[qi] = total - begin
        slot = (slot + jnp.minimum(total - begin, 1)) & 3
    for u in range(8):
        plan[total + u] = 12 + 256 * slot

    def frame_of(t):
        return plan[t] & 15

    def held_of(t):
        return (plan[t] >> 4) & 7

    def slot_of(t):
        return plan[t] >> 8

    def place(r3, z, a):
        y = jnp.where(my_core == 0, a, lax.rem(my_y + 4 - r3, 4))
        x = jnp.where(my_core == 0, lax.rem(my_x + 4 - r3, 4), a)
        return [pl.multiple_of(y * 768 + (c * 16 + z * 4 + x) * 24, 8) for c in range(2)]

    spots = [[place(r3, z, a) for z in range(4) for a in range(4)] for r3 in range(4)]
    for i, spot in enumerate(spots):
        copies[i].wait()
        for b, rows in enumerate(spot):
            block = qv[i * len(spot) + b].astype(F32)
            for c, row in enumerate(rows):
                yb[pl.ds(row, 24), :WIDE] = block[c * 24:(c + 1) * 24]

    def turn(qi, _):
        rows = pl.ds(pl.multiple_of(qi * 256, 256), 256)
        zero = jnp.zeros((64, 256), BF16)
        for hp in range(NH // 2):
            turned = yb[rows, hp * 128:(hp + 1) * 128].astype(BF16).T
            qm[qi, 2 * hp] = jnp.concatenate([turned[:64], zero], axis=0)
            qm[qi, 2 * hp + 1] = jnp.concatenate([zero, turned[64:]], axis=0)
        return 0

    def turns(u, _):
        for i in range(3):
            turn(u * 3 + i, 0)
        return 0

    lax.fori_loop(0, 4, turns, 0)
    def blank(qi, _):
        @pl.when(cnt[qi] == 0)
        def _():
            rows = pl.ds(pl.multiple_of(qi * 256, 256), 256)
            yb[rows, :WIDE] = jnp.zeros((256, WIDE), F32)
            lane = lax.broadcasted_iota(jnp.int32, (256, 128), 1)
            yb[rows, WIDE:] = jnp.where(lane < NH, NO_TOP, 0.0)

        return 0

    lax.fori_loop(0, 12, blank, 0)
    for copy in copies[4:]:
        copy.wait()
    acc[...] = jnp.zeros_like(acc)
    qm[12] = jnp.zeros((NH, 128, 256), BF16)

    def score(t, p, h):
        hp = h // 2
        keys = k[held_of(t + p), :, hp * 128:(hp + 1) * 128]
        s = jnp.dot(keys, qm[frame_of(t + p), h], preferred_element_type=F32) * scale
        sb[p, h] = s
        return jnp.max(s, axis=0, keepdims=True)

    def settle(t, p, highs, old):
        first = frame_of(t + p) != frame_of(jnp.maximum(t + p - 1, 0))
        old = jnp.where(first, NO_TOP, old)
        high = jnp.concatenate(highs, axis=0)
        new = jnp.maximum(old, jnp.ceil(high * (1.0 / TOP_STEP)) * TOP_STEP)
        top[p] = new
        shrink[p] = jnp.exp2(old - new)
        return new

    def weigh(t, p, h, tops, shrinks):
        weights = jnp.exp2(sb[p, h] - tops[h:h + 1]).astype(BF16)
        vals = jnp.concatenate([vt[held_of(t + p), h * 64:(h + 1) * 64, :], ones], axis=0)
        part = jnp.dot(vals, weights, preferred_element_type=F32)
        at = slot_of(t + p)
        acc[at, h] = acc[at, h] * shrinks[h:h + 1] + part

    def finish(t, p, tops):
        qi = frame_of(t + p)

        @pl.when((qi < 12) & (frame_of(t + p + 1) != qi))
        def _():
            at = slot_of(t + p)
            rows = pl.ds(pl.multiple_of(qi * 256, 256), 256)
            totals = jnp.concatenate([acc[at, h, 64:65, :] for h in range(NH)], axis=0)
            hi = totals.astype(BF16).astype(F32)
            extra = [tops, hi, totals - hi, jnp.zeros((128 - 3 * NH, 256), F32)]
            for hp in range(NH // 2):
                both = jnp.concatenate([acc[at, 2 * hp, :64, :], acc[at, 2 * hp + 1, :64, :]], axis=0)
                yb[rows, hp * 128:(hp + 1) * 128] = both.astype(BF16).T.astype(F32)
            yb[rows, WIDE:] = jnp.concatenate(extra, axis=0).astype(BF16).T.astype(F32)

    old = jnp.full((NH, 256), NO_TOP, F32)
    for p in range(4):
        old = settle(0, p, [score(0, p, h) for h in range(NH)], old)

    def two(u, _):
        t = u * 4
        tops, shrinks = [top[p] for p in range(4)], [shrink[p] for p in range(4)]
        highs = [[] for p in range(4)]
        for p in range(4):
            for h in range(NH):
                weigh(t, p, h, tops[p], shrinks[p])
                highs[p].append(score(t + 4, p, h))
        old = tops[3]
        for p in range(4):
            old = settle(t + 4, p, highs[p], old)
        for p in range(4):
            finish(t, p, tops[p])
        return 0

    lax.fori_loop(0, (total + 3) // 4, two, 0)

    for o, spot in zip(outs, spots):
        for b, rows in enumerate(spot):
            data, tail = [], jnp.zeros((8, 128), F32)
            for c, row in enumerate(rows):
                block = yb[pl.ds(row, 24), :]
                data.append(block[:, :WIDE])
                for p in range(3):
                    piece = block[p * 8:(p + 1) * 8, WIDE:]
                    g = c * 3 + p
                    tail = tail + (pltpu.roll(piece, 16 * g, 1) if g else piece)
            data.append(jnp.concatenate([tail, jnp.zeros((8, WIDE - 128), F32)], axis=1))
            o[b] = jnp.concatenate(data, axis=0).astype(BF16)


def attend(me, need, q, k0, v0, after, part):
    vmem = pl.BlockSpec(memory_space=pltpu.VMEM)
    smem = pl.BlockSpec(memory_space=pltpu.SMEM)
    whole = pl.BlockSpec(memory_space=pl.ANY)
    return pl.pallas_call(
        functools.partial(attend_kernel, part=part),
        out_shape=[jax.ShapeDtypeStruct((16, 56, WIDE), BF16)] * 4,
        in_specs=[smem] * 2 + [whole] * 7,
        out_specs=[vmem] * 4,
        scratch_shapes=[
            pltpu.SMEM((12,), jnp.int32),
            pltpu.SMEM((112,), jnp.int32),
            pltpu.VMEM((64, 48, WIDE), BF16),
            pltpu.VMEM((8, 256, WIDE), BF16),
            pltpu.VMEM((8, WIDE, 256), BF16),
            pltpu.VMEM((13, NH, 128, 256), BF16),
            pltpu.VMEM((4, NH, 80, 256), F32),
            pltpu.VMEM((4, NH, 256, 256), F32),
            pltpu.VMEM((4, NH, 256), F32),
            pltpu.VMEM((4, NH, 256), F32),
            pltpu.VMEM((3072, WIDE + 128), F32),
            pltpu.SemaphoreType.DMA((6,)),
        ],
        compiler_params=pltpu.CompilerParams(vmem_limit_bytes=24 * 2**20),
        cost_estimate=pl.CostEstimate(flops=10**10, bytes_accessed=2**23, transcendentals=2 * 10**7),
        name="attend",
    )(me, need, *q, k0, v0, after)


def turn_kernel(me, v0, v1, k0, k1, out, keys, parts, held, sem):
    parts[0] = 0
    parts[1] = 1
    col = pl.multiple_of(me[1] * 512, 512)
    copies = [
        pltpu.make_async_copy(src.at[:, :, pl.ds(col, 512)], dst.at[pl.ds(i % 2 * 4, 4)], sem.at[i])
        for i, (src, dst) in enumerate([(v0, held), (v1, held), (k0, keys), (k1, keys)])
    ]
    for copy in copies:
        copy.start()
    for copy in copies[:2]:
        copy.wait()

    def one(j, _):
        for at in range(0, 512, 128):
            out[j, at:at + 128, :] = held[j, :, at:at + 128].astype(F32).T.astype(BF16)
        return 0

    lax.fori_loop(0, 8, one, 0)
    for copy in copies[2:]:
        copy.wait()


def turn_values(me, v0, v1, k0, k1):
    vmem = pl.BlockSpec(memory_space=pltpu.VMEM)
    smem = pl.BlockSpec(memory_space=pltpu.SMEM)
    whole = pl.BlockSpec(memory_space=pl.ANY)
    return pl.pallas_call(
        turn_kernel,
        out_shape=[
            jax.ShapeDtypeStruct((8, 512, 256), BF16),
            jax.ShapeDtypeStruct((8, 256, 512), BF16),
            jax.ShapeDtypeStruct((2,), jnp.int32),
        ],
        in_specs=[smem] + [whole] * 4,
        out_specs=[vmem, vmem, smem],
        scratch_shapes=[pltpu.VMEM((8, 256, 512), BF16), pltpu.SemaphoreType.DMA((4,))],
        cost_estimate=pl.CostEstimate(flops=10**6, bytes_accessed=2**23, transcendentals=0),
        compiler_params=pltpu.CompilerParams(vmem_limit_bytes=16 * 2**20),
        name="turn",
    )(me, v0, v1, k0, k1)


def add_up(data, tails, spread):
    n = len(data)
    best = functools.reduce(jnp.maximum, tails)
    shares = [jnp.exp2(jnp.minimum(t - best, 0.0)) for t in tails]
    total = sum(f * (pltpu.roll(t, 128 - NH, 1) + pltpu.roll(t, 128 - 2 * NH, 1)) for f, t in zip(shares, tails))
    stack = jnp.concatenate(shares, axis=0)
    groups = data[0].shape[0] // 8
    stack = jnp.concatenate([stack] + [pltpu.roll(stack, 128 - 16 * g, 1) for g in range(1, groups)], axis=0)
    wide = jnp.dot(stack.astype(BF16), spread, preferred_element_type=F32)
    numer = []
    for g in range(groups):
        at = g * 8 * n
        numer.append(
            sum(wide[at + s * 8:at + s * 8 + 8] * d[g * 8:g * 8 + 8, :].astype(F32) for s, d in enumerate(data))
        )
    return numer, best, total


def make_spread():
    src = lax.broadcasted_iota(jnp.int32, (128, WIDE), 0)
    dst = lax.broadcasted_iota(jnp.int32, (128, WIDE), 1) // HD
    return src == dst


def add_blocks(held, spread, is_top):
    data, tails = [p[:48] for p in held], [p[48:56, :128].astype(F32) for p in held]
    numer, best, total = add_up(data, tails, spread)
    total = jnp.where(is_top, total, 0.0)
    hi = total.astype(BF16).astype(F32)
    tail = jnp.where(is_top, best, 0.0) + pltpu.roll(hi, NH, 1) + pltpu.roll(total - hi, 2 * NH, 1)
    return numer, jnp.concatenate([tail, jnp.zeros((8, WIDE - 128), F32)], axis=1)


def merge_kernel(p0, p1, p2, p3, after, out):
    spread = make_spread().astype(BF16)
    is_top = lax.broadcasted_iota(jnp.int32, (8, 128), 1) % 16 < NH
    for b in range(16):
        numer, tail = add_blocks([p[b] for p in (p0, p1, p2, p3)], spread, is_top)
        out[b] = jnp.concatenate(numer + [tail], axis=0).astype(BF16)


def merge(parts, after):
    vmem = pl.BlockSpec(memory_space=pltpu.VMEM)
    return pl.pallas_call(
        merge_kernel,
        out_shape=jax.ShapeDtypeStruct((16, 56, WIDE), BF16),
        in_specs=[vmem] * 4 + [pl.BlockSpec(memory_space=pl.ANY)],
        out_specs=vmem,
        compiler_params=pltpu.CompilerParams(vmem_limit_bytes=16 * 2**20),
        name="merge",
    )(*parts, after)


def settle_rows(got):
    spread = make_spread()
    held = [got[i] for i in range(16)]
    numer, _, total = add_up([p[:48] for p in held], [p[48:56, :128].astype(F32) for p in held], spread.astype(BF16))
    totals = jnp.concatenate([total] + [pltpu.roll(total, 128 - 16 * g, 1) for g in range(1, 6)], axis=0)
    wide = jnp.dot(totals, spread.astype(F32), precision=lax.Precision.HIGHEST, preferred_element_type=F32)
    return jnp.concatenate(numer, axis=0) / wide


def first_close_kernel(got, out):
    out[...] = settle_rows(got)


def first_close(got):
    vmem = pl.BlockSpec(memory_space=pltpu.VMEM)
    return pl.pallas_call(
        first_close_kernel,
        out_shape=jax.ShapeDtypeStruct((48, WIDE), F32),
        in_specs=[vmem],
        out_specs=vmem,
        name="first_close",
    )(got)


def close_kernel(me, ready, got, keep, give, both):
    both[:, :WIDE] = ready[...]
    both[:, WIDE:] = settle_rows(got)
    row = pl.multiple_of(me[1] * 24, 8)
    keep[...] = both[pl.ds(row, 24), :].astype(BF16)
    give[...] = both[pl.ds(24 - row, 24), :].astype(BF16)


def close(me, ready, got):
    vmem = pl.BlockSpec(memory_space=pltpu.VMEM)
    smem = pl.BlockSpec(memory_space=pltpu.SMEM)
    return pl.pallas_call(
        close_kernel,
        out_shape=[jax.ShapeDtypeStruct((24, 512), BF16)] * 2,
        in_specs=[smem, vmem, vmem],
        out_specs=[vmem] * 2,
        scratch_shapes=[pltpu.VMEM((48, 512), F32)],
        name="close",
    )(me, ready, got)


def swap(x):
    return lax.ppermute(x, "core", [(0, 1), (1, 0)])


def shift(x, axes, by):
    pairs = []
    for y, c, z, w in itertools.product(range(4), range(2), range(4), range(4)):
        to = {"y": y, "z": z, "x": w}
        to[axes[c]] = (to[axes[c]] + by) % 4
        pairs.append((((y * 2 + c) * 4 + z) * 4 + w, ((to["y"] * 2 + c) * 4 + to["z"]) * 4 + to["x"]))
    return lax.ppermute(x, ALL, pairs)


def ring(x, axes):
    return [x] + [shift(x, axes, by) for by in (1, 2, 3)]


def spot(y, c, z, x):
    return ((y * 2 + c) * 4 + z) * 4 + x


GROUPS = [[spot(a, 0, z, w) for z in range(4) for a in range(4)] for w in range(4)] + [
    [spot(w, 1, z, a) for z in range(4) for a in range(4)] for w in range(4)
]


def exchange(x):
    return lax.all_to_all(x, ALL, 0, 0, axis_index_groups=GROUPS)


def deliver(parts, axes):
    return [parts[0]] + [shift(parts[by], axes, -by) for by in (1, 2, 3)]


def body(queries, keys, values, frame_slot, covisible, counts, out_weight):
    core = lax.axis_index("core")
    device = lax.axis_index(ALL)
    partner = device + 16 - 32 * core
    own_col = core * 512

    theirs = swap(lax.dynamic_slice_in_dim(queries, 512 - own_col, 512, 1))
    me = jnp.stack([lax.axis_index(a) for a in ALL]).astype(jnp.int32)
    plane = exchange(spread_rows(me, queries, theirs))
    k_theirs, v_theirs = swap(keys), swap(values)
    v_turned, k_half, parts = turn_values(me, values, v_theirs, keys, k_theirs)
    q_parts = [ring(lax.dynamic_index_in_dim(plane, parts[c], 1, False), "xy") for c in range(2)]

    four = jnp.arange(4, dtype=jnp.int32)
    slots = jnp.concatenate([device * 4 + four, partner * 4 + four])
    frame_ids = jnp.arange(frame_slot.shape[0], dtype=jnp.int32)
    local = jnp.sum(jnp.where(frame_slot[None, :] == slots[:, None], frame_ids[None, :], 0), axis=1)
    used = jnp.arange(covisible.shape[1], dtype=jnp.int32)[None, :] < counts[:, None]
    need = jnp.any((covisible[:, None, :] == local[None, :, None]) & used[:, None, :], axis=2)
    need = need.astype(jnp.int32)

    early = attend(me, need, q_parts[0], k_half, v_turned, q_parts[0][0], 0)
    late = attend(me, need, q_parts[1], k_half, v_turned, early[0], 1)
    early = exchange(merge(deliver(early, "xy"), late[0]))
    late = exchange(merge(deliver(late, "xy"), late[0]))
    keep, give = close(me, first_close(early), late)
    give = swap(give)
    first = core == 0
    rows = jnp.concatenate([jnp.where(first, keep, give), jnp.where(first, give, keep)], axis=1)
    return jnp.dot(rows, out_weight, preferred_element_type=F32).astype(BF16)


def solution(mesh):
    fine = Mesh(mesh.devices.reshape(4, 2, 4, 4), ALL)
    return jax.shard_map(
        body,
        mesh=fine,
        in_specs=(P(ALL, None), P(ALL, None, None), P(ALL, None, None), P(), P(), P(), P()),
        out_specs=P(ALL, None),
        check_vma=False,
    )
```

```python
import functools
import itertools

import jax
import jax.numpy as jnp
from jax import lax
from jax.experimental import pallas as pl
from jax.experimental.pallas import tpu as pltpu
from jax.sharding import Mesh, PartitionSpec as P

HD = 64
LOG2E = 1.4426950408889634
TOP_STEP = 16.0
NO_TOP = -32768.0
NH = 4
WIDE = NH * HD
ALL = ("y", "core", "z", "x")
F32 = jnp.float32
BF16 = jnp.bfloat16


def spread_kernel(me, q, theirs, out):
    first = me[1] == 0
    mine = jnp.where(first, q[:, :512].astype(F32), q[:, 512:].astype(F32))
    other = theirs[...].astype(F32)
    pair = jnp.concatenate([jnp.where(first, mine, other), jnp.where(first, other, mine)], axis=0).astype(BF16)
    for i in range(16):
        for c in range(2):
            out[i, c] = pair[:, c * WIDE:(c + 1) * WIDE]


def spread_rows(me, q, theirs):
    vmem = pl.BlockSpec(memory_space=pltpu.VMEM)
    smem = pl.BlockSpec(memory_space=pltpu.SMEM)
    return pl.pallas_call(
        spread_kernel,
        out_shape=jax.ShapeDtypeStruct((16, 2, 48, WIDE), BF16),
        in_specs=[smem, vmem, vmem],
        out_specs=vmem,
        name="spread",
    )(me, q, theirs)


def attend_kernel(
    me, need, *refs, part,
):
    qs, (k0, k1, v0, _), outs = refs[:4], refs[4:8], refs[8:12]
    cnt, plan, qv, k, vt, qm, acc, sb, top, shrink, yb, sem = refs[12:]
    my_y, my_core, my_x = me[0], me[1], me[3]
    col = pl.multiple_of(my_core * 512 + part * WIDE, WIDE)
    copies = [
        pltpu.make_async_copy(src, dst, sem.at[i])
        for i, (src, dst) in enumerate(
            [(q, qv.at[pl.ds(i * q.shape[0], q.shape[0])]) for i, q in enumerate(qs)]
            + [
                (k0.at[:, :, pl.ds(col, WIDE)], k.at[pl.ds(0, 4)]),
                (k1.at[:, :, pl.ds(col, WIDE)], k.at[pl.ds(4, 4)]),
                (v0.at[:, pl.ds(part * WIDE, WIDE), :], vt),
            ]
        )
    ]
    for copy in copies:
        copy.start()
    scale = HD ** -0.5 * LOG2E
    ones = jnp.ones((16, 256), BF16)

    total, slot = jnp.int32(0), jnp.int32(0)
    for qi in range(12):
        begin = total
        for j in range(8):
            plan[total] = qi + 16 * j + 256 * slot
            total = total + need[qi, j]
        cnt[qi] = total - begin
        slot = (slot + jnp.minimum(total - begin, 1)) & 3
    for u in range(8):
        plan[total + u] = 12 + 256 * slot

    def frame_of(t):
        return plan[t] & 15

    def held_of(t):
        return (plan[t] >> 4) & 7

    def slot_of(t):
        return plan[t] >> 8

    def place(r3, z, a):
        y = jnp.where(my_core == 0, a, lax.rem(my_y + 4 - r3, 4))
        x = jnp.where(my_core == 0, lax.rem(my_x + 4 - r3, 4), a)
        return [pl.multiple_of(y * 768 + (c * 16 + z * 4 + x) * 24, 8) for c in range(2)]

    spots = [[place(r3, z, a) for z in range(4) for a in range(4)] for r3 in range(4)]
    for i, spot in enumerate(spots):
        copies[i].wait()
        for b, rows in enumerate(spot):
            block = qv[i * len(spot) + b].astype(F32)
            for c, row in enumerate(rows):
                yb[pl.ds(row, 24), :WIDE] = block[c * 24:(c + 1) * 24]

    def turn(qi, _):
        rows = pl.ds(pl.multiple_of(qi * 256, 256), 256)
        zero = jnp.zeros((64, 256), BF16)
        for hp in range(NH // 2):
            turned = yb[rows, hp * 128:(hp + 1) * 128].astype(BF16).T
            qm[qi, 2 * hp] = jnp.concatenate([turned[:64], zero], axis=0)
            qm[qi, 2 * hp + 1] = jnp.concatenate([zero, turned[64:]], axis=0)
        return 0

    def turns(u, _):
        for i in range(3):
            turn(u * 3 + i, 0)
        return 0

    lax.fori_loop(0, 4, turns, 0)
    def blank(qi, _):
        @pl.when(cnt[qi] == 0)
        def _():
            rows = pl.ds(pl.multiple_of(qi * 256, 256), 256)
            yb[rows, :WIDE] = jnp.zeros((256, WIDE), F32)
            lane = lax.broadcasted_iota(jnp.int32, (256, 128), 1)
            yb[rows, WIDE:] = jnp.where(lane < NH, NO_TOP, 0.0)

        return 0

    lax.fori_loop(0, 12, blank, 0)
    for copy in copies[4:]:
        copy.wait()
    acc[...] = jnp.zeros_like(acc)
    qm[12] = jnp.zeros((NH, 128, 256), BF16)

    def score(t, p, h):
        hp = h // 2
        keys = k[held_of(t + p), :, hp * 128:(hp + 1) * 128]
        s = jnp.dot(keys, qm[frame_of(t + p), h], preferred_element_type=F32) * scale
        sb[p, h] = s
        return jnp.max(s, axis=0, keepdims=True)

    def settle(t, p, highs, old):
        first = frame_of(t + p) != frame_of(jnp.maximum(t + p - 1, 0))
        old = jnp.where(first, NO_TOP, old)
        high = jnp.concatenate(highs, axis=0)
        new = jnp.maximum(old, jnp.ceil(high * (1.0 / TOP_STEP)) * TOP_STEP)
        top[p] = new
        shrink[p] = jnp.exp2(old - new)
        return new

    def weigh(t, p, h, tops, shrinks):
        weights = jnp.exp2(sb[p, h] - tops[h:h + 1]).astype(BF16)
        vals = jnp.concatenate([vt[held_of(t + p), h * 64:(h + 1) * 64, :], ones], axis=0)
        part = jnp.dot(vals, weights, preferred_element_type=F32)
        at = slot_of(t + p)
        acc[at, h] = acc[at, h] * shrinks[h:h + 1] + part

    def finish(t, p, tops):
        qi = frame_of(t + p)

        @pl.when((qi < 12) & (frame_of(t + p + 1) != qi))
        def _():
            at = slot_of(t + p)
            rows = pl.ds(pl.multiple_of(qi * 256, 256), 256)
            totals = jnp.concatenate([acc[at, h, 64:65, :] for h in range(NH)], axis=0)
            hi = totals.astype(BF16).astype(F32)
            extra = [tops, hi, totals - hi, jnp.zeros((128 - 3 * NH, 256), F32)]
            for hp in range(NH // 2):
                both = jnp.concatenate([acc[at, 2 * hp, :64, :], acc[at, 2 * hp + 1, :64, :]], axis=0)
                yb[rows, hp * 128:(hp + 1) * 128] = both.astype(BF16).T.astype(F32)
            yb[rows, WIDE:] = jnp.concatenate(extra, axis=0).astype(BF16).T.astype(F32)

    old = jnp.full((NH, 256), NO_TOP, F32)
    for p in range(4):
        old = settle(0, p, [score(0, p, h) for h in range(NH)], old)

    def two(u, _):
        t = u * 4
        tops, shrinks = [top[p] for p in range(4)], [shrink[p] for p in range(4)]
        highs = [[] for p in range(4)]
        for p in range(4):
            for h in range(NH):
                weigh(t, p, h, tops[p], shrinks[p])
                highs[p].append(score(t + 4, p, h))
        old = tops[3]
        for p in range(4):
            old = settle(t + 4, p, highs[p], old)
        for p in range(4):
            finish(t, p, tops[p])
        return 0

    lax.fori_loop(0, (total + 3) // 4, two, 0)

    for o, spot in zip(outs, spots):
        for b, rows in enumerate(spot):
            data, tail = [], jnp.zeros((8, 128), F32)
            for c, row in enumerate(rows):
                block = yb[pl.ds(row, 24), :]
                data.append(block[:, :WIDE])
                for p in range(3):
                    piece = block[p * 8:(p + 1) * 8, WIDE:]
                    g = c * 3 + p
                    tail = tail + (pltpu.roll(piece, 16 * g, 1) if g else piece)
            data.append(jnp.concatenate([tail, jnp.zeros((8, WIDE - 128), F32)], axis=1))
            o[b] = jnp.concatenate(data, axis=0).astype(BF16)


def attend(me, need, q, k0, k1, v0, after, part):
    vmem = pl.BlockSpec(memory_space=pltpu.VMEM)
    smem = pl.BlockSpec(memory_space=pltpu.SMEM)
    whole = pl.BlockSpec(memory_space=pl.ANY)
    far = pl.BlockSpec(memory_space=pltpu.HBM)
    return pl.pallas_call(
        functools.partial(attend_kernel, part=part),
        out_shape=[jax.ShapeDtypeStruct((16, 56, WIDE), BF16)] * 4,
        in_specs=[smem] * 2 + [whole] * 4 + [far, whole, far, whole],
        out_specs=[vmem] * 4,
        scratch_shapes=[
            pltpu.SMEM((12,), jnp.int32),
            pltpu.SMEM((112,), jnp.int32),
            pltpu.VMEM((64, 48, WIDE), BF16),
            pltpu.VMEM((8, 256, WIDE), BF16),
            pltpu.VMEM((8, WIDE, 256), BF16),
            pltpu.VMEM((13, NH, 128, 256), BF16),
            pltpu.VMEM((4, NH, 80, 256), F32),
            pltpu.VMEM((4, NH, 256, 256), F32),
            pltpu.VMEM((4, NH, 256), F32),
            pltpu.VMEM((4, NH, 256), F32),
            pltpu.VMEM((3072, WIDE + 128), F32),
            pltpu.SemaphoreType.DMA((7,)),
        ],
        compiler_params=pltpu.CompilerParams(vmem_limit_bytes=24 * 2**20),
        cost_estimate=pl.CostEstimate(flops=10**10, bytes_accessed=2**23, transcendentals=2 * 10**7),
        name="attend",
    )(me, need, *q, pltpu.with_memory_space_constraint(k0, pltpu.HBM), k1, pltpu.with_memory_space_constraint(v0, pltpu.HBM), after)


def turn_kernel(me, v0, v1, k, out, parts, held, turned, sem):
    parts[0] = 0
    parts[1] = 1
    col = pl.multiple_of(me[1] * 512, 512)
    copies = [
        pltpu.make_async_copy(v.at[:, :, pl.ds(col, 512)], held.at[pl.ds(i * 4, 4)], sem.at[i])
        for i, v in enumerate((v0, v1))
    ]
    for copy in copies:
        copy.start()
    backs = []
    for j in range(8):
        if j % 4 == 0:
            copies[j // 4].wait()
        for at in range(0, 512, 128):
            turned[j, at:at + 128, :] = held[j, :, at:at + 128].T
        back = pltpu.make_async_copy(turned.at[j], out.at[j], sem.at[2 + j])
        back.start()
        backs.append(back)
    for back in backs:
        back.wait()


def turn_values(me, v0, v1, k):
    smem = pl.BlockSpec(memory_space=pltpu.SMEM)
    far = pl.BlockSpec(memory_space=pltpu.HBM)
    whole = pl.BlockSpec(memory_space=pl.ANY)
    return pl.pallas_call(
        turn_kernel,
        out_shape=[pltpu.HBM((8, 512, 256), BF16), jax.ShapeDtypeStruct((2,), jnp.int32)],
        in_specs=[smem, far, whole, whole],
        out_specs=[far, smem],
        scratch_shapes=[
            pltpu.VMEM((8, 256, 512), BF16),
            pltpu.VMEM((8, 512, 256), BF16),
            pltpu.SemaphoreType.DMA((10,)),
        ],
        cost_estimate=pl.CostEstimate(flops=10**6, bytes_accessed=2**23, transcendentals=0),
        compiler_params=pltpu.CompilerParams(vmem_limit_bytes=16 * 2**20),
        name="turn",
    )(me, pltpu.with_memory_space_constraint(v0, pltpu.HBM), v1, k)


def add_up(data, tails, spread):
    n = len(data)
    best = functools.reduce(jnp.maximum, tails)
    shares = [jnp.exp2(jnp.minimum(t - best, 0.0)) for t in tails]
    total = sum(f * (pltpu.roll(t, 128 - NH, 1) + pltpu.roll(t, 128 - 2 * NH, 1)) for f, t in zip(shares, tails))
    stack = jnp.concatenate(shares, axis=0)
    groups = data[0].shape[0] // 8
    stack = jnp.concatenate([stack] + [pltpu.roll(stack, 128 - 16 * g, 1) for g in range(1, groups)], axis=0)
    wide = jnp.dot(stack.astype(BF16), spread, preferred_element_type=F32)
    numer = []
    for g in range(groups):
        at = g * 8 * n
        numer.append(
            sum(wide[at + s * 8:at + s * 8 + 8] * d[g * 8:g * 8 + 8, :].astype(F32) for s, d in enumerate(data))
        )
    return numer, best, total


def make_spread():
    src = lax.broadcasted_iota(jnp.int32, (128, WIDE), 0)
    dst = lax.broadcasted_iota(jnp.int32, (128, WIDE), 1) // HD
    return src == dst


def add_blocks(held, spread, is_top):
    data, tails = [p[:48] for p in held], [p[48:56, :128].astype(F32) for p in held]
    numer, best, total = add_up(data, tails, spread)
    total = jnp.where(is_top, total, 0.0)
    hi = total.astype(BF16).astype(F32)
    tail = jnp.where(is_top, best, 0.0) + pltpu.roll(hi, NH, 1) + pltpu.roll(total - hi, 2 * NH, 1)
    return numer, jnp.concatenate([tail, jnp.zeros((8, WIDE - 128), F32)], axis=1)


def merge_kernel(p0, p1, p2, p3, after, out):
    spread = make_spread().astype(BF16)
    is_top = lax.broadcasted_iota(jnp.int32, (8, 128), 1) % 16 < NH
    for b in range(16):
        numer, tail = add_blocks([p[b] for p in (p0, p1, p2, p3)], spread, is_top)
        out[b] = jnp.concatenate(numer + [tail], axis=0).astype(BF16)


def merge(parts, after):
    vmem = pl.BlockSpec(memory_space=pltpu.VMEM)
    return pl.pallas_call(
        merge_kernel,
        out_shape=jax.ShapeDtypeStruct((16, 56, WIDE), BF16),
        in_specs=[vmem] * 4 + [pl.BlockSpec(memory_space=pl.ANY)],
        out_specs=vmem,
        compiler_params=pltpu.CompilerParams(vmem_limit_bytes=16 * 2**20),
        name="merge",
    )(*parts, after)


def settle_rows(got):
    spread = make_spread()
    held = [got[i] for i in range(16)]
    numer, _, total = add_up([p[:48] for p in held], [p[48:56, :128].astype(F32) for p in held], spread.astype(BF16))
    totals = jnp.concatenate([total] + [pltpu.roll(total, 128 - 16 * g, 1) for g in range(1, 6)], axis=0)
    wide = jnp.dot(totals, spread.astype(F32), precision=lax.Precision.HIGHEST, preferred_element_type=F32)
    return jnp.concatenate(numer, axis=0) / wide


def first_close_kernel(got, out):
    out[...] = settle_rows(got)


def first_close(got):
    vmem = pl.BlockSpec(memory_space=pltpu.VMEM)
    return pl.pallas_call(
        first_close_kernel,
        out_shape=jax.ShapeDtypeStruct((48, WIDE), F32),
        in_specs=[vmem],
        out_specs=vmem,
        name="first_close",
    )(got)


def close_kernel(me, ready, got, keep, give, both):
    both[:, :WIDE] = ready[...]
    both[:, WIDE:] = settle_rows(got)
    row = pl.multiple_of(me[1] * 24, 8)
    keep[...] = both[pl.ds(row, 24), :].astype(BF16)
    give[...] = both[pl.ds(24 - row, 24), :].astype(BF16)


def close(me, ready, got):
    vmem = pl.BlockSpec(memory_space=pltpu.VMEM)
    smem = pl.BlockSpec(memory_space=pltpu.SMEM)
    return pl.pallas_call(
        close_kernel,
        out_shape=[jax.ShapeDtypeStruct((24, 512), BF16)] * 2,
        in_specs=[smem, vmem, vmem],
        out_specs=[vmem] * 2,
        scratch_shapes=[pltpu.VMEM((48, 512), F32)],
        name="close",
    )(me, ready, got)


def swap(x):
    return lax.ppermute(x, "core", [(0, 1), (1, 0)])


def shift(x, axes, by):
    pairs = []
    for y, c, z, w in itertools.product(range(4), range(2), range(4), range(4)):
        to = {"y": y, "z": z, "x": w}
        to[axes[c]] = (to[axes[c]] + by) % 4
        pairs.append((((y * 2 + c) * 4 + z) * 4 + w, ((to["y"] * 2 + c) * 4 + to["z"]) * 4 + to["x"]))
    return lax.ppermute(x, ALL, pairs)


def ring(x, axes):
    return [x] + [shift(x, axes, by) for by in (1, 2, 3)]


def spot(y, c, z, x):
    return ((y * 2 + c) * 4 + z) * 4 + x


GROUPS = [[spot(a, 0, z, w) for z in range(4) for a in range(4)] for w in range(4)] + [
    [spot(w, 1, z, a) for z in range(4) for a in range(4)] for w in range(4)
]


def exchange(x):
    return lax.all_to_all(x, ALL, 0, 0, axis_index_groups=GROUPS)


def deliver(parts, axes):
    return [parts[0]] + [shift(parts[by], axes, -by) for by in (1, 2, 3)]


def body(queries, keys, values, frame_slot, covisible, counts, out_weight):
    core = lax.axis_index("core")
    device = lax.axis_index(ALL)
    partner = device + 16 - 32 * core
    own_col = core * 512

    theirs = swap(lax.dynamic_slice_in_dim(queries, 512 - own_col, 512, 1))
    me = jnp.stack([lax.axis_index(a) for a in ALL]).astype(jnp.int32)
    plane = exchange(spread_rows(me, queries, theirs))
    k_theirs, v_theirs = swap(keys), swap(values)
    v_turned, parts = turn_values(me, values, v_theirs, k_theirs)
    q_parts = [ring(lax.dynamic_index_in_dim(plane, parts[c], 1, False), "xy") for c in range(2)]

    four = jnp.arange(4, dtype=jnp.int32)
    slots = jnp.concatenate([device * 4 + four, partner * 4 + four])
    frame_ids = jnp.arange(frame_slot.shape[0], dtype=jnp.int32)
    local = jnp.sum(jnp.where(frame_slot[None, :] == slots[:, None], frame_ids[None, :], 0), axis=1)
    used = jnp.arange(covisible.shape[1], dtype=jnp.int32)[None, :] < counts[:, None]
    need = jnp.any((covisible[:, None, :] == local[None, :, None]) & used[:, None, :], axis=2)
    need = need.astype(jnp.int32)

    early = attend(me, need, q_parts[0], keys, k_theirs, v_turned, q_parts[0][0], 0)
    late = attend(me, need, q_parts[1], keys, k_theirs, v_turned, early[0], 1)
    early = exchange(merge(deliver(early, "xy"), late[0]))
    late = exchange(merge(deliver(late, "xy"), late[0]))
    keep, give = close(me, first_close(early), late)
    give = swap(give)
    first = core == 0
    rows = jnp.concatenate([jnp.where(first, keep, give), jnp.where(first, give, keep)], axis=1)
    return jnp.dot(rows, out_weight, preferred_element_type=F32).astype(BF16)


def solution(mesh):
    fine = Mesh(mesh.devices.reshape(4, 2, 4, 4), ALL)
    return jax.shard_map(
        body,
        mesh=fine,
        in_specs=(P(ALL, None), P(ALL, None, None), P(ALL, None, None), P(), P(), P(), P()),
        out_specs=P(ALL, None),
        check_vma=False,
    )
```

```python
import functools
import itertools

import jax
import jax.numpy as jnp
from jax import lax
from jax.experimental import pallas as pl
from jax.experimental.pallas import tpu as pltpu
from jax.sharding import Mesh, PartitionSpec as P

HD = 64
LOG2E = 1.4426950408889634
TOP_STEP = 16.0
NO_TOP = -32768.0
NH = 4
WIDE = NH * HD
ALL = ("y", "core", "z", "x")
F32 = jnp.float32
BF16 = jnp.bfloat16


def spread_kernel(me, q, theirs, out):
    first = me[1] == 0
    mine = jnp.where(first, q[:, :512].astype(F32), q[:, 512:].astype(F32))
    other = theirs[...].astype(F32)
    pair = jnp.concatenate([jnp.where(first, mine, other), jnp.where(first, other, mine)], axis=0).astype(BF16)
    for i in range(16):
        for c in range(2):
            out[i, c] = pair[:, c * WIDE:(c + 1) * WIDE]


def spread_rows(me, q, theirs):
    vmem = pl.BlockSpec(memory_space=pltpu.VMEM)
    smem = pl.BlockSpec(memory_space=pltpu.SMEM)
    return pl.pallas_call(
        spread_kernel,
        out_shape=jax.ShapeDtypeStruct((16, 2, 48, WIDE), BF16),
        in_specs=[smem, vmem, vmem],
        out_specs=vmem,
        name="spread",
    )(me, q, theirs)


def attend_kernel(
    me, need, *refs, part,
):
    qs, (k0, k1, v0, _), outs = refs[:4], refs[4:8], refs[8:12]
    cnt, plan, qv, k, vt, qm, acc, sb, top, shrink, yb, sem = refs[12:]
    my_y, my_core, my_x = me[0], me[1], me[3]
    col = pl.multiple_of(my_core * 512 + part * WIDE, WIDE)
    copies = [
        pltpu.make_async_copy(src, dst, sem.at[i])
        for i, (src, dst) in enumerate(
            [(q, qv.at[pl.ds(i * q.shape[0], q.shape[0])]) for i, q in enumerate(qs)]
            + [
                (k0.at[:, :, pl.ds(col, WIDE)], k.at[pl.ds(0, 4)]),
                (k1.at[:, :, pl.ds(col, WIDE)], k.at[pl.ds(4, 4)]),
                (v0.at[:, pl.ds(part * WIDE, WIDE), :], vt),
            ]
        )
    ]
    for copy in copies:
        copy.start()
    scale = HD ** -0.5 * LOG2E
    ones = jnp.ones((16, 256), BF16)

    total, slot = jnp.int32(0), jnp.int32(0)
    for qi in range(12):
        begin = total
        for j in range(8):
            plan[total] = qi + 16 * j + 256 * slot
            total = total + need[qi, j]
        cnt[qi] = total - begin
        slot = (slot + jnp.minimum(total - begin, 1)) & 3
    for u in range(8):
        plan[total + u] = 12 + 256 * slot

    def frame_of(t):
        return plan[t] & 15

    def held_of(t):
        return (plan[t] >> 4) & 7

    def slot_of(t):
        return plan[t] >> 8

    def place(r3, z, a):
        y = jnp.where(my_core == 0, a, lax.rem(my_y + 4 - r3, 4))
        x = jnp.where(my_core == 0, lax.rem(my_x + 4 - r3, 4), a)
        return [pl.multiple_of(y * 768 + (c * 16 + z * 4 + x) * 24, 8) for c in range(2)]

    spots = [[place(r3, z, a) for z in range(4) for a in range(4)] for r3 in range(4)]
    for i, spot in enumerate(spots):
        copies[i].wait()
        for b, rows in enumerate(spot):
            block = qv[i * len(spot) + b].astype(F32)
            for c, row in enumerate(rows):
                yb[pl.ds(row, 24), :WIDE] = block[c * 24:(c + 1) * 24]

    def turn(qi, _):
        rows = pl.ds(pl.multiple_of(qi * 256, 256), 256)
        zero = jnp.zeros((64, 256), BF16)
        for hp in range(NH // 2):
            turned = yb[rows, hp * 128:(hp + 1) * 128].astype(BF16).T
            qm[qi, 2 * hp] = jnp.concatenate([turned[:64], zero], axis=0)
            qm[qi, 2 * hp + 1] = jnp.concatenate([zero, turned[64:]], axis=0)
        return 0

    def turns(u, _):
        for i in range(3):
            turn(u * 3 + i, 0)
        return 0

    lax.fori_loop(0, 4, turns, 0)
    def blank(qi, _):
        @pl.when(cnt[qi] == 0)
        def _():
            rows = pl.ds(pl.multiple_of(qi * 256, 256), 256)
            yb[rows, :WIDE] = jnp.zeros((256, WIDE), F32)
            lane = lax.broadcasted_iota(jnp.int32, (256, 128), 1)
            yb[rows, WIDE:] = jnp.where(lane < NH, NO_TOP, 0.0)

        return 0

    lax.fori_loop(0, 12, blank, 0)
    for copy in copies[4:]:
        copy.wait()
    acc[...] = jnp.zeros_like(acc)
    qm[12] = jnp.zeros((NH, 128, 256), BF16)

    def score(t, p, h):
        hp = h // 2
        keys = k[held_of(t + p), :, hp * 128:(hp + 1) * 128]
        s = jnp.dot(keys, qm[frame_of(t + p), h], preferred_element_type=F32) * scale
        sb[p, h] = s
        return jnp.max(s, axis=0, keepdims=True)

    def settle(t, p, highs, old):
        first = frame_of(t + p) != frame_of(jnp.maximum(t + p - 1, 0))
        old = jnp.where(first, NO_TOP, old)
        high = jnp.concatenate(highs, axis=0)
        new = jnp.maximum(old, jnp.ceil(high * (1.0 / TOP_STEP)) * TOP_STEP)
        top[p] = new
        shrink[p] = jnp.exp2(old - new)
        return new

    def weigh(t, p, h, tops, shrinks):
        weights = jnp.exp2(sb[p, h] - tops[h:h + 1]).astype(BF16)
        vals = jnp.concatenate([vt[held_of(t + p), h * 64:(h + 1) * 64, :], ones], axis=0)
        part = jnp.dot(vals, weights, preferred_element_type=F32)
        at = slot_of(t + p)
        acc[at, h] = acc[at, h] * shrinks[h:h + 1] + part

    def finish(t, p, tops):
        qi = frame_of(t + p)

        @pl.when((qi < 12) & (frame_of(t + p + 1) != qi))
        def _():
            at = slot_of(t + p)
            rows = pl.ds(pl.multiple_of(qi * 256, 256), 256)
            totals = jnp.concatenate([acc[at, h, 64:65, :] for h in range(NH)], axis=0)
            hi = totals.astype(BF16).astype(F32)
            extra = [tops, hi, totals - hi, jnp.zeros((128 - 3 * NH, 256), F32)]
            for hp in range(NH // 2):
                both = jnp.concatenate([acc[at, 2 * hp, :64, :], acc[at, 2 * hp + 1, :64, :]], axis=0)
                yb[rows, hp * 128:(hp + 1) * 128] = both.astype(BF16).T.astype(F32)
            yb[rows, WIDE:] = jnp.concatenate(extra, axis=0).astype(BF16).T.astype(F32)

    old = jnp.full((NH, 256), NO_TOP, F32)
    for p in range(4):
        old = settle(0, p, [score(0, p, h) for h in range(NH)], old)

    def two(u, _):
        t = u * 4
        tops, shrinks = [top[p] for p in range(4)], [shrink[p] for p in range(4)]
        highs = [[] for p in range(4)]
        for p in range(4):
            for h in range(NH):
                weigh(t, p, h, tops[p], shrinks[p])
                highs[p].append(score(t + 4, p, h))
        old = tops[3]
        for p in range(4):
            old = settle(t + 4, p, highs[p], old)
        for p in range(4):
            finish(t, p, tops[p])
        return 0

    lax.fori_loop(0, (total + 3) // 4, two, 0)

    for o, spot in zip(outs, spots):
        for b, rows in enumerate(spot):
            data, tail = [], jnp.zeros((8, 128), F32)
            for c, row in enumerate(rows):
                block = yb[pl.ds(row, 24), :]
                data.append(block[:, :WIDE])
                for p in range(3):
                    piece = block[p * 8:(p + 1) * 8, WIDE:]
                    g = c * 3 + p
                    tail = tail + (pltpu.roll(piece, 16 * g, 1) if g else piece)
            data.append(jnp.concatenate([tail, jnp.zeros((8, WIDE - 128), F32)], axis=1))
            o[b] = jnp.concatenate(data, axis=0).astype(BF16)


def attend(me, need, q, k0, k1, v0, after, part):
    vmem = pl.BlockSpec(memory_space=pltpu.VMEM)
    smem = pl.BlockSpec(memory_space=pltpu.SMEM)
    whole = pl.BlockSpec(memory_space=pl.ANY)
    far = pl.BlockSpec(memory_space=pltpu.HBM)
    return pl.pallas_call(
        functools.partial(attend_kernel, part=part),
        out_shape=[jax.ShapeDtypeStruct((16, 56, WIDE), BF16)] * 4,
        in_specs=[smem] * 2 + [whole] * 4 + [far, whole, far, whole],
        out_specs=[vmem] * 4,
        scratch_shapes=[
            pltpu.SMEM((12,), jnp.int32),
            pltpu.SMEM((112,), jnp.int32),
            pltpu.VMEM((64, 48, WIDE), BF16),
            pltpu.VMEM((8, 256, WIDE), BF16),
            pltpu.VMEM((8, WIDE, 256), BF16),
            pltpu.VMEM((13, NH, 128, 256), BF16),
            pltpu.VMEM((4, NH, 80, 256), F32),
            pltpu.VMEM((4, NH, 256, 256), F32),
            pltpu.VMEM((4, NH, 256), F32),
            pltpu.VMEM((4, NH, 256), F32),
            pltpu.VMEM((3072, WIDE + 128), F32),
            pltpu.SemaphoreType.DMA((7,)),
        ],
        compiler_params=pltpu.CompilerParams(vmem_limit_bytes=24 * 2**20),
        cost_estimate=pl.CostEstimate(flops=10**10, bytes_accessed=2**23, transcendentals=2 * 10**7),
        name="attend",
    )(me, need, *q, pltpu.with_memory_space_constraint(k0, pltpu.HBM), k1, pltpu.with_memory_space_constraint(v0, pltpu.HBM), after)


def turn_kernel(me, v0, v1, k, out, parts, held, turned, sem):
    parts[0] = 0
    parts[1] = 1
    col = pl.multiple_of(me[1] * 512, 512)
    copies = [
        pltpu.make_async_copy(v.at[:, :, pl.ds(col, 512)], held.at[pl.ds(i * 4, 4)], sem.at[i])
        for i, v in enumerate((v0, v1))
    ]
    for copy in copies:
        copy.start()
    backs = []
    for j in range(8):
        if j % 4 == 0:
            copies[j // 4].wait()
        for at in range(0, 512, 128):
            turned[j, at:at + 128, :] = held[j, :, at:at + 128].T
        back = pltpu.make_async_copy(turned.at[j], out.at[j], sem.at[2 + j])
        back.start()
        backs.append(back)
    for back in backs:
        back.wait()


def turn_values(me, v0, v1, k):
    smem = pl.BlockSpec(memory_space=pltpu.SMEM)
    far = pl.BlockSpec(memory_space=pltpu.HBM)
    whole = pl.BlockSpec(memory_space=pl.ANY)
    return pl.pallas_call(
        turn_kernel,
        out_shape=[pltpu.HBM((8, 512, 256), BF16), jax.ShapeDtypeStruct((2,), jnp.int32)],
        in_specs=[smem, far, whole, whole],
        out_specs=[far, smem],
        scratch_shapes=[
            pltpu.VMEM((8, 256, 512), BF16),
            pltpu.VMEM((8, 512, 256), BF16),
            pltpu.SemaphoreType.DMA((10,)),
        ],
        cost_estimate=pl.CostEstimate(flops=10**6, bytes_accessed=2**23, transcendentals=0),
        compiler_params=pltpu.CompilerParams(vmem_limit_bytes=16 * 2**20),
        name="turn",
    )(me, pltpu.with_memory_space_constraint(v0, pltpu.HBM), v1, k)


def add_up(data, tails, spread):
    n = len(data)
    best = functools.reduce(jnp.maximum, tails)
    shares = [jnp.exp2(jnp.minimum(t - best, 0.0)) for t in tails]
    total = sum(f * (pltpu.roll(t, 128 - NH, 1) + pltpu.roll(t, 128 - 2 * NH, 1)) for f, t in zip(shares, tails))
    stack = jnp.concatenate(shares, axis=0)
    groups = data[0].shape[0] // 8
    stack = jnp.concatenate([stack] + [pltpu.roll(stack, 128 - 16 * g, 1) for g in range(1, groups)], axis=0)
    wide = jnp.dot(stack.astype(BF16), spread, preferred_element_type=F32)
    numer = []
    for g in range(groups):
        at = g * 8 * n
        numer.append(
            sum(wide[at + s * 8:at + s * 8 + 8] * d[g * 8:g * 8 + 8, :].astype(F32) for s, d in enumerate(data))
        )
    return numer, best, total


def make_spread():
    src = lax.broadcasted_iota(jnp.int32, (128, WIDE), 0)
    dst = lax.broadcasted_iota(jnp.int32, (128, WIDE), 1) // HD
    return src == dst


def add_blocks(held, spread, is_top):
    data, tails = [p[:48] for p in held], [p[48:56, :128].astype(F32) for p in held]
    numer, best, total = add_up(data, tails, spread)
    total = jnp.where(is_top, total, 0.0)
    hi = total.astype(BF16).astype(F32)
    tail = jnp.where(is_top, best, 0.0) + pltpu.roll(hi, NH, 1) + pltpu.roll(total - hi, 2 * NH, 1)
    return numer, jnp.concatenate([tail, jnp.zeros((8, WIDE - 128), F32)], axis=1)


def merge_kernel(p0, p1, p2, p3, after, out):
    spread = make_spread().astype(BF16)
    is_top = lax.broadcasted_iota(jnp.int32, (8, 128), 1) % 16 < NH
    for b in range(16):
        numer, tail = add_blocks([p[b] for p in (p0, p1, p2, p3)], spread, is_top)
        out[b] = jnp.concatenate(numer + [tail], axis=0).astype(BF16)


def merge(parts, after):
    vmem = pl.BlockSpec(memory_space=pltpu.VMEM)
    return pl.pallas_call(
        merge_kernel,
        out_shape=jax.ShapeDtypeStruct((16, 56, WIDE), BF16),
        in_specs=[vmem] * 4 + [pl.BlockSpec(memory_space=pl.ANY)],
        out_specs=vmem,
        compiler_params=pltpu.CompilerParams(vmem_limit_bytes=16 * 2**20),
        name="merge",
    )(*parts, after)


def settle_rows(held):
    spread = make_spread()
    numer, _, total = add_up([p[:48] for p in held], [p[48:56, :128].astype(F32) for p in held], spread.astype(BF16))
    totals = jnp.concatenate([total] + [pltpu.roll(total, 128 - 16 * g, 1) for g in range(1, 6)], axis=0)
    wide = jnp.dot(totals, spread.astype(F32), precision=lax.Precision.HIGHEST, preferred_element_type=F32)
    return jnp.concatenate(numer, axis=0) / wide


def hand_on_kernel(me, p0, p1, p2, p3, after, *outs):
    spread = make_spread().astype(BF16)
    is_top = lax.broadcasted_iota(jnp.int32, (8, 128), 1) % 16 < NH
    blocks = outs[0].shape[0]
    if blocks == 4:
        own = jnp.where(me[1] == 0, me[0], me[3])
    else:
        own = me[2]
    for r, out in enumerate(outs):
        at = lax.rem(own + 4 - r, 4)
        for z in range(blocks):
            held = [p[z * 4 + at] for p in (p0, p1, p2, p3)]
            numer, tail = add_blocks(held, spread, is_top)
            out[z] = jnp.concatenate(numer + [tail], axis=0).astype(BF16)


def hand_on(me, parts, after):
    vmem = pl.BlockSpec(memory_space=pltpu.VMEM)
    smem = pl.BlockSpec(memory_space=pltpu.SMEM)
    blocks = parts[0].shape[0] // 4
    return pl.pallas_call(
        hand_on_kernel,
        out_shape=[jax.ShapeDtypeStruct((blocks, 56, WIDE), BF16)] * 4,
        in_specs=[smem] + [vmem] * 4 + [pl.BlockSpec(memory_space=pl.ANY)],
        out_specs=[vmem] * 4,
        compiler_params=pltpu.CompilerParams(vmem_limit_bytes=16 * 2**20),
        name="hand_on",
    )(me, *parts, after)


def first_close_kernel(p0, p1, p2, p3, out):
    out[...] = settle_rows([p[0] for p in (p0, p1, p2, p3)])


def first_close(parts):
    vmem = pl.BlockSpec(memory_space=pltpu.VMEM)
    return pl.pallas_call(
        first_close_kernel,
        out_shape=jax.ShapeDtypeStruct((48, WIDE), F32),
        in_specs=[vmem] * 4,
        out_specs=vmem,
        name="first_close",
    )(*parts)


def close_kernel(me, ready, got, keep, give, both):
    both[:, :WIDE] = ready[...]
    both[:, WIDE:] = settle_rows([got[i] for i in range(16)])
    row = pl.multiple_of(me[1] * 24, 8)
    keep[...] = both[pl.ds(row, 24), :].astype(BF16)
    give[...] = both[pl.ds(24 - row, 24), :].astype(BF16)


def close(me, ready, got):
    vmem = pl.BlockSpec(memory_space=pltpu.VMEM)
    smem = pl.BlockSpec(memory_space=pltpu.SMEM)
    return pl.pallas_call(
        close_kernel,
        out_shape=[jax.ShapeDtypeStruct((24, 512), BF16)] * 2,
        in_specs=[smem, vmem, vmem],
        out_specs=[vmem] * 2,
        scratch_shapes=[pltpu.VMEM((48, 512), F32)],
        name="close",
    )(me, ready, got)


def swap(x):
    return lax.ppermute(x, "core", [(0, 1), (1, 0)])


def shift(x, axes, by):
    pairs = []
    for y, c, z, w in itertools.product(range(4), range(2), range(4), range(4)):
        to = {"y": y, "z": z, "x": w}
        to[axes[c]] = (to[axes[c]] + by) % 4
        pairs.append((((y * 2 + c) * 4 + z) * 4 + w, ((to["y"] * 2 + c) * 4 + to["z"]) * 4 + to["x"]))
    return lax.ppermute(x, ALL, pairs)


def ring(x, axes):
    return [x] + [shift(x, axes, by) for by in (1, 2, 3)]


def spot(y, c, z, x):
    return ((y * 2 + c) * 4 + z) * 4 + x


GROUPS = [[spot(a, 0, z, w) for z in range(4) for a in range(4)] for w in range(4)] + [
    [spot(w, 1, z, a) for z in range(4) for a in range(4)] for w in range(4)
]


def exchange(x):
    return lax.all_to_all(x, ALL, 0, 0, axis_index_groups=GROUPS)


def deliver(parts, axes):
    return [parts[0]] + [shift(parts[by], axes, -by) for by in (1, 2, 3)]


def body(queries, keys, values, frame_slot, covisible, counts, out_weight):
    core = lax.axis_index("core")
    device = lax.axis_index(ALL)
    partner = device + 16 - 32 * core
    own_col = core * 512

    theirs = swap(lax.dynamic_slice_in_dim(queries, 512 - own_col, 512, 1))
    me = jnp.stack([lax.axis_index(a) for a in ALL]).astype(jnp.int32)
    plane = exchange(spread_rows(me, queries, theirs))
    k_theirs, v_theirs = swap(keys), swap(values)
    v_turned, parts = turn_values(me, values, v_theirs, k_theirs)
    q_parts = [ring(lax.dynamic_index_in_dim(plane, parts[c], 1, False), "xy") for c in range(2)]

    four = jnp.arange(4, dtype=jnp.int32)
    slots = jnp.concatenate([device * 4 + four, partner * 4 + four])
    frame_ids = jnp.arange(frame_slot.shape[0], dtype=jnp.int32)
    local = jnp.sum(jnp.where(frame_slot[None, :] == slots[:, None], frame_ids[None, :], 0), axis=1)
    used = jnp.arange(covisible.shape[1], dtype=jnp.int32)[None, :] < counts[:, None]
    need = jnp.any((covisible[:, None, :] == local[None, :, None]) & used[:, None, :], axis=2)
    need = need.astype(jnp.int32)

    early = attend(me, need, q_parts[0], keys, k_theirs, v_turned, q_parts[0][0], 0)
    late = attend(me, need, q_parts[1], keys, k_theirs, v_turned, early[0], 1)
    early = deliver(hand_on(me, deliver(early, "xy"), late[0]), "yx")
    late = merge(deliver(late, "xy"), late[0])
    early = deliver(hand_on(me, early, late), "zz")
    late = exchange(late)
    keep, give = close(me, first_close(early), late)
    give = swap(give)
    first = core == 0
    rows = jnp.concatenate([jnp.where(first, keep, give), jnp.where(first, give, keep)], axis=1)
    return jnp.dot(rows, out_weight, preferred_element_type=F32).astype(BF16)


def solution(mesh):
    fine = Mesh(mesh.devices.reshape(4, 2, 4, 4), ALL)
    return jax.shard_map(
        body,
        mesh=fine,
        in_specs=(P(ALL, None), P(ALL, None, None), P(ALL, None, None), P(), P(), P(), P()),
        out_specs=P(ALL, None),
        check_vma=False,
    )
```

```python
import functools
import itertools

import jax
import jax.numpy as jnp
from jax import lax
from jax.experimental import pallas as pl
from jax.experimental.pallas import tpu as pltpu
from jax.sharding import Mesh, PartitionSpec as P

HD = 64
LOG2E = 1.4426950408889634
TOP_STEP = 16.0
NO_TOP = -32768.0
NH = 4
WIDE = NH * HD
ALL = ("y", "core", "z", "x")
F32 = jnp.float32
BF16 = jnp.bfloat16


def spread_kernel(me, mine, theirs, out):
    first = me[1] == 0
    mine, other = mine[...].astype(F32), theirs[...].astype(F32)
    pair = jnp.concatenate([jnp.where(first, mine, other), jnp.where(first, other, mine)], axis=0).astype(BF16)
    for i in range(16):
        for c in range(2):
            out[i, c] = pair[:, c * WIDE:(c + 1) * WIDE]


def spread_rows(me, mine, theirs):
    vmem = pl.BlockSpec(memory_space=pltpu.VMEM)
    smem = pl.BlockSpec(memory_space=pltpu.SMEM)
    return pl.pallas_call(
        spread_kernel,
        out_shape=jax.ShapeDtypeStruct((16, 2, 48, WIDE), BF16),
        in_specs=[smem, vmem, vmem],
        out_specs=vmem,
        compiler_params=pltpu.CompilerParams(vmem_limit_bytes=6 * 2**20),
        name="spread",
    )(me, mine, theirs)


def attend_kernel(
    me, need, *refs, part,
):
    qs, (k0, k1, v0, _), outs = refs[:4], refs[4:8], refs[8:12]
    cnt, plan, k, vt, qm, acc, sb, top, shrink, yb, sem = refs[12:]
    my_y, my_core, my_x = me[0], me[1], me[3]
    col = pl.multiple_of(my_core * 512 + part * WIDE, WIDE)
    copies = [
        pltpu.make_async_copy(src, dst, sem.at[i])
        for i, (src, dst) in enumerate(
            [
                (k0.at[:, :, pl.ds(col, WIDE)], k.at[pl.ds(0, 4)]),
                (k1.at[:, :, pl.ds(col, WIDE)], k.at[pl.ds(4, 4)]),
                (v0.at[:, pl.ds(part * WIDE, WIDE), :], vt),
            ]
        )
    ]
    for copy in copies:
        copy.start()
    scale = HD ** -0.5 * LOG2E
    ones = jnp.ones((16, 256), BF16)

    total, slot = jnp.int32(0), jnp.int32(0)
    for qi in range(12):
        begin = total
        for j in range(8):
            plan[total] = qi + 16 * j + 256 * slot
            total = total + need[qi, j]
        cnt[qi] = total - begin
        slot = (slot + jnp.minimum(total - begin, 1)) & 3
    for u in range(8):
        plan[total + u] = 12 + 256 * slot

    def frame_of(t):
        return plan[t] & 15

    def held_of(t):
        return (plan[t] >> 4) & 7

    def slot_of(t):
        return plan[t] >> 8

    def place(r3, z, a):
        y = jnp.where(my_core == 0, a, lax.rem(my_y + 4 - r3, 4))
        x = jnp.where(my_core == 0, lax.rem(my_x + 4 - r3, 4), a)
        return [pl.multiple_of(y * 768 + (c * 16 + z * 4 + x) * 24, 8) for c in range(2)]

    spots = [[place(r3, z, a) for z in range(4) for a in range(4)] for r3 in range(4)]
    for i, spot in enumerate(spots):
        for b, rows in enumerate(spot):
            block = qs[i][b].astype(F32)
            for c, row in enumerate(rows):
                yb[pl.ds(row, 24), :WIDE] = block[c * 24:(c + 1) * 24]

    def turn(qi, _):
        rows = pl.ds(pl.multiple_of(qi * 256, 256), 256)
        zero = jnp.zeros((64, 256), BF16)
        for hp in range(NH // 2):
            turned = yb[rows, hp * 128:(hp + 1) * 128].astype(BF16).T
            qm[qi, 2 * hp] = jnp.concatenate([turned[:64], zero], axis=0)
            qm[qi, 2 * hp + 1] = jnp.concatenate([zero, turned[64:]], axis=0)
        return 0

    def turns(u, _):
        for i in range(3):
            turn(u * 3 + i, 0)
        return 0

    lax.fori_loop(0, 4, turns, 0)
    def blank(qi, _):
        @pl.when(cnt[qi] == 0)
        def _():
            rows = pl.ds(pl.multiple_of(qi * 256, 256), 256)
            yb[rows, :WIDE] = jnp.zeros((256, WIDE), F32)
            lane = lax.broadcasted_iota(jnp.int32, (256, 128), 1)
            yb[rows, WIDE:] = jnp.where(lane < NH, NO_TOP, 0.0)

        return 0

    lax.fori_loop(0, 12, blank, 0)
    for copy in copies:
        copy.wait()
    acc[...] = jnp.zeros_like(acc)
    qm[12] = jnp.zeros((NH, 128, 256), BF16)

    def score(t, p, h):
        hp = h // 2
        keys = k[held_of(t + p), :, hp * 128:(hp + 1) * 128]
        s = jnp.dot(keys, qm[frame_of(t + p), h], preferred_element_type=F32) * scale
        sb[p, h] = s
        return jnp.max(s, axis=0, keepdims=True)

    def settle(t, p, highs, old):
        first = frame_of(t + p) != frame_of(jnp.maximum(t + p - 1, 0))
        old = jnp.where(first, NO_TOP, old)
        high = jnp.concatenate(highs, axis=0)
        new = jnp.maximum(old, jnp.ceil(high * (1.0 / TOP_STEP)) * TOP_STEP)
        top[p] = new
        shrink[p] = jnp.exp2(old - new)
        return new

    def weigh(t, p, h, tops, shrinks):
        weights = jnp.exp2(sb[p, h] - tops[h:h + 1]).astype(BF16)
        vals = jnp.concatenate([vt[held_of(t + p), h * 64:(h + 1) * 64, :], ones], axis=0)
        part = jnp.dot(vals, weights, preferred_element_type=F32)
        at = slot_of(t + p)
        acc[at, h] = acc[at, h] * shrinks[h:h + 1] + part

    def finish(t, p, tops):
        qi = frame_of(t + p)

        @pl.when((qi < 12) & (frame_of(t + p + 1) != qi))
        def _():
            at = slot_of(t + p)
            rows = pl.ds(pl.multiple_of(qi * 256, 256), 256)
            totals = jnp.concatenate([acc[at, h, 64:65, :] for h in range(NH)], axis=0)
            hi = totals.astype(BF16).astype(F32)
            extra = [tops, hi, totals - hi, jnp.zeros((128 - 3 * NH, 256), F32)]
            for hp in range(NH // 2):
                both = jnp.concatenate([acc[at, 2 * hp, :64, :], acc[at, 2 * hp + 1, :64, :]], axis=0)
                yb[rows, hp * 128:(hp + 1) * 128] = both.astype(BF16).T.astype(F32)
            yb[rows, WIDE:] = jnp.concatenate(extra, axis=0).astype(BF16).T.astype(F32)

    old = jnp.full((NH, 256), NO_TOP, F32)
    for p in range(4):
        old = settle(0, p, [score(0, p, h) for h in range(NH)], old)

    def two(u, _):
        t = u * 4
        tops, shrinks = [top[p] for p in range(4)], [shrink[p] for p in range(4)]
        highs = [[] for p in range(4)]
        for p in range(4):
            for h in range(NH):
                weigh(t, p, h, tops[p], shrinks[p])
                highs[p].append(score(t + 4, p, h))
        old = tops[3]
        for p in range(4):
            old = settle(t + 4, p, highs[p], old)
        for p in range(4):
            finish(t, p, tops[p])
        return 0

    lax.fori_loop(0, (total + 3) // 4, two, 0)

    for o, spot in zip(outs, spots):
        for b, rows in enumerate(spot):
            data, tail = [], jnp.zeros((8, 128), F32)
            for c, row in enumerate(rows):
                block = yb[pl.ds(row, 24), :]
                data.append(block[:, :WIDE])
                for p in range(3):
                    piece = block[p * 8:(p + 1) * 8, WIDE:]
                    g = c * 3 + p
                    tail = tail + (pltpu.roll(piece, 16 * g, 1) if g else piece)
            data.append(jnp.concatenate([tail, jnp.zeros((8, WIDE - 128), F32)], axis=1))
            o[b] = jnp.concatenate(data, axis=0).astype(BF16)


def attend(me, need, q, k0, k1, v0, after, part):
    vmem = pl.BlockSpec(memory_space=pltpu.VMEM)
    smem = pl.BlockSpec(memory_space=pltpu.SMEM)
    whole = pl.BlockSpec(memory_space=pl.ANY)
    far = pl.BlockSpec(memory_space=pltpu.HBM)
    return pl.pallas_call(
        functools.partial(attend_kernel, part=part),
        out_shape=[jax.ShapeDtypeStruct((16, 56, WIDE), BF16)] * 4,
        in_specs=[smem] * 2 + [vmem] * 4 + [far, whole, far, whole],
        out_specs=[vmem] * 4,
        scratch_shapes=[
            pltpu.SMEM((12,), jnp.int32),
            pltpu.SMEM((112,), jnp.int32),
            pltpu.VMEM((8, 256, WIDE), BF16),
            pltpu.VMEM((8, WIDE, 256), BF16),
            pltpu.VMEM((13, NH, 128, 256), BF16),
            pltpu.VMEM((4, NH, 80, 256), F32),
            pltpu.VMEM((4, NH, 256, 256), F32),
            pltpu.VMEM((4, NH, 256), F32),
            pltpu.VMEM((4, NH, 256), F32),
            pltpu.VMEM((3072, WIDE + 128), F32),
            pltpu.SemaphoreType.DMA((3,)),
        ],
        compiler_params=pltpu.CompilerParams(vmem_limit_bytes=24 * 2**20),
        cost_estimate=pl.CostEstimate(flops=10**10, bytes_accessed=2**23, transcendentals=2 * 10**7),
        name="attend",
    )(me, need, *q, pltpu.with_memory_space_constraint(k0, pltpu.HBM), k1, pltpu.with_memory_space_constraint(v0, pltpu.HBM), after)


def turn_kernel(me, v0, v1, k, out, parts, held, turned, sem):
    parts[0] = 0
    parts[1] = 1
    col = pl.multiple_of(me[1] * 512, 512)
    copies = [
        pltpu.make_async_copy(v.at[:, :, pl.ds(col, 512)], held.at[pl.ds(i * 4, 4)], sem.at[i])
        for i, v in enumerate((v0, v1))
    ]
    for copy in copies:
        copy.start()
    backs = []
    for j in range(8):
        if j % 4 == 0:
            copies[j // 4].wait()
        for at in range(0, 512, 128):
            turned[j, at:at + 128, :] = held[j, :, at:at + 128].T
        back = pltpu.make_async_copy(turned.at[j], out.at[j], sem.at[2 + j])
        back.start()
        backs.append(back)
    for back in backs:
        back.wait()


def turn_values(me, v0, v1, k):
    smem = pl.BlockSpec(memory_space=pltpu.SMEM)
    far = pl.BlockSpec(memory_space=pltpu.HBM)
    whole = pl.BlockSpec(memory_space=pl.ANY)
    return pl.pallas_call(
        turn_kernel,
        out_shape=[pltpu.HBM((8, 512, 256), BF16), jax.ShapeDtypeStruct((2,), jnp.int32)],
        in_specs=[smem, far, whole, whole],
        out_specs=[far, smem],
        scratch_shapes=[
            pltpu.VMEM((8, 256, 512), BF16),
            pltpu.VMEM((8, 512, 256), BF16),
            pltpu.SemaphoreType.DMA((10,)),
        ],
        cost_estimate=pl.CostEstimate(flops=10**6, bytes_accessed=2**23, transcendentals=0),
        compiler_params=pltpu.CompilerParams(vmem_limit_bytes=16 * 2**20),
        name="turn",
    )(me, pltpu.with_memory_space_constraint(v0, pltpu.HBM), v1, k)


def add_up(data, tails, spread):
    n = len(data)
    best = functools.reduce(jnp.maximum, tails)
    shares = [jnp.exp2(jnp.minimum(t - best, 0.0)) for t in tails]
    total = sum(f * (pltpu.roll(t, 128 - NH, 1) + pltpu.roll(t, 128 - 2 * NH, 1)) for f, t in zip(shares, tails))
    stack = jnp.concatenate(shares, axis=0)
    groups = data[0].shape[0] // 8
    stack = jnp.concatenate([stack] + [pltpu.roll(stack, 128 - 16 * g, 1) for g in range(1, groups)], axis=0)
    wide = jnp.dot(stack.astype(BF16), spread, preferred_element_type=F32)
    numer = []
    for g in range(groups):
        at = g * 8 * n
        numer.append(
            sum(wide[at + s * 8:at + s * 8 + 8] * d[g * 8:g * 8 + 8, :].astype(F32) for s, d in enumerate(data))
        )
    return numer, best, total


def make_spread():
    src = lax.broadcasted_iota(jnp.int32, (128, WIDE), 0)
    dst = lax.broadcasted_iota(jnp.int32, (128, WIDE), 1) // HD
    return src == dst


def add_blocks(held, spread, is_top):
    data, tails = [p[:48] for p in held], [p[48:56, :128].astype(F32) for p in held]
    numer, best, total = add_up(data, tails, spread)
    total = jnp.where(is_top, total, 0.0)
    hi = total.astype(BF16).astype(F32)
    tail = jnp.where(is_top, best, 0.0) + pltpu.roll(hi, NH, 1) + pltpu.roll(total - hi, 2 * NH, 1)
    return numer, jnp.concatenate([tail, jnp.zeros((8, WIDE - 128), F32)], axis=1)


def merge_kernel(p0, p1, p2, p3, after, out):
    spread = make_spread().astype(BF16)
    is_top = lax.broadcasted_iota(jnp.int32, (8, 128), 1) % 16 < NH
    for b in range(16):
        numer, tail = add_blocks([p[b] for p in (p0, p1, p2, p3)], spread, is_top)
        out[b] = jnp.concatenate(numer + [tail], axis=0).astype(BF16)


def merge(parts, after):
    vmem = pl.BlockSpec(memory_space=pltpu.VMEM)
    return pl.pallas_call(
        merge_kernel,
        out_shape=jax.ShapeDtypeStruct((16, 56, WIDE), BF16),
        in_specs=[vmem] * 4 + [pl.BlockSpec(memory_space=pl.ANY)],
        out_specs=vmem,
        compiler_params=pltpu.CompilerParams(vmem_limit_bytes=10 * 2**20),
        name="merge",
    )(*parts, after)


def settle_rows(got):
    spread = make_spread()
    held = [got[i] for i in range(16)]
    numer, _, total = add_up([p[:48] for p in held], [p[48:56, :128].astype(F32) for p in held], spread.astype(BF16))
    totals = jnp.concatenate([total] + [pltpu.roll(total, 128 - 16 * g, 1) for g in range(1, 6)], axis=0)
    wide = jnp.dot(totals, spread.astype(F32), precision=lax.Precision.HIGHEST, preferred_element_type=F32)
    return jnp.concatenate(numer, axis=0) / wide


def first_close_kernel(got, out):
    out[...] = settle_rows(got)


def first_close(got):
    vmem = pl.BlockSpec(memory_space=pltpu.VMEM)
    return pl.pallas_call(
        first_close_kernel,
        out_shape=jax.ShapeDtypeStruct((48, WIDE), F32),
        in_specs=[vmem],
        out_specs=vmem,
        compiler_params=pltpu.CompilerParams(vmem_limit_bytes=6 * 2**20),
        name="first_close",
    )(got)


def close_kernel(me, ready, got, keep, give, both):
    both[:, :WIDE] = ready[...]
    both[:, WIDE:] = settle_rows(got)
    row = pl.multiple_of(me[1] * 24, 8)
    keep[...] = both[pl.ds(row, 24), :].astype(BF16)
    give[...] = both[pl.ds(24 - row, 24), :].astype(BF16)


def close(me, ready, got):
    vmem = pl.BlockSpec(memory_space=pltpu.VMEM)
    smem = pl.BlockSpec(memory_space=pltpu.SMEM)
    return pl.pallas_call(
        close_kernel,
        out_shape=[jax.ShapeDtypeStruct((24, 512), BF16)] * 2,
        in_specs=[smem, vmem, vmem],
        out_specs=[vmem] * 2,
        scratch_shapes=[pltpu.VMEM((48, 512), F32)],
        compiler_params=pltpu.CompilerParams(vmem_limit_bytes=6 * 2**20),
        name="close",
    )(me, ready, got)


def swap(x):
    return lax.ppermute(x, "core", [(0, 1), (1, 0)])


def shift(x, axes, by):
    pairs = []
    for y, c, z, w in itertools.product(range(4), range(2), range(4), range(4)):
        to = {"y": y, "z": z, "x": w}
        to[axes[c]] = (to[axes[c]] + by) % 4
        pairs.append((((y * 2 + c) * 4 + z) * 4 + w, ((to["y"] * 2 + c) * 4 + to["z"]) * 4 + to["x"]))
    return lax.ppermute(x, ALL, pairs)


def ring(x, axes):
    return [x] + [shift(x, axes, by) for by in (1, 2, 3)]


def spot(y, c, z, x):
    return ((y * 2 + c) * 4 + z) * 4 + x


GROUPS = [[spot(a, 0, z, w) for z in range(4) for a in range(4)] for w in range(4)] + [
    [spot(w, 1, z, a) for z in range(4) for a in range(4)] for w in range(4)
]


def exchange(x):
    return lax.all_to_all(x, ALL, 0, 0, axis_index_groups=GROUPS)


def deliver(parts, axes):
    return [parts[0]] + [shift(parts[by], axes, -by) for by in (1, 2, 3)]


def body(queries, keys, values, frame_slot, covisible, counts, out_weight):
    core = lax.axis_index("core")
    device = lax.axis_index(ALL)
    partner = device + 16 - 32 * core
    own_col = core * 512

    theirs = swap(lax.dynamic_slice_in_dim(queries, 512 - own_col, 512, 1))
    me = jnp.stack([lax.axis_index(a) for a in ALL]).astype(jnp.int32)
    mine = lax.dynamic_slice_in_dim(queries, own_col, 512, 1)
    plane = exchange(spread_rows(me, mine, theirs))
    k_theirs, v_theirs = swap(keys), swap(values)
    v_turned, parts = turn_values(me, values, v_theirs, k_theirs)
    q_parts = [ring(lax.dynamic_index_in_dim(plane, parts[c], 1, False), "xy") for c in range(2)]

    four = jnp.arange(4, dtype=jnp.int32)
    slots = jnp.concatenate([device * 4 + four, partner * 4 + four])
    frame_ids = jnp.arange(frame_slot.shape[0], dtype=jnp.int32)
    local = jnp.sum(jnp.where(frame_slot[None, :] == slots[:, None], frame_ids[None, :], 0), axis=1)
    used = jnp.arange(covisible.shape[1], dtype=jnp.int32)[None, :] < counts[:, None]
    need = jnp.any((covisible[:, None, :] == local[None, :, None]) & used[:, None, :], axis=2)
    need = need.astype(jnp.int32)

    early = attend(me, need, q_parts[0], keys, k_theirs, v_turned, q_parts[0][0], 0)
    late = attend(me, need, q_parts[1], keys, k_theirs, v_turned, early[0], 1)
    early = exchange(merge(deliver(early, "xy"), late[0]))
    late = exchange(merge(deliver(late, "xy"), late[0]))
    keep, give = close(me, first_close(early), late)
    give = swap(give)
    first = core == 0
    rows = jnp.concatenate([jnp.where(first, keep, give), jnp.where(first, give, keep)], axis=1)
    return jnp.dot(rows, out_weight, preferred_element_type=F32).astype(BF16)


def solution(mesh):
    fine = Mesh(mesh.devices.reshape(4, 2, 4, 4), ALL)
    return jax.shard_map(
        body,
        mesh=fine,
        in_specs=(P(ALL, None), P(ALL, None, None), P(ALL, None, None), P(), P(), P(), P()),
        out_specs=P(ALL, None),
        check_vma=False,
    )
```

```python
import functools
import itertools

import jax
import jax.numpy as jnp
from jax import lax
from jax.experimental import pallas as pl
from jax.experimental.pallas import tpu as pltpu
from jax.sharding import Mesh, PartitionSpec as P

HD = 64
LOG2E = 1.4426950408889634
TOP_STEP = 16.0
NO_TOP = -32768.0
NH = 4
WIDE = NH * HD
ALL = ("y", "core", "z", "x")
F32 = jnp.float32
BF16 = jnp.bfloat16


def spread_kernel(me, mine, theirs, out):
    first = me[1] == 0
    mine, other = mine[...].astype(F32), theirs[...].astype(F32)
    pair = jnp.concatenate([jnp.where(first, mine, other), jnp.where(first, other, mine)], axis=0).astype(BF16)
    for i in range(16):
        for c in range(2):
            out[i, c] = pair[:, c * WIDE:(c + 1) * WIDE]


def spread_rows(me, mine, theirs):
    vmem = pl.BlockSpec(memory_space=pltpu.VMEM)
    smem = pl.BlockSpec(memory_space=pltpu.SMEM)
    return pl.pallas_call(
        spread_kernel,
        out_shape=jax.ShapeDtypeStruct((16, 2, 48, WIDE), BF16),
        in_specs=[smem, vmem, vmem],
        out_specs=vmem,
        compiler_params=pltpu.CompilerParams(vmem_limit_bytes=6 * 2**20),
        name="spread",
    )(me, mine, theirs)


def attend_kernel(
    me, need, *refs, part,
):
    qs, (k0, k1, v0, _), outs = refs[:4], refs[4:8], refs[8:12]
    cnt, plan, k, vt, qm, acc, sb, top, shrink, yb, sem = refs[12:]
    my_y, my_core, my_x = me[0], me[1], me[3]
    col = pl.multiple_of(my_core * 512 + part * WIDE, WIDE)
    copies = [
        pltpu.make_async_copy(src, dst, sem.at[i])
        for i, (src, dst) in enumerate(
            [
                (k0.at[:, :, pl.ds(col, WIDE)], k.at[pl.ds(0, 4)]),
                (k1.at[:, :, pl.ds(col, WIDE)], k.at[pl.ds(4, 4)]),
                (v0.at[:, pl.ds(part * WIDE, WIDE), :], vt),
            ]
        )
    ]
    for copy in copies:
        copy.start()
    scale = HD ** -0.5 * LOG2E
    ones = jnp.ones((16, 256), BF16)

    total, slot = jnp.int32(0), jnp.int32(0)
    for qi in range(12):
        begin = total
        for j in range(8):
            plan[total] = qi + 16 * j + 256 * slot
            total = total + need[qi, j]
        cnt[qi] = total - begin
        slot = (slot + jnp.minimum(total - begin, 1)) & 3
    for u in range(8):
        plan[total + u] = 12 + 256 * slot

    def frame_of(t):
        return plan[t] & 15

    def held_of(t):
        return (plan[t] >> 4) & 7

    def slot_of(t):
        return plan[t] >> 8

    def place(r3, z, a):
        y = jnp.where(my_core == 0, a, lax.rem(my_y + 4 - r3, 4))
        x = jnp.where(my_core == 0, lax.rem(my_x + 4 - r3, 4), a)
        return [pl.multiple_of(y * 768 + (c * 16 + z * 4 + x) * 24, 8) for c in range(2)]

    spots = [[place(r3, z, a) for z in range(4) for a in range(4)] for r3 in range(4)]
    for i, spot in enumerate(spots):
        for b, rows in enumerate(spot):
            block = qs[i][b].astype(F32)
            for c, row in enumerate(rows):
                yb[pl.ds(row, 24), :WIDE] = block[c * 24:(c + 1) * 24]

    def turn(qi, _):
        rows = pl.ds(pl.multiple_of(qi * 256, 256), 256)
        zero = jnp.zeros((64, 256), BF16)
        for hp in range(NH // 2):
            turned = yb[rows, hp * 128:(hp + 1) * 128].astype(BF16).T
            qm[qi, 2 * hp] = jnp.concatenate([turned[:64], zero], axis=0)
            qm[qi, 2 * hp + 1] = jnp.concatenate([zero, turned[64:]], axis=0)
        return 0

    def turns(u, _):
        for i in range(3):
            turn(u * 3 + i, 0)
        return 0

    lax.fori_loop(0, 4, turns, 0)
    def blank(qi, _):
        @pl.when(cnt[qi] == 0)
        def _():
            rows = pl.ds(pl.multiple_of(qi * 256, 256), 256)
            yb[rows, :WIDE] = jnp.zeros((256, WIDE), F32)
            lane = lax.broadcasted_iota(jnp.int32, (256, 128), 1)
            yb[rows, WIDE:] = jnp.where(lane < NH, NO_TOP, 0.0)

        return 0

    lax.fori_loop(0, 12, blank, 0)
    for copy in copies:
        copy.wait()
    acc[...] = jnp.zeros_like(acc)
    qm[12] = jnp.zeros((NH, 128, 256), BF16)

    def score(t, p, h):
        hp = h // 2
        keys = k[held_of(t + p), :, hp * 128:(hp + 1) * 128]
        s = jnp.dot(keys, qm[frame_of(t + p), h], preferred_element_type=F32) * scale
        sb[p, h] = s
        return jnp.max(s, axis=0, keepdims=True)

    def settle(t, p, highs, old):
        first = frame_of(t + p) != frame_of(jnp.maximum(t + p - 1, 0))
        old = jnp.where(first, NO_TOP, old)
        high = jnp.concatenate(highs, axis=0)
        new = jnp.maximum(old, jnp.ceil(high * (1.0 / TOP_STEP)) * TOP_STEP)
        top[p] = new
        shrink[p] = jnp.exp2(old - new)
        return new

    def weigh(t, p, h, tops, shrinks):
        weights = jnp.exp2(sb[p, h] - tops[h:h + 1]).astype(BF16)
        vals = jnp.concatenate([vt[held_of(t + p), h * 64:(h + 1) * 64, :], ones], axis=0)
        part = jnp.dot(vals, weights, preferred_element_type=F32)
        at = slot_of(t + p)
        acc[at, h] = acc[at, h] * shrinks[h:h + 1] + part

    def finish(t, p, tops):
        qi = frame_of(t + p)

        @pl.when((qi < 12) & (frame_of(t + p + 1) != qi))
        def _():
            at = slot_of(t + p)
            rows = pl.ds(pl.multiple_of(qi * 256, 256), 256)
            totals = jnp.concatenate([acc[at, h, 64:65, :] for h in range(NH)], axis=0)
            hi = totals.astype(BF16).astype(F32)
            extra = [tops, hi, totals - hi, jnp.zeros((128 - 3 * NH, 256), F32)]
            for hp in range(NH // 2):
                both = jnp.concatenate([acc[at, 2 * hp, :64, :], acc[at, 2 * hp + 1, :64, :]], axis=0)
                yb[rows, hp * 128:(hp + 1) * 128] = both.astype(BF16).T.astype(F32)
            yb[rows, WIDE:] = jnp.concatenate(extra, axis=0).astype(BF16).T.astype(F32)

    old = jnp.full((NH, 256), NO_TOP, F32)
    for p in range(4):
        old = settle(0, p, [score(0, p, h) for h in range(NH)], old)

    def two(u, _):
        t = u * 4
        tops, shrinks = [top[p] for p in range(4)], [shrink[p] for p in range(4)]
        highs = [[] for p in range(4)]
        for p in range(4):
            for h in range(NH):
                weigh(t, p, h, tops[p], shrinks[p])
                highs[p].append(score(t + 4, p, h))
        old = tops[3]
        for p in range(4):
            old = settle(t + 4, p, highs[p], old)
        for p in range(4):
            finish(t, p, tops[p])
        return 0

    lax.fori_loop(0, (total + 3) // 4, two, 0)

    for o, spot in zip(outs, spots):
        for b, rows in enumerate(spot):
            data, tail = [], jnp.zeros((8, 128), F32)
            for c, row in enumerate(rows):
                block = yb[pl.ds(row, 24), :]
                data.append(block[:, :WIDE])
                for p in range(3):
                    piece = block[p * 8:(p + 1) * 8, WIDE:]
                    g = c * 3 + p
                    tail = tail + (pltpu.roll(piece, 16 * g, 1) if g else piece)
            data.append(jnp.concatenate([tail, jnp.zeros((8, WIDE - 128), F32)], axis=1))
            o[b] = jnp.concatenate(data, axis=0).astype(BF16)


def attend(me, need, q, k0, k1, v0, after, part):
    vmem = pl.BlockSpec(memory_space=pltpu.VMEM)
    smem = pl.BlockSpec(memory_space=pltpu.SMEM)
    whole = pl.BlockSpec(memory_space=pl.ANY)
    far = pl.BlockSpec(memory_space=pltpu.HBM)
    return pl.pallas_call(
        functools.partial(attend_kernel, part=part),
        out_shape=[jax.ShapeDtypeStruct((16, 56, WIDE), BF16)] * 4,
        in_specs=[smem] * 2 + [vmem] * 4 + [far, whole, far, whole],
        out_specs=[vmem] * 4,
        scratch_shapes=[
            pltpu.SMEM((12,), jnp.int32),
            pltpu.SMEM((112,), jnp.int32),
            pltpu.VMEM((8, 256, WIDE), BF16),
            pltpu.VMEM((8, WIDE, 256), BF16),
            pltpu.VMEM((13, NH, 128, 256), BF16),
            pltpu.VMEM((4, NH, 80, 256), F32),
            pltpu.VMEM((4, NH, 256, 256), F32),
            pltpu.VMEM((4, NH, 256), F32),
            pltpu.VMEM((4, NH, 256), F32),
            pltpu.VMEM((3072, WIDE + 128), F32),
            pltpu.SemaphoreType.DMA((3,)),
        ],
        compiler_params=pltpu.CompilerParams(vmem_limit_bytes=24 * 2**20),
        cost_estimate=pl.CostEstimate(flops=10**10, bytes_accessed=2**23, transcendentals=2 * 10**7),
        name="attend",
    )(me, need, *q, pltpu.with_memory_space_constraint(k0, pltpu.HBM), k1, pltpu.with_memory_space_constraint(v0, pltpu.HBM), after)


def turn_kernel(me, v0, v1, k, out, parts, held, turned, sem):
    parts[0] = 0
    parts[1] = 1
    col = pl.multiple_of(me[1] * 512, 512)
    copies = [
        pltpu.make_async_copy(v.at[:, :, pl.ds(col, 512)], held.at[pl.ds(i * 4, 4)], sem.at[i])
        for i, v in enumerate((v0, v1))
    ]
    for copy in copies:
        copy.start()
    backs = []
    for j in range(8):
        if j % 4 == 0:
            copies[j // 4].wait()
        for at in range(0, 512, 128):
            turned[j, at:at + 128, :] = held[j, :, at:at + 128].T
        back = pltpu.make_async_copy(turned.at[j], out.at[j], sem.at[2 + j])
        back.start()
        backs.append(back)
    for back in backs:
        back.wait()


def turn_values(me, v0, v1, k):
    smem = pl.BlockSpec(memory_space=pltpu.SMEM)
    far = pl.BlockSpec(memory_space=pltpu.HBM)
    whole = pl.BlockSpec(memory_space=pl.ANY)
    return pl.pallas_call(
        turn_kernel,
        out_shape=[pltpu.HBM((8, 512, 256), BF16), jax.ShapeDtypeStruct((2,), jnp.int32)],
        in_specs=[smem, far, whole, whole],
        out_specs=[far, smem],
        scratch_shapes=[
            pltpu.VMEM((8, 256, 512), BF16),
            pltpu.VMEM((8, 512, 256), BF16),
            pltpu.SemaphoreType.DMA((10,)),
        ],
        cost_estimate=pl.CostEstimate(flops=10**6, bytes_accessed=2**23, transcendentals=0),
        compiler_params=pltpu.CompilerParams(vmem_limit_bytes=16 * 2**20),
        name="turn",
    )(me, pltpu.with_memory_space_constraint(v0, pltpu.HBM), v1, k)


def add_up(data, tails, spread):
    n = len(data)
    best = functools.reduce(jnp.maximum, tails)
    shares = [jnp.exp2(jnp.minimum(t - best, 0.0)) for t in tails]
    total = sum(f * (pltpu.roll(t, 128 - NH, 1) + pltpu.roll(t, 128 - 2 * NH, 1)) for f, t in zip(shares, tails))
    stack = jnp.concatenate(shares, axis=0)
    groups = data[0].shape[0] // 8
    stack = jnp.concatenate([stack] + [pltpu.roll(stack, 128 - 16 * g, 1) for g in range(1, groups)], axis=0)
    wide = jnp.dot(stack.astype(BF16), spread, preferred_element_type=F32)
    numer = []
    for g in range(groups):
        at = g * 8 * n
        numer.append(
            sum(wide[at + s * 8:at + s * 8 + 8] * d[g * 8:g * 8 + 8, :].astype(F32) for s, d in enumerate(data))
        )
    return numer, best, total


def make_spread():
    src = lax.broadcasted_iota(jnp.int32, (128, WIDE), 0)
    dst = lax.broadcasted_iota(jnp.int32, (128, WIDE), 1) // HD
    return src == dst


def add_blocks(held, spread, is_top):
    data, tails = [p[:48] for p in held], [p[48:56, :128].astype(F32) for p in held]
    numer, best, total = add_up(data, tails, spread)
    total = jnp.where(is_top, total, 0.0)
    hi = total.astype(BF16).astype(F32)
    tail = jnp.where(is_top, best, 0.0) + pltpu.roll(hi, NH, 1) + pltpu.roll(total - hi, 2 * NH, 1)
    return numer, jnp.concatenate([tail, jnp.zeros((8, WIDE - 128), F32)], axis=1)


def merge_kernel(p0, p1, p2, p3, after, out):
    spread = make_spread().astype(BF16)
    is_top = lax.broadcasted_iota(jnp.int32, (8, 128), 1) % 16 < NH
    for b in range(16):
        numer, tail = add_blocks([p[b] for p in (p0, p1, p2, p3)], spread, is_top)
        out[b] = jnp.concatenate(numer + [tail], axis=0).astype(BF16)


def merge(parts, after):
    vmem = pl.BlockSpec(memory_space=pltpu.VMEM)
    return pl.pallas_call(
        merge_kernel,
        out_shape=jax.ShapeDtypeStruct((16, 56, WIDE), BF16),
        in_specs=[vmem] * 4 + [pl.BlockSpec(memory_space=pl.ANY)],
        out_specs=vmem,
        compiler_params=pltpu.CompilerParams(vmem_limit_bytes=10 * 2**20),
        name="merge",
    )(*parts, after)


def settle_rows(got, c):
    spread = make_spread()
    held = [got[i, c] for i in range(16)]
    numer, _, total = add_up([p[:48] for p in held], [p[48:56, :128].astype(F32) for p in held], spread.astype(BF16))
    totals = jnp.concatenate([total] + [pltpu.roll(total, 128 - 16 * g, 1) for g in range(1, 6)], axis=0)
    wide = jnp.dot(totals, spread.astype(F32), precision=lax.Precision.HIGHEST, preferred_element_type=F32)
    return jnp.concatenate(numer, axis=0) / wide


def join_kernel(p0, p1, p2, p3, ready, out):
    spread = make_spread().astype(BF16)
    is_top = lax.broadcasted_iota(jnp.int32, (8, 128), 1) % 16 < NH
    for b in range(16):
        numer, tail = add_blocks([p[b] for p in (p0, p1, p2, p3)], spread, is_top)
        out[b, 0] = ready[b]
        out[b, 1] = jnp.concatenate(numer + [tail], axis=0).astype(BF16)


def join(parts, ready):
    vmem = pl.BlockSpec(memory_space=pltpu.VMEM)
    return pl.pallas_call(
        join_kernel,
        out_shape=jax.ShapeDtypeStruct((16, 2, 56, WIDE), BF16),
        in_specs=[vmem] * 5,
        out_specs=vmem,
        compiler_params=pltpu.CompilerParams(vmem_limit_bytes=10 * 2**20),
        name="join",
    )(*parts, ready)


def close_kernel(me, got, keep, give, both):
    for c in range(2):
        both[:, c * WIDE:(c + 1) * WIDE] = settle_rows(got, c)
    row = pl.multiple_of(me[1] * 24, 8)
    keep[...] = both[pl.ds(row, 24), :].astype(BF16)
    give[...] = both[pl.ds(24 - row, 24), :].astype(BF16)


def close(me, got):
    vmem = pl.BlockSpec(memory_space=pltpu.VMEM)
    smem = pl.BlockSpec(memory_space=pltpu.SMEM)
    return pl.pallas_call(
        close_kernel,
        out_shape=[jax.ShapeDtypeStruct((24, 512), BF16)] * 2,
        in_specs=[smem, vmem],
        out_specs=[vmem] * 2,
        scratch_shapes=[pltpu.VMEM((48, 512), F32)],
        compiler_params=pltpu.CompilerParams(vmem_limit_bytes=6 * 2**20),
        name="close",
    )(me, got)


def swap(x):
    return lax.ppermute(x, "core", [(0, 1), (1, 0)])


def shift(x, axes, by):
    pairs = []
    for y, c, z, w in itertools.product(range(4), range(2), range(4), range(4)):
        to = {"y": y, "z": z, "x": w}
        to[axes[c]] = (to[axes[c]] + by) % 4
        pairs.append((((y * 2 + c) * 4 + z) * 4 + w, ((to["y"] * 2 + c) * 4 + to["z"]) * 4 + to["x"]))
    return lax.ppermute(x, ALL, pairs)


def ring(x, axes):
    far = shift(x, axes, 2)
    return [x, shift(x, axes, 1), far, shift(x, axes, 3)]


def spot(y, c, z, x):
    return ((y * 2 + c) * 4 + z) * 4 + x


GROUPS = [[spot(a, 0, z, w) for z in range(4) for a in range(4)] for w in range(4)] + [
    [spot(w, 1, z, a) for z in range(4) for a in range(4)] for w in range(4)
]


def exchange(x):
    return lax.all_to_all(x, ALL, 0, 0, axis_index_groups=GROUPS)


def deliver(parts, axes):
    far = shift(parts[2], axes, -2)
    return [parts[0], shift(parts[1], axes, -1), far, shift(parts[3], axes, -3)]


def body(queries, keys, values, frame_slot, covisible, counts, out_weight):
    core = lax.axis_index("core")
    device = lax.axis_index(ALL)
    partner = device + 16 - 32 * core
    own_col = core * 512

    theirs = swap(lax.dynamic_slice_in_dim(queries, 512 - own_col, 512, 1))
    me = jnp.stack([lax.axis_index(a) for a in ALL]).astype(jnp.int32)
    mine = lax.dynamic_slice_in_dim(queries, own_col, 512, 1)
    plane = exchange(spread_rows(me, mine, theirs))
    k_theirs, v_theirs = swap(keys), swap(values)
    v_turned, parts = turn_values(me, values, v_theirs, k_theirs)
    q_parts = [ring(lax.dynamic_index_in_dim(plane, parts[c], 1, False), "xy") for c in range(2)]

    four = jnp.arange(4, dtype=jnp.int32)
    slots = jnp.concatenate([device * 4 + four, partner * 4 + four])
    frame_ids = jnp.arange(frame_slot.shape[0], dtype=jnp.int32)
    local = jnp.sum(jnp.where(frame_slot[None, :] == slots[:, None], frame_ids[None, :], 0), axis=1)
    used = jnp.arange(covisible.shape[1], dtype=jnp.int32)[None, :] < counts[:, None]
    need = jnp.any((covisible[:, None, :] == local[None, :, None]) & used[:, None, :], axis=2)
    need = need.astype(jnp.int32)

    early = attend(me, need, q_parts[0], keys, k_theirs, v_turned, q_parts[0][0], 0)
    late = attend(me, need, q_parts[1], keys, k_theirs, v_turned, early[0], 1)
    early = merge(deliver(early, "xy"), late[0])
    keep, give = close(me, exchange(join(deliver(late, "xy"), early)))
    give = swap(give)
    first = core == 0
    rows = jnp.concatenate([jnp.where(first, keep, give), jnp.where(first, give, keep)], axis=1)
    return jnp.dot(rows, out_weight, preferred_element_type=F32).astype(BF16)


def solution(mesh):
    fine = Mesh(mesh.devices.reshape(4, 2, 4, 4), ALL)
    return jax.shard_map(
        body,
        mesh=fine,
        in_specs=(P(ALL, None), P(ALL, None, None), P(ALL, None, None), P(), P(), P(), P()),
        out_specs=P(ALL, None),
        check_vma=False,
    )
```

```python
import functools
import itertools

import jax
import jax.numpy as jnp
from jax import lax
from jax.experimental import pallas as pl
from jax.experimental.pallas import tpu as pltpu
from jax.sharding import Mesh, PartitionSpec as P

HD = 64
LOG2E = 1.4426950408889634
TOP_STEP = 16.0
NO_TOP = -32768.0
NH = 4
WIDE = NH * HD
ALL = ("y", "core", "z", "x")
F32 = jnp.float32
BF16 = jnp.bfloat16


def spread_kernel(me, mine, theirs, out):
    first = me[1] == 0
    mine, other = mine[...].astype(F32), theirs[...].astype(F32)
    pair = jnp.concatenate([jnp.where(first, mine, other), jnp.where(first, other, mine)], axis=0).astype(BF16)
    for i in range(16):
        for c in range(2):
            out[i, c] = pair[:, c * WIDE:(c + 1) * WIDE]


def spread_rows(me, mine, theirs):
    vmem = pl.BlockSpec(memory_space=pltpu.VMEM)
    smem = pl.BlockSpec(memory_space=pltpu.SMEM)
    return pl.pallas_call(
        spread_kernel,
        out_shape=jax.ShapeDtypeStruct((16, 2, 48, WIDE), BF16),
        in_specs=[smem, vmem, vmem],
        out_specs=vmem,
        compiler_params=pltpu.CompilerParams(vmem_limit_bytes=6 * 2**20),
        name="spread",
    )(me, mine, theirs)


def attend_kernel(
    me, need, *refs, part,
):
    qs, (k0, k1, v0, _), outs = refs[:4], refs[4:8], refs[8:12]
    cnt, plan, k, vt, qm, acc, sb, top, shrink, yb, sem = refs[12:]
    my_y, my_core, my_x = me[0], me[1], me[3]
    col = pl.multiple_of(my_core * 512 + part * WIDE, WIDE)
    copies = [
        pltpu.make_async_copy(src, dst, sem.at[i])
        for i, (src, dst) in enumerate(
            [
                (k0.at[:, :, pl.ds(col, WIDE)], k.at[pl.ds(0, 4)]),
                (k1.at[:, :, pl.ds(col, WIDE)], k.at[pl.ds(4, 4)]),
                (v0.at[:, pl.ds(part * WIDE, WIDE), :], vt),
            ]
        )
    ]
    for copy in copies:
        copy.start()
    scale = HD ** -0.5 * LOG2E
    ones = jnp.ones((16, 256), BF16)

    total, slot = jnp.int32(0), jnp.int32(0)
    for qi in range(12):
        begin = total
        for j in range(8):
            plan[total] = qi + 16 * j + 256 * slot
            total = total + need[qi, j]
        cnt[qi] = total - begin
        slot = (slot + jnp.minimum(total - begin, 1)) & 3
    for u in range(8):
        plan[total + u] = 12 + 256 * slot

    def frame_of(t):
        return plan[t] & 15

    def held_of(t):
        return (plan[t] >> 4) & 7

    def slot_of(t):
        return plan[t] >> 8

    def place(r3, z, a):
        y = jnp.where(my_core == 0, a, lax.rem(my_y + 4 - r3, 4))
        x = jnp.where(my_core == 0, lax.rem(my_x + 4 - r3, 4), a)
        return [pl.multiple_of(y * 768 + (c * 16 + z * 4 + x) * 24, 8) for c in range(2)]

    spots = [[place(r3, z, a) for z in range(4) for a in range(4)] for r3 in range(4)]
    for i, spot in enumerate(spots):
        for b, rows in enumerate(spot):
            block = qs[i][b].astype(F32)
            for c, row in enumerate(rows):
                yb[pl.ds(row, 24), :WIDE] = block[c * 24:(c + 1) * 24]

    def turn(qi, _):
        rows = pl.ds(pl.multiple_of(qi * 256, 256), 256)
        zero = jnp.zeros((64, 256), BF16)
        for hp in range(NH // 2):
            turned = yb[rows, hp * 128:(hp + 1) * 128].astype(BF16).T
            qm[qi, 2 * hp] = jnp.concatenate([turned[:64], zero], axis=0)
            qm[qi, 2 * hp + 1] = jnp.concatenate([zero, turned[64:]], axis=0)
        return 0

    def turns(u, _):
        for i in range(3):
            turn(u * 3 + i, 0)
        return 0

    lax.fori_loop(0, 4, turns, 0)
    def blank(qi, _):
        @pl.when(cnt[qi] == 0)
        def _():
            rows = pl.ds(pl.multiple_of(qi * 256, 256), 256)
            yb[rows, :WIDE] = jnp.zeros((256, WIDE), F32)
            lane = lax.broadcasted_iota(jnp.int32, (256, 128), 1)
            yb[rows, WIDE:] = jnp.where(lane < NH, NO_TOP, 0.0)

        return 0

    lax.fori_loop(0, 12, blank, 0)
    for copy in copies:
        copy.wait()
    acc[...] = jnp.zeros_like(acc)
    qm[12] = jnp.zeros((NH, 128, 256), BF16)

    def score(t, p, h):
        hp = h // 2
        keys = k[held_of(t + p), :, hp * 128:(hp + 1) * 128]
        s = jnp.dot(keys, qm[frame_of(t + p), h], preferred_element_type=F32) * scale
        sb[p, h] = s
        return jnp.max(s, axis=0, keepdims=True)

    def settle(t, p, highs, old):
        first = frame_of(t + p) != frame_of(jnp.maximum(t + p - 1, 0))
        old = jnp.where(first, NO_TOP, old)
        high = jnp.concatenate(highs, axis=0)
        new = jnp.maximum(old, jnp.ceil(high * (1.0 / TOP_STEP)) * TOP_STEP)
        top[p] = new
        shrink[p] = jnp.exp2(old - new)
        return new

    def weigh(t, p, h, tops, shrinks):
        weights = jnp.exp2(sb[p, h] - tops[h:h + 1]).astype(BF16)
        vals = jnp.concatenate([vt[held_of(t + p), h * 64:(h + 1) * 64, :], ones], axis=0)
        part = jnp.dot(vals, weights, preferred_element_type=F32)
        at = slot_of(t + p)
        acc[at, h] = acc[at, h] * shrinks[h:h + 1] + part

    def finish(t, p, tops):
        qi = frame_of(t + p)

        @pl.when((qi < 12) & (frame_of(t + p + 1) != qi))
        def _():
            at = slot_of(t + p)
            rows = pl.ds(pl.multiple_of(qi * 256, 256), 256)
            totals = jnp.concatenate([acc[at, h, 64:65, :] for h in range(NH)], axis=0)
            hi = totals.astype(BF16).astype(F32)
            extra = [tops, hi, totals - hi, jnp.zeros((128 - 3 * NH, 256), F32)]
            for hp in range(NH // 2):
                both = jnp.concatenate([acc[at, 2 * hp, :64, :], acc[at, 2 * hp + 1, :64, :]], axis=0)
                yb[rows, hp * 128:(hp + 1) * 128] = both.astype(BF16).T.astype(F32)
            yb[rows, WIDE:] = jnp.concatenate(extra, axis=0).astype(BF16).T.astype(F32)

    old = jnp.full((NH, 256), NO_TOP, F32)
    for p in range(4):
        old = settle(0, p, [score(0, p, h) for h in range(NH)], old)

    def two(u, _):
        t = u * 4
        tops, shrinks = [top[p] for p in range(4)], [shrink[p] for p in range(4)]
        highs = [[] for p in range(4)]
        for p in range(4):
            for h in range(NH):
                weigh(t, p, h, tops[p], shrinks[p])
                highs[p].append(score(t + 4, p, h))
        old = tops[3]
        for p in range(4):
            old = settle(t + 4, p, highs[p], old)
        for p in range(4):
            finish(t, p, tops[p])
        return 0

    lax.fori_loop(0, (total + 3) // 4, two, 0)

    for o, spot in zip(outs, spots):
        for b, rows in enumerate(spot):
            data, tail = [], jnp.zeros((8, 128), F32)
            for c, row in enumerate(rows):
                block = yb[pl.ds(row, 24), :]
                data.append(block[:, :WIDE])
                for p in range(3):
                    piece = block[p * 8:(p + 1) * 8, WIDE:]
                    g = c * 3 + p
                    tail = tail + (pltpu.roll(piece, 16 * g, 1) if g else piece)
            data.append(jnp.concatenate([tail, jnp.zeros((8, WIDE - 128), F32)], axis=1))
            o[b] = jnp.concatenate(data, axis=0).astype(BF16)


def attend(me, need, q, k0, k1, v0, after, part):
    vmem = pl.BlockSpec(memory_space=pltpu.VMEM)
    smem = pl.BlockSpec(memory_space=pltpu.SMEM)
    whole = pl.BlockSpec(memory_space=pl.ANY)
    far = pl.BlockSpec(memory_space=pltpu.HBM)
    return pl.pallas_call(
        functools.partial(attend_kernel, part=part),
        out_shape=[jax.ShapeDtypeStruct((16, 56, WIDE), BF16)] * 4,
        in_specs=[smem] * 2 + [vmem] * 4 + [far, whole, far, whole],
        out_specs=[vmem] * 4,
        scratch_shapes=[
            pltpu.SMEM((12,), jnp.int32),
            pltpu.SMEM((112,), jnp.int32),
            pltpu.VMEM((8, 256, WIDE), BF16),
            pltpu.VMEM((8, WIDE, 256), BF16),
            pltpu.VMEM((13, NH, 128, 256), BF16),
            pltpu.VMEM((4, NH, 80, 256), F32),
            pltpu.VMEM((4, NH, 256, 256), F32),
            pltpu.VMEM((4, NH, 256), F32),
            pltpu.VMEM((4, NH, 256), F32),
            pltpu.VMEM((3072, WIDE + 128), F32),
            pltpu.SemaphoreType.DMA((3,)),
        ],
        compiler_params=pltpu.CompilerParams(vmem_limit_bytes=24 * 2**20),
        cost_estimate=pl.CostEstimate(flops=10**10, bytes_accessed=2**23, transcendentals=2 * 10**7),
        name="attend",
    )(me, need, *q, pltpu.with_memory_space_constraint(k0, pltpu.HBM), k1, pltpu.with_memory_space_constraint(v0, pltpu.HBM), after)


def turn_kernel(me, v0, v1, k, out, parts, held, turned, sem):
    parts[0] = 0
    parts[1] = 1
    col = pl.multiple_of(me[1] * 512, 512)
    copies = [
        pltpu.make_async_copy(v.at[:, :, pl.ds(col, 512)], held.at[pl.ds(i * 4, 4)], sem.at[i])
        for i, v in enumerate((v0, v1))
    ]
    for copy in copies:
        copy.start()
    backs = []
    for j in range(8):
        if j % 4 == 0:
            copies[j // 4].wait()
        for at in range(0, 512, 128):
            turned[j, at:at + 128, :] = held[j, :, at:at + 128].T
        back = pltpu.make_async_copy(turned.at[j], out.at[j], sem.at[2 + j])
        back.start()
        backs.append(back)
    for back in backs:
        back.wait()


def turn_values(me, v0, v1, k):
    smem = pl.BlockSpec(memory_space=pltpu.SMEM)
    far = pl.BlockSpec(memory_space=pltpu.HBM)
    whole = pl.BlockSpec(memory_space=pl.ANY)
    return pl.pallas_call(
        turn_kernel,
        out_shape=[pltpu.HBM((8, 512, 256), BF16), jax.ShapeDtypeStruct((2,), jnp.int32)],
        in_specs=[smem, far, whole, whole],
        out_specs=[far, smem],
        scratch_shapes=[
            pltpu.VMEM((8, 256, 512), BF16),
            pltpu.VMEM((8, 512, 256), BF16),
            pltpu.SemaphoreType.DMA((10,)),
        ],
        cost_estimate=pl.CostEstimate(flops=10**6, bytes_accessed=2**23, transcendentals=0),
        compiler_params=pltpu.CompilerParams(vmem_limit_bytes=16 * 2**20),
        name="turn",
    )(me, pltpu.with_memory_space_constraint(v0, pltpu.HBM), v1, k)


def add_up(data, tails, spread):
    n = len(data)
    best = functools.reduce(jnp.maximum, tails)
    shares = [jnp.exp2(jnp.minimum(t - best, 0.0)) for t in tails]
    total = sum(f * (pltpu.roll(t, 128 - NH, 1) + pltpu.roll(t, 128 - 2 * NH, 1)) for f, t in zip(shares, tails))
    stack = jnp.concatenate(shares, axis=0)
    groups = data[0].shape[0] // 8
    stack = jnp.concatenate([stack] + [pltpu.roll(stack, 128 - 16 * g, 1) for g in range(1, groups)], axis=0)
    wide = jnp.dot(stack.astype(BF16), spread, preferred_element_type=F32)
    numer = []
    for g in range(groups):
        at = g * 8 * n
        numer.append(
            sum(wide[at + s * 8:at + s * 8 + 8] * d[g * 8:g * 8 + 8, :].astype(F32) for s, d in enumerate(data))
        )
    return numer, best, total


def make_spread():
    src = lax.broadcasted_iota(jnp.int32, (128, WIDE), 0)
    dst = lax.broadcasted_iota(jnp.int32, (128, WIDE), 1) // HD
    return src == dst


def add_blocks(held, spread, is_top):
    data, tails = [p[:48] for p in held], [p[48:56, :128].astype(F32) for p in held]
    numer, best, total = add_up(data, tails, spread)
    total = jnp.where(is_top, total, 0.0)
    hi = total.astype(BF16).astype(F32)
    tail = jnp.where(is_top, best, 0.0) + pltpu.roll(hi, NH, 1) + pltpu.roll(total - hi, 2 * NH, 1)
    return numer, jnp.concatenate([tail, jnp.zeros((8, WIDE - 128), F32)], axis=1)


def merge_kernel(p0, p1, p2, p3, i1, i2, i3, out, o1, o2, o3):
    spread = make_spread().astype(BF16)
    is_top = lax.broadcasted_iota(jnp.int32, (8, 128), 1) % 16 < NH
    for b in range(16):
        numer, tail = add_blocks([p[b] for p in (p0, p1, p2, p3)], spread, is_top)
        out[b] = jnp.concatenate(numer + [tail], axis=0).astype(BF16)


def merge(parts, after):
    vmem = pl.BlockSpec(memory_space=pltpu.VMEM)
    whole = pl.BlockSpec(memory_space=pl.ANY)
    block = jax.ShapeDtypeStruct((16, 56, WIDE), BF16)
    return pl.pallas_call(
        merge_kernel,
        out_shape=[block] * 4,
        in_specs=[vmem] * 4 + [whole] * 3,
        out_specs=[vmem] + [whole] * 3,
        input_output_aliases={4: 1, 5: 2, 6: 3},
        compiler_params=pltpu.CompilerParams(vmem_limit_bytes=10 * 2**20),
        name="merge",
    )(*parts, *after)


def settle_rows(got, c):
    spread = make_spread()
    held = [got[i, c] for i in range(16)]
    numer, _, total = add_up([p[:48] for p in held], [p[48:56, :128].astype(F32) for p in held], spread.astype(BF16))
    totals = jnp.concatenate([total] + [pltpu.roll(total, 128 - 16 * g, 1) for g in range(1, 6)], axis=0)
    wide = jnp.dot(totals, spread.astype(F32), precision=lax.Precision.HIGHEST, preferred_element_type=F32)
    return jnp.concatenate(numer, axis=0) / wide


def join_kernel(p0, p1, p2, p3, ready, out):
    spread = make_spread().astype(BF16)
    is_top = lax.broadcasted_iota(jnp.int32, (8, 128), 1) % 16 < NH
    for b in range(16):
        numer, tail = add_blocks([p[b] for p in (p0, p1, p2, p3)], spread, is_top)
        out[b, 0] = ready[b]
        out[b, 1] = jnp.concatenate(numer + [tail], axis=0).astype(BF16)


def join(parts, ready):
    vmem = pl.BlockSpec(memory_space=pltpu.VMEM)
    return pl.pallas_call(
        join_kernel,
        out_shape=jax.ShapeDtypeStruct((16, 2, 56, WIDE), BF16),
        in_specs=[vmem] * 5,
        out_specs=vmem,
        compiler_params=pltpu.CompilerParams(vmem_limit_bytes=10 * 2**20),
        name="join",
    )(*parts, ready)


def close_kernel(me, got, keep, give, both):
    for c in range(2):
        both[:, c * WIDE:(c + 1) * WIDE] = settle_rows(got, c)
    row = pl.multiple_of(me[1] * 24, 8)
    keep[...] = both[pl.ds(row, 24), :].astype(BF16)
    give[...] = both[pl.ds(24 - row, 24), :].astype(BF16)


def close(me, got):
    vmem = pl.BlockSpec(memory_space=pltpu.VMEM)
    smem = pl.BlockSpec(memory_space=pltpu.SMEM)
    return pl.pallas_call(
        close_kernel,
        out_shape=[jax.ShapeDtypeStruct((24, 512), BF16)] * 2,
        in_specs=[smem, vmem],
        out_specs=[vmem] * 2,
        scratch_shapes=[pltpu.VMEM((48, 512), F32)],
        compiler_params=pltpu.CompilerParams(vmem_limit_bytes=6 * 2**20),
        name="close",
    )(me, got)


def swap(x):
    return lax.ppermute(x, "core", [(0, 1), (1, 0)])


def shift(x, axes, by):
    pairs = []
    for y, c, z, w in itertools.product(range(4), range(2), range(4), range(4)):
        to = {"y": y, "z": z, "x": w}
        to[axes[c]] = (to[axes[c]] + by) % 4
        pairs.append((((y * 2 + c) * 4 + z) * 4 + w, ((to["y"] * 2 + c) * 4 + to["z"]) * 4 + to["x"]))
    return lax.ppermute(x, ALL, pairs)


def ring(x, axes):
    return [x] + [shift(x, axes, by) for by in (1, 2, 3)]


def spot(y, c, z, x):
    return ((y * 2 + c) * 4 + z) * 4 + x


GROUPS = [[spot(a, 0, z, w) for z in range(4) for a in range(4)] for w in range(4)] + [
    [spot(w, 1, z, a) for z in range(4) for a in range(4)] for w in range(4)
]


def exchange(x):
    return lax.all_to_all(x, ALL, 0, 0, axis_index_groups=GROUPS)


def deliver(parts, axes):
    return [parts[0]] + [shift(parts[by], axes, -by) for by in (1, 2, 3)]


def body(queries, keys, values, frame_slot, covisible, counts, out_weight):
    core = lax.axis_index("core")
    device = lax.axis_index(ALL)
    partner = device + 16 - 32 * core
    own_col = core * 512

    theirs = swap(lax.dynamic_slice_in_dim(queries, 512 - own_col, 512, 1))
    me = jnp.stack([lax.axis_index(a) for a in ALL]).astype(jnp.int32)
    mine = lax.dynamic_slice_in_dim(queries, own_col, 512, 1)
    plane = exchange(spread_rows(me, mine, theirs))
    k_theirs, v_theirs = swap(keys), swap(values)
    v_turned, parts = turn_values(me, values, v_theirs, k_theirs)
    q_parts = [ring(lax.dynamic_index_in_dim(plane, parts[c], 1, False), "xy") for c in range(2)]

    four = jnp.arange(4, dtype=jnp.int32)
    slots = jnp.concatenate([device * 4 + four, partner * 4 + four])
    frame_ids = jnp.arange(frame_slot.shape[0], dtype=jnp.int32)
    local = jnp.sum(jnp.where(frame_slot[None, :] == slots[:, None], frame_ids[None, :], 0), axis=1)
    used = jnp.arange(covisible.shape[1], dtype=jnp.int32)[None, :] < counts[:, None]
    need = jnp.any((covisible[:, None, :] == local[None, :, None]) & used[:, None, :], axis=2)
    need = need.astype(jnp.int32)

    early = attend(me, need, q_parts[0], keys, k_theirs, v_turned, q_parts[0][0], 0)
    late = attend(me, need, q_parts[1], keys, k_theirs, v_turned, early[0], 1)
    early, *sent = merge(deliver(early, "xy"), late[1:])
    keep, give = close(me, exchange(join(deliver([late[0], *sent], "xy"), early)))
    give = swap(give)
    first = core == 0
    rows = jnp.concatenate([jnp.where(first, keep, give), jnp.where(first, give, keep)], axis=1)
    return jnp.dot(rows, out_weight, preferred_element_type=F32).astype(BF16)


def solution(mesh):
    fine = Mesh(mesh.devices.reshape(4, 2, 4, 4), ALL)
    return jax.shard_map(
        body,
        mesh=fine,
        in_specs=(P(ALL, None), P(ALL, None, None), P(ALL, None, None), P(), P(), P(), P()),
        out_specs=P(ALL, None),
        check_vma=False,
    )
```
